512 devices in a mesh: section: 8 (over x, y_hi), seq: 64 (over z, y_lo, core).
Axes of the slice: x: 4, y: 4 (y_hi: 2, y_lo: 2; y = y_hi * 2 + y_lo), z: 16, core: 2. Of those that a mesh axis runs over, the one named last changes fastest.
Arguments:
- codes: int32 [8, 2, 112, 8192], P('section', None, None, 'seq'), may hold values from -240 to 240
- exponents: int32 [8, 2, 112], P('section'), may hold values from -12 to -7
- sample_ids: int32 [8, 2], replicated, may hold values from 0 to 2, as said below
- buffer_in: bfloat16 [8, 3, 112, 8192], P('section', None, None, 'seq'), may hold values from -16 to 16
- buffer_out: bfloat16 [8, 3, 112, 8192], P('section', None, None, 'seq'), may hold values from -6 to 6
- norm_gain: bfloat16 [8, 8192], P('section', 'seq'), may hold values from 0.25 to 1.75
- w_query: bfloat16 [8, 8192, 8192], P('section', None, 'seq'), may hold values from -0.0625 to 0.0625
- w_keyval: bfloat16 [8, 8192, 2048], P('section', None, 'seq'), may hold values from -0.0625 to 0.0625
- w_output: bfloat16 [8, 8192, 8192], P('section', None, 'seq'), may hold values from -0.5 to 0.5
Outputs:
- next_input: bfloat16 [8, 2, 112, 8192], P('section', None, None, 'seq')
- buffer_in_new: bfloat16 [8, 3, 112, 8192], P('section', None, None, 'seq')
- buffer_out_new: bfloat16 [8, 3, 112, 8192], P('section', None, None, 'seq')
The draws below stay inside these ranges and needn't reach their ends.
Inputs may be any that keep to these rules, and one draw needn't show every extreme that they name: `sample_ids`: each row names 2 different slots.
All inputs are finite; a program needn't handle non-finite values.
Results may differ from the reference program's by a relative error of at most 0.015.
Values may be sent and summed in bfloat16 or wider, within the bound.
No kernel may reach another device: no remote copies, remote signals or barrier semaphores. Data moves between devices by JAX's collectives and lax.ppermute only.
A program may use at most 64 MiB of HBM per device.

```python
import math
import jax
import jax.numpy as jnp
from jax import lax

D = 8192
KV_HEADS = 8
HEAD = 128
SEQS = 2
SLOTS = 3
LEN = 112
HEADS = 64
SECTIONS = 8


def draw_sample_ids(key, part):
    key = jax.random.fold_in(key, 11)
    first_key, other_key = jax.random.split(key)
    section_keys = jax.random.split(other_key, SECTIONS)
    picked = jax.vmap(lambda section_key: jax.random.permutation(section_key, SLOTS)[:SEQS])(section_keys)
    remaining = jax.random.permutation(first_key, SLOTS - 1)
    first_row = jnp.concatenate([jnp.array([SLOTS - 1]), remaining])[:SEQS]
    picked = picked.at[0].set(first_row)
    return picked.astype(jnp.int32)


def draw_buffer_in(key, part):
    key = jax.random.fold_in(key, 5)
    columns = jnp.arange(D).astype(jnp.float32) / max(D - 1, 1)
    base = jnp.clip(jax.random.normal(key, (SECTIONS, SLOTS, LEN, D), jnp.float32), -5.0, 5.0)
    rising = jnp.exp(columns * math.log(3.0))
    return (base * rising).astype(jnp.bfloat16)


def plant(drawn, key, smallest, largest):
    dims = drawn.shape
    spot = [jax.random.randint(jax.random.fold_in(key, axis), (), 0, dims[axis]) for axis in range(len(dims))]
    drawn = drawn.at[tuple(spot)].set(smallest)
    longest = dims.index(max(dims))
    spot[longest] = (spot[longest] + 1) % dims[longest]
    return drawn.at[tuple(spot)].set(largest)


def steps_of(rng, shape, cuts, least, high):
    level, own = 1.0, jax.random.fold_in(rng, 6)
    for dim, parts in cuts:
        draws = jnp.exp(jax.random.uniform(jax.random.fold_in(own, dim), (parts,), jnp.float32, least / len(cuts), high / len(cuts)))
        level = level * jnp.repeat(draws, shape[dim] // parts).reshape([-1 if axis == dim else 1 for axis in range(len(shape))])
    return level


def gaussian(rng, shape, width, limit, shards=(), held_as=jnp.bfloat16):
    result = jax.random.normal(rng, shape, jnp.float32) * width
    if len(shards) > 0:
        result = steps_of(rng, shape, shards, -0.22, 0.18) * result
    return jnp.clip(result, min=-limit, max=limit).astype(held_as)


def setup_inputs(seed: int = 0) -> dict:
    streams_of = jax.random.split(jax.random.key(seed), 10)
    codes = plant(jax.random.randint(streams_of[0], (SECTIONS, SEQS, LEN, D), -240, 241), jax.random.fold_in(streams_of[0], 1), -240, 240).astype(jnp.int32)
    exponents = plant(jax.random.randint(streams_of[1], (SECTIONS, SEQS, LEN), -12, -6), jax.random.fold_in(streams_of[1], 1), -12, (-6) - 1).astype(jnp.int32)
    sample_ids = draw_sample_ids(jax.random.fold_in(streams_of[9], 71), 0)
    buffer_in = draw_buffer_in(jax.random.fold_in(streams_of[9], 71), 0)
    buffer_out = gaussian(streams_of[4], (SECTIONS, SLOTS, LEN, D), 1.0, 6.0, ((0, 8), (3, 64)))
    norm_gain = jnp.clip(1.0 + 0.15 * jax.random.normal(streams_of[5], (SECTIONS, D), jnp.float32), 0.25, 1.75).astype(jnp.bfloat16)
    w_query = gaussian(streams_of[6], (SECTIONS, D, HEADS * HEAD), D ** -0.5, 0.0625, ((0, 8), (2, 64)))
    w_keyval = gaussian(streams_of[7], (SECTIONS, D, 2 * KV_HEADS * HEAD), D ** -0.5, 0.0625, ((0, 8), (2, 64)))
    w_output = gaussian(streams_of[8], (SECTIONS, HEADS * HEAD, D), HEAD ** -0.5, 0.5, ((0, 8), (2, 64)))
    return {"codes": codes, "exponents": exponents, "sample_ids": sample_ids, "buffer_in": buffer_in, "buffer_out": buffer_out, "norm_gain": norm_gain, "w_query": w_query, "w_keyval": w_keyval, "w_output": w_output}


rope_base = 500000.0
norm_eps = 1e-05

def rotate(values, positions):
    half_width = values.shape[-1] // 2
    freq_steps = jnp.arange(half_width, dtype=jnp.float32)
    frequency = jnp.exp(freq_steps * (-2.0 * math.log(rope_base) / values.shape[-1]))
    rotation = positions[..., None] * frequency
    cos_part = jnp.cos(rotation)
    sin_part = jnp.sin(rotation)
    first_half = values[..., :half_width]
    second_half = values[..., half_width:]
    return jnp.concatenate([first_half * cos_part - second_half * sin_part, second_half * cos_part + first_half * sin_part], axis=-1)

def reference(codes, exponents, sample_ids, buffer_in, buffer_out, norm_gain, w_query, w_keyval, w_output):
    section_total = codes.shape[0]
    seq_total = codes.shape[1]
    seq_length = codes.shape[2]
    model_width = codes.shape[3]
    head_total = w_query.shape[2] // HEAD
    group_size = head_total // KV_HEADS
    positions = jnp.arange(seq_length).astype(jnp.float32)[None, :, None]
    causal = jnp.arange(seq_length)[:, None] >= jnp.arange(seq_length)[None, :]
    previous = jnp.zeros((seq_total, seq_length, model_width), jnp.bfloat16)
    follow_list = []
    store_in_list = []
    store_out_list = []
    for section in range(section_total):
        slot_ids = sample_ids[section]
        stored = buffer_in[section][slot_ids].astype(jnp.float32)
        scales = jnp.exp2(exponents[section].astype(jnp.float32))
        inputs = (stored + codes[section].astype(jnp.float32) * scales[..., None]).astype(jnp.bfloat16)
        stored_in = buffer_in[section].at[slot_ids].set(inputs)
        widened = inputs.astype(jnp.float32)
        inverse = lax.rsqrt(lax.optimization_barrier(jnp.mean(widened * widened, axis=-1, keepdims=True)) + norm_eps)
        normed = (widened * inverse * norm_gain[section].astype(jnp.float32)).astype(jnp.bfloat16)
        flat_rows = normed.reshape(seq_total * seq_length, model_width)
        queries = jnp.dot(flat_rows, w_query[section], preferred_element_type=jnp.float32)
        queries = rotate(queries.reshape(seq_total, seq_length, head_total, HEAD), positions).astype(jnp.bfloat16)
        keyval = jnp.dot(flat_rows, w_keyval[section], preferred_element_type=jnp.float32).astype(jnp.bfloat16)
        keyval = keyval.reshape(seq_total, seq_length, 2, KV_HEADS, HEAD)
        key_rows = rotate(keyval[:, :, 0].astype(jnp.float32), positions).astype(jnp.bfloat16)
        value_rows = keyval[:, :, 1]
        key_rows = jnp.repeat(key_rows, group_size, axis=2)
        value_rows = jnp.repeat(value_rows, group_size, axis=2)
        scores = jnp.einsum('sqhd,skhd->shqk', queries.astype(jnp.float32), key_rows.astype(jnp.float32)) / math.sqrt(HEAD)
        scores = jnp.where(causal[None, None], scores, -1e+30)
        row_peak = lax.optimization_barrier(jnp.max(scores, axis=-1, keepdims=True))
        raised = jnp.exp(scores - row_peak)
        weights = (raised / lax.optimization_barrier(jnp.sum(raised, axis=-1, keepdims=True))).astype(jnp.bfloat16)
        context = jnp.einsum('shqk,skhd->sqhd', weights.astype(jnp.float32), value_rows.astype(jnp.float32)).astype(jnp.bfloat16)
        context = context.reshape(seq_total * seq_length, head_total * HEAD)
        mixed_rows = jnp.dot(context, w_output[section], preferred_element_type=jnp.float32)
        updated = widened + mixed_rows.reshape(seq_total, seq_length, model_width)
        stored_out = buffer_out[section][slot_ids].astype(jnp.float32)
        message = (updated - stored_out).astype(jnp.bfloat16)
        new_out = buffer_out[section].at[slot_ids].set((stored_out + message.astype(jnp.float32)).astype(jnp.bfloat16))
        sender_ids = sample_ids[max(section - 1, 0)]
        following = (stored_in[sender_ids].astype(jnp.float32) + previous.astype(jnp.float32)).astype(jnp.bfloat16)
        stored_in = stored_in.at[sender_ids].set(following)
        previous = message
        follow_list.append(following)
        store_in_list.append(stored_in)
        store_out_list.append(new_out)
    return (jnp.stack(follow_list), jnp.stack(store_in_list), jnp.stack(store_out_list))
```

```python
import functools
import math

import jax
import jax.numpy as jnp
import numpy as np
from jax import lax
from jax.experimental import pallas as pl
from jax.experimental.pallas import tpu as pltpu
from jax.sharding import Mesh
from jax.sharding import PartitionSpec as P

SEQS, LEN, SLOTS, HEAD, KV_HEADS = 2, 112, 3, 128, 8
ROWS = SEQS * LEN
PAY = ROWS + 16
ZN, YN, CN = 16, 2, 2
PIECES = 4
LANES = ("z", "y", "core")
rope_base = 500000.0
norm_eps = 1e-05

VMEM = pl.BlockSpec(memory_space=pltpu.VMEM)
SMEM = pl.BlockSpec(memory_space=pltpu.SMEM)
PARAMS = pltpu.CompilerParams(vmem_limit_bytes=40 * 1024 * 1024)
NT = (((1,), (1,)), ((), ()))


def rope_tables():
    half = HEAD // 2
    frequency = np.exp(np.arange(half) * (-2.0 * math.log(rope_base) / HEAD))
    positions = np.arange(ROWS) % LEN
    angle = positions[:, None] * frequency[None, :]
    return np.cos(angle).astype(np.float32), np.sin(angle).astype(np.float32)


def call(kernel, outs, n_in, flops, bytes_accessed, smem=(), scratch=()):
    return pl.pallas_call(
        kernel,
        out_shape=outs,
        in_specs=[SMEM if i in smem else VMEM for i in range(n_in)],
        out_specs=jax.tree.map(lambda _: VMEM, outs),
        scratch_shapes=list(scratch),
        compiler_params=PARAMS,
        cost_estimate=pl.CostEstimate(
            flops=flops, bytes_accessed=bytes_accessed, transcendentals=0
        ),
    )


def shape(dims, dtype=jnp.bfloat16):
    return jax.ShapeDtypeStruct(dims, dtype)


def prepare(
    ids, codes, exponents, buffer_in, gain, query, keyval, output,
    packed, packed_out, pay, inputs_out,
    codes_v, exponents_v, stored_v, gain_v, keyval_v, half_v, keyval_half_v, sems, half_sems,
):
    section = lax.axis_index("section")
    far = lax.axis_index("y") ^ 1
    copies = [
        pltpu.make_async_copy(exponents, exponents_v, sems.at[0]),
        pltpu.make_async_copy(gain, gain_v, sems.at[1]),
        pltpu.make_async_copy(codes, codes_v, sems.at[2]),
        pltpu.make_async_copy(buffer_in.at[0, ids[0, section]], stored_v.at[0], sems.at[3]),
        pltpu.make_async_copy(buffer_in.at[0, ids[1, section]], stored_v.at[1], sems.at[4]),
        pltpu.make_async_copy(keyval, keyval_v, sems.at[5]),
    ]
    for item in copies:
        item.start()

    step = ZN // PIECES
    loads, stores = [], []
    for i in range(2 * PIECES):
        source, target = (query, packed) if i < PIECES else (output, packed_out)
        part = pl.ds(i % PIECES * step, step)
        loads.append(
            pltpu.make_async_copy(source.at[part, far], half_v.at[i], half_sems.at[0, i])
        )
        stores.append(
            pltpu.make_async_copy(half_v.at[i], target.at[part], half_sems.at[1, i])
        )
        loads[-1].start()
    for item in copies[:5]:
        item.wait()
    eye = lax.broadcasted_iota(jnp.int32, (LEN, LEN), 0) == lax.broadcasted_iota(
        jnp.int32, (LEN, LEN), 1
    )
    gains = gain_v[...].astype(jnp.float32)
    sums = []
    for s in range(SEQS):
        steps = jnp.exp2(exponents_v[0, s : s + 1, :].astype(jnp.float32))
        diagonal = jnp.where(eye, steps, 0.0).astype(jnp.bfloat16)
        scales = jnp.dot(
            diagonal, jnp.ones((LEN, HEAD), jnp.bfloat16), preferred_element_type=jnp.float32
        )
        stored = stored_v[s].astype(jnp.float32)
        inputs = (stored + codes_v[0, s].astype(jnp.float32) * scales).astype(jnp.bfloat16)
        inputs_out[s] = inputs
        widened = inputs.astype(jnp.float32)
        pay[s * LEN : (s + 1) * LEN, :] = (widened * gains).astype(jnp.bfloat16)
        squares = widened * widened
        high = squares.astype(jnp.bfloat16)
        low = (squares - high.astype(jnp.float32)).astype(jnp.bfloat16)
        ones = jnp.ones((16, HEAD), jnp.bfloat16)
        total = lax.dot_general(ones, high, NT, preferred_element_type=jnp.float32)
        total += lax.dot_general(ones, low, NT, preferred_element_type=jnp.float32)
        sums.append(jnp.concatenate([total, jnp.zeros((16, HEAD - LEN), jnp.float32)], axis=1))
    row = lax.broadcasted_iota(jnp.int32, (16, HEAD), 0)
    value = jnp.where(row % 2 == 0, sums[0], sums[1])
    first = value.astype(jnp.bfloat16).astype(jnp.float32)
    second = value - first
    tail = jnp.where(row < 2, first, jnp.where(row < 4, second, 0.0))
    pay[ROWS:PAY, :] = tail.astype(jnp.bfloat16)

    copies[5].wait()
    kv_width = keyval.shape[1]
    per_row = CN * HEAD // kv_width
    for z in range(ZN):
        for core in range(CN):
            i = z * CN + core
            start = (i % per_row) * kv_width
            keyval_half_v[i // per_row, start : start + kv_width, :] = keyval_v[
                0, :, head_rows(z, far, core)
            ]
    last = pltpu.make_async_copy(
        keyval_half_v, packed.at[pl.ds(ZN, keyval_half_v.shape[0])], sems.at[6]
    )
    last.start()
    for load, store in zip(loads, stores):
        load.wait()
        store.start()
    last.wait()
    for store in stores:
        store.wait()


def head_rows(z, y, core):
    head = z * (YN * CN) + y * CN + core
    return pl.ds(pl.multiple_of(head * HEAD, HEAD), HEAD)


def half_rows(z, core):
    return pl.ds(pl.multiple_of((z * CN + core) * HEAD, HEAD), HEAD)


def keyval_kernel(here, there, weight, received, out, sums_out):
    y, core = lax.axis_index("y"), lax.axis_index("core")
    kv_width = weight.shape[1]
    sums = jnp.sum(here[:, ROWS:PAY, :].astype(jnp.float32), axis=0)
    sums += jnp.sum(there[:, ROWS:PAY, :].astype(jnp.float32), axis=0)
    sums = jnp.concatenate(
        [sums[s : s + 1, :LEN] + sums[SEQS + s : SEQS + s + 1, :LEN] for s in range(SEQS)], axis=1
    )
    high = sums.astype(jnp.bfloat16).astype(jnp.float32)
    row = lax.broadcasted_iota(jnp.int32, (PAY - ROWS, ROWS), 0)
    tail = jnp.where(row == 0, high, jnp.where(row == 1, sums - high, 0.0))
    sums_out[...] = tail.astype(jnp.bfloat16)
    acc = jnp.zeros((2 * kv_width, ROWS), jnp.float32)
    for z in range(ZN):
        block = jnp.concatenate([here[z, :ROWS, :], there[z, :ROWS, :]], axis=1)
        parts = []
        for side in (core, core ^ 1):
            start = ZN * CN * HEAD + (z * CN + side) * kv_width
            mine = weight[0, :, head_rows(z, y, side)]
            other = received[pl.ds(pl.multiple_of(start, kv_width), kv_width), :]
            parts.append(jnp.concatenate([mine, other], axis=0))
        part = jnp.concatenate(parts, axis=1)
        acc += lax.dot_general(part, block, NT, preferred_element_type=jnp.float32)
    out[...] = acc.astype(jnp.bfloat16)


def both_partials(here, there, weight, received):
    y, core = lax.axis_index("y"), lax.axis_index("core")
    acc = jnp.zeros((ROWS, 2 * HEAD), jnp.float32)
    for z in range(ZN):
        block = jnp.concatenate([here[z, :ROWS, :], there[z, :ROWS, :]], axis=1)
        parts = []
        for side in (core, core ^ 1):
            mine = weight[0, head_rows(z, y, side), :]
            other = received[half_rows(z, side), :]
            parts.append(jnp.concatenate([mine, other], axis=1))
        part = jnp.concatenate(parts, axis=0)
        acc += jnp.dot(block, part, preferred_element_type=jnp.float32)
    return acc


def query_kernel(here, there, weight, received, mine_out, other_out):
    acc = both_partials(here, there, weight, received)
    mine_out[...] = acc[:, :HEAD]
    other_out[...] = acc[:, HEAD:].astype(jnp.bfloat16)


def sum_kernel(near, far, cos_t, sin_t, out, factors_out):
    z_odd, y, core = lax.axis_index("z") % 2, lax.axis_index("y"), lax.axis_index("core")
    width = (near.shape[0] - (PAY - ROWS)) // 4
    tail = near[4 * width :, :].astype(jnp.float32) + far[4 * width :, :].astype(jnp.float32)
    square_sum = tail[0:1, :] + tail[1:2, :]
    inverse = lax.rsqrt(square_sum / (ZN * YN * CN * HEAD) + norm_eps)
    factors = jnp.broadcast_to(inverse, (width, ROWS))
    factors_out[...] = jnp.broadcast_to(inverse, (HEAD, ROWS)).T

    def piece(kind, which):
        plane = z_odd ^ kind
        a = near[pl.ds(pl.multiple_of((plane * 2 + (which ^ y)) * width, width), width), :]
        b = far[pl.ds(pl.multiple_of((plane * 2 + 1 - (which ^ y)) * width, width), width), :]
        return ((a.astype(jnp.float32) + b.astype(jnp.float32)) * factors).astype(jnp.bfloat16)

    first, second = piece(0, 0).astype(jnp.float32), piece(0, 1).astype(jnp.float32)
    rows = pl.ds(pl.multiple_of(core * width, width), width)
    c, s = cos_t[rows, :], sin_t[rows, :]
    out[0] = (first * c - second * s).astype(jnp.bfloat16)
    out[1] = (second * c + first * s).astype(jnp.bfloat16)
    out[2] = piece(1, 0)
    out[3] = piece(1, 1)


def rope_kernel(mine, other, factors, cos, sin, out):
    acc = (mine[...] + other[...].astype(jnp.float32)) * factors[...]
    first, second = acc[:, : HEAD // 2], acc[:, HEAD // 2 :]
    c, s = cos[...], sin[...]
    out[...] = jnp.concatenate(
        [first * c - second * s, second * c + first * s], axis=1
    ).astype(jnp.bfloat16)


def attention_kernel(query, own, sibling, out):
    core = lax.axis_index("core")
    keys_values = []
    for kind in range(2):
        parts = []
        for which in range(2):
            a, b = own[2 * kind + which], sibling[2 * kind + which]
            parts += [jnp.where(core == 0, a, b), jnp.where(core == 0, b, a)]
        keys_values.append(jnp.concatenate(parts, axis=0))
    keys, values = keys_values
    scores = jnp.dot(query[...], keys, preferred_element_type=jnp.float32) / math.sqrt(HEAD)
    row = lax.broadcasted_iota(jnp.int32, (ROWS, ROWS), 0)
    column = lax.broadcasted_iota(jnp.int32, (ROWS, ROWS), 1)
    allowed = (column <= row) & ((row < LEN) | (column >= LEN))
    scores = jnp.where(allowed, scores, -1e30)
    peak = jnp.max(scores, axis=-1, keepdims=True)
    raised = jnp.exp(scores - peak)
    weights = (raised / jnp.sum(raised, axis=-1, keepdims=True)).astype(jnp.bfloat16)
    context = lax.dot_general(weights, values, NT, preferred_element_type=jnp.float32)
    out[...] = context.astype(jnp.bfloat16)


def output_kernel(here, there, weight, received, mine_out, other_out):
    acc = both_partials(here, there, weight, received)
    mine_out[...] = acc[:, :HEAD]
    other_out[...] = acc[:, HEAD:].astype(jnp.bfloat16)


def message_kernel(ids, mine, other, inputs, buffer_out, message_out):
    section = lax.axis_index("section")
    for s in range(SEQS):
        rows = slice(s * LEN, (s + 1) * LEN)
        stored = buffer_out[0, ids[s, section]].astype(jnp.float32)
        mixed = mine[rows, :] + other[rows, :].astype(jnp.float32)
        message_out[s] = (inputs[s].astype(jnp.float32) + mixed - stored).astype(jnp.bfloat16)


def refresh_kernel(ids, message, buffer_out, new_out):
    section = lax.axis_index("section")
    new_out[...] = buffer_out[...]
    for s in range(SEQS):
        slot = ids[s, section]
        stored = buffer_out[0, slot].astype(jnp.float32)
        new_out[0, slot] = (stored + message[s].astype(jnp.float32)).astype(jnp.bfloat16)


def finish_kernel(ids, buffer_in, inputs, arrived, following_out, stored_out):
    section = lax.axis_index("section")
    before = jnp.maximum(section - 1, 0)
    stored_out[...] = buffer_in[...]
    for s in range(SEQS):
        stored_out[0, ids[s, section]] = inputs[s]
    results = []
    for s in range(SEQS):
        current = stored_out[0, ids[s, before]].astype(jnp.float32)
        results.append((current + arrived[s].astype(jnp.float32)).astype(jnp.bfloat16))
    for s in range(SEQS):
        following_out[0, s] = results[s]
        stored_out[0, ids[s, before]] = results[s]


def lane(z, y, core):
    return (z % ZN) * (YN * CN) + y * CN + core


def permute(x, target):
    pairs = [
        (lane(z, y, c), lane(*target(z, y, c)))
        for z in range(ZN)
        for y in range(YN)
        for c in range(CN)
    ]
    return lax.ppermute(x, LANES, pairs)


def swap_core(x):
    return permute(x, lambda z, y, c: (z, y, c ^ 1))


def swap_y(x):
    return permute(x, lambda z, y, c: (z, y ^ 1, c))


def after(x, earlier):
    return lax.optimization_barrier((x, earlier))[0]


def gather_z(x):
    return lax.all_gather(x, "z", axis=0)


def per_device(
    codes, exponents, sample_ids, buffer_in, buffer_out, norm_gain, w_query, w_keyval, w_output
):
    cos, sin = rope_tables()
    sample_ids = sample_ids.T
    kv_width = w_keyval.shape[2]
    half = ZN * CN * HEAD
    w_keyval = jnp.swapaxes(w_keyval, 1, 2)
    partial_flops = 2 * ROWS * half * 256
    wide = shape((ROWS, HEAD), jnp.float32)

    by_half = (ZN, YN, CN * HEAD, HEAD)
    any_spec = pl.BlockSpec(memory_space=pl.ANY)
    bf16, int32 = jnp.bfloat16, jnp.int32
    packed, packed_out, pay, inputs = pl.pallas_call(
        prepare,
        out_shape=(
            shape((ZN + ZN * kv_width // HEAD, CN * HEAD, HEAD)),
            shape((ZN, CN * HEAD, HEAD)),
            shape((PAY, HEAD)),
            shape((SEQS, LEN, HEAD)),
        ),
        in_specs=[SMEM] + [any_spec] * 7,
        out_specs=(any_spec, any_spec, VMEM, VMEM),
        scratch_shapes=[
            pltpu.VMEM(codes.shape, int32),
            pltpu.VMEM(exponents.shape, int32),
            pltpu.VMEM((SEQS, LEN, HEAD), bf16),
            pltpu.VMEM(norm_gain.shape, bf16),
            pltpu.VMEM(w_keyval.shape, bf16),
            pltpu.VMEM((2 * PIECES, ZN // PIECES, CN * HEAD, HEAD), bf16),
            pltpu.VMEM((ZN * kv_width // HEAD, CN * HEAD, HEAD), bf16),
            pltpu.SemaphoreType.DMA((7,)),
            pltpu.SemaphoreType.DMA((2, 2 * PIECES)),
        ],
        cost_estimate=pl.CostEstimate(flops=10**7, bytes_accessed=4 * 10**6, transcendentals=0),
    )(
        sample_ids, codes, exponents, buffer_in, norm_gain,
        w_query.reshape(by_half), w_keyval, w_output.reshape(by_half),
    )
    received = swap_y(packed).reshape(-1, HEAD)
    received_out = swap_y(packed_out).reshape(half, HEAD)
    here = gather_z(pay)
    there = swap_core(here)

    keyval, sums = call(
        keyval_kernel,
        (shape((2 * kv_width, ROWS)), shape((PAY - ROWS, ROWS))),
        4,
        partial_flops,
        5 * 10**6,
    )(here, there, w_keyval, received)
    even = permute(keyval, lambda z, y, c: (2 * z if z < 8 else 2 * (z - 8) + 1, y, c))
    odd = permute(keyval, lambda z, y, c: (2 * z + 1 if z < 8 else 2 * (z - 8), y, c))
    mine, other = call(
        query_kernel, (wide, shape((ROWS, HEAD))), 4, partial_flops, 6 * 10**6
    )(here, there, w_query, after(received, keyval))
    other = swap_y(other)
    near = after(jnp.concatenate([even, odd, sums]), mine)
    far = swap_y(near)
    own, factors = call(
        sum_kernel, (shape((4, kv_width, ROWS)), wide), 4, 10**6, 10**6
    )(after(near, received_out), far, cos.T.copy(), sin.T.copy())
    sibling = swap_core(own)
    queries = call(rope_kernel, shape((ROWS, HEAD)), 5, 10**6, 10**6)(
        mine, other, factors, cos, sin
    )
    context = call(attention_kernel, shape((ROWS, HEAD)), 3, 4 * ROWS * ROWS * HEAD, 10**6)(
        queries, own, sibling
    )

    here = gather_z(context)
    there = swap_core(here)
    mine, other = call(
        output_kernel, (wide, shape((ROWS, HEAD))), 4, partial_flops, 6 * 10**6
    )(here, there, w_output, received_out)
    other = swap_y(other)
    message = call(
        message_kernel, shape((SEQS, LEN, HEAD)), 5, 10**6, 10**6, smem=(0,)
    )(sample_ids, mine, other, inputs, buffer_out)

    sections = lax.axis_size("section")
    arrived = lax.ppermute(message, "section", [(i, i + 1) for i in range(sections - 1)])
    following, new_in = call(
        finish_kernel,
        (shape((1, SEQS, LEN, HEAD)), shape(buffer_in.shape)),
        4,
        10**6,
        10**6,
        smem=(0,),
    )(sample_ids, buffer_in, inputs, arrived)
    new_out = call(refresh_kernel, shape(buffer_out.shape), 3, 10**6, 10**6, smem=(0,))(
        sample_ids, message, buffer_out
    )
    return following, new_in, new_out


def solution(mesh):
    sections = mesh.shape["section"]
    fine = Mesh(mesh.devices.reshape(sections, ZN, YN, CN), ("section",) + LANES)
    return jax.shard_map(
        per_device,
        mesh=fine,
        in_specs=(
            P("section", None, None, LANES),
            P("section", None, None),
            P(),
            P("section", None, None, LANES),
            P("section", None, None, LANES),
            P("section", LANES),
            P("section", None, LANES),
            P("section", None, LANES),
            P("section", None, LANES),
        ),
        out_specs=(
            P("section", None, None, LANES),
            P("section", None, None, LANES),
            P("section", None, None, LANES),
        ),
        check_vma=False,
    )
```

```python
import functools
import math

import jax
import jax.numpy as jnp
import numpy as np
from jax import lax
from jax.experimental import pallas as pl
from jax.experimental.pallas import tpu as pltpu
from jax.sharding import Mesh
from jax.sharding import PartitionSpec as P

SEQS, LEN, SLOTS, HEAD, KV_HEADS = 2, 112, 3, 128, 8
ROWS = SEQS * LEN
PAY = ROWS + 16
ZN, YN, CN = 16, 2, 2
PIECES = 4
LANES = ("z", "y", "core")
rope_base = 500000.0
norm_eps = 1e-05

VMEM = pl.BlockSpec(memory_space=pltpu.VMEM)
SMEM = pl.BlockSpec(memory_space=pltpu.SMEM)
PARAMS = pltpu.CompilerParams(vmem_limit_bytes=40 * 1024 * 1024)
NT = (((1,), (1,)), ((), ()))


def rope_tables():
    half = HEAD // 2
    frequency = np.exp(np.arange(half) * (-2.0 * math.log(rope_base) / HEAD))
    positions = np.arange(ROWS) % LEN
    angle = positions[:, None] * frequency[None, :]
    return np.cos(angle).astype(np.float32), np.sin(angle).astype(np.float32)


def call(kernel, outs, n_in, flops, bytes_accessed, smem=(), scratch=()):
    return pl.pallas_call(
        kernel,
        out_shape=outs,
        in_specs=[SMEM if i in smem else VMEM for i in range(n_in)],
        out_specs=jax.tree.map(lambda _: VMEM, outs),
        scratch_shapes=list(scratch),
        compiler_params=PARAMS,
        cost_estimate=pl.CostEstimate(
            flops=flops, bytes_accessed=bytes_accessed, transcendentals=0
        ),
    )


def shape(dims, dtype=jnp.bfloat16):
    return jax.ShapeDtypeStruct(dims, dtype)


def prepare(
    ids, codes, exponents, buffer_in, gain, query, keyval,
    packed, pay, inputs_out,
    codes_v, exponents_v, stored_v, gain_v, keyval_v, half_v, keyval_half_v, sems, half_sems,
):
    section = lax.axis_index("section")
    far = lax.axis_index("y") ^ 1
    copies = [
        pltpu.make_async_copy(exponents, exponents_v, sems.at[0]),
        pltpu.make_async_copy(gain, gain_v, sems.at[1]),
        pltpu.make_async_copy(codes, codes_v, sems.at[2]),
        pltpu.make_async_copy(buffer_in.at[0, ids[0, section]], stored_v.at[0], sems.at[3]),
        pltpu.make_async_copy(buffer_in.at[0, ids[1, section]], stored_v.at[1], sems.at[4]),
        pltpu.make_async_copy(keyval, keyval_v, sems.at[5]),
    ]
    for item in copies:
        item.start()

    step = ZN // PIECES
    loads, stores = [], []
    for i in range(PIECES):
        part = pl.ds(i * step, step)
        loads.append(
            pltpu.make_async_copy(query.at[part, far], half_v.at[i], half_sems.at[0, i])
        )
        stores.append(
            pltpu.make_async_copy(half_v.at[i], packed.at[part], half_sems.at[1, i])
        )
        loads[-1].start()
    for item in copies[:5]:
        item.wait()
    eye = lax.broadcasted_iota(jnp.int32, (LEN, LEN), 0) == lax.broadcasted_iota(
        jnp.int32, (LEN, LEN), 1
    )
    gains = gain_v[...].astype(jnp.float32)
    sums = []
    for s in range(SEQS):
        steps = jnp.exp2(exponents_v[0, s : s + 1, :].astype(jnp.float32))
        diagonal = jnp.where(eye, steps, 0.0).astype(jnp.bfloat16)
        scales = jnp.dot(
            diagonal, jnp.ones((LEN, HEAD), jnp.bfloat16), preferred_element_type=jnp.float32
        )
        stored = stored_v[s].astype(jnp.float32)
        inputs = (stored + codes_v[0, s].astype(jnp.float32) * scales).astype(jnp.bfloat16)
        inputs_out[s] = inputs
        widened = inputs.astype(jnp.float32)
        pay[s * LEN : (s + 1) * LEN, :] = (widened * gains).astype(jnp.bfloat16)
        squares = widened * widened
        high = squares.astype(jnp.bfloat16)
        low = (squares - high.astype(jnp.float32)).astype(jnp.bfloat16)
        ones = jnp.ones((16, HEAD), jnp.bfloat16)
        total = lax.dot_general(ones, high, NT, preferred_element_type=jnp.float32)
        total += lax.dot_general(ones, low, NT, preferred_element_type=jnp.float32)
        sums.append(jnp.concatenate([total, jnp.zeros((16, HEAD - LEN), jnp.float32)], axis=1))
    row = lax.broadcasted_iota(jnp.int32, (16, HEAD), 0)
    value = jnp.where(row % 2 == 0, sums[0], sums[1])
    first = value.astype(jnp.bfloat16).astype(jnp.float32)
    second = value - first
    tail = jnp.where(row < 2, first, jnp.where(row < 4, second, 0.0))
    pay[ROWS:PAY, :] = tail.astype(jnp.bfloat16)

    copies[5].wait()
    kv_width = keyval.shape[1]
    per_row = CN * HEAD // kv_width
    for z in range(ZN):
        for core in range(CN):
            i = z * CN + core
            start = (i % per_row) * kv_width
            keyval_half_v[i // per_row, start : start + kv_width, :] = keyval_v[
                0, :, head_rows(z, far, core)
            ]
    last = pltpu.make_async_copy(
        keyval_half_v, packed.at[pl.ds(ZN, keyval_half_v.shape[0])], sems.at[6]
    )
    last.start()
    for load, store in zip(loads, stores):
        load.wait()
        store.start()
    last.wait()
    for store in stores:
        store.wait()


def head_rows(z, y, core):
    head = z * (YN * CN) + y * CN + core
    return pl.ds(pl.multiple_of(head * HEAD, HEAD), HEAD)


def half_rows(z, core):
    return pl.ds(pl.multiple_of((z * CN + core) * HEAD, HEAD), HEAD)


def keyval_kernel(here, there, weight, received, out, sums_out):
    y, core = lax.axis_index("y"), lax.axis_index("core")
    kv_width = weight.shape[1]
    sums = jnp.sum(here[:, ROWS:PAY, :].astype(jnp.float32), axis=0)
    sums += jnp.sum(there[:, ROWS:PAY, :].astype(jnp.float32), axis=0)
    sums = jnp.concatenate(
        [sums[s : s + 1, :LEN] + sums[SEQS + s : SEQS + s + 1, :LEN] for s in range(SEQS)], axis=1
    )
    high = sums.astype(jnp.bfloat16).astype(jnp.float32)
    row = lax.broadcasted_iota(jnp.int32, (PAY - ROWS, ROWS), 0)
    tail = jnp.where(row == 0, high, jnp.where(row == 1, sums - high, 0.0))
    sums_out[...] = tail.astype(jnp.bfloat16)
    acc = jnp.zeros((2 * kv_width, ROWS), jnp.float32)
    for z in range(ZN):
        block = jnp.concatenate([here[z, :ROWS, :], there[z, :ROWS, :]], axis=1)
        parts = []
        for side in (core, core ^ 1):
            start = ZN * CN * HEAD + (z * CN + side) * kv_width
            mine = weight[0, :, head_rows(z, y, side)]
            other = received[pl.ds(pl.multiple_of(start, kv_width), kv_width), :]
            parts.append(jnp.concatenate([mine, other], axis=0))
        part = jnp.concatenate(parts, axis=1)
        acc += lax.dot_general(part, block, NT, preferred_element_type=jnp.float32)
    out[...] = acc.astype(jnp.bfloat16)


def both_partials(here, there, weight, received):
    y, core = lax.axis_index("y"), lax.axis_index("core")
    acc = jnp.zeros((ROWS, 2 * HEAD), jnp.float32)
    for z in range(ZN):
        block = jnp.concatenate([here[z, :ROWS, :], there[z, :ROWS, :]], axis=1)
        parts = []
        for side in (core, core ^ 1):
            mine = weight[0, head_rows(z, y, side), :]
            other = received[half_rows(z, side), :]
            parts.append(jnp.concatenate([mine, other], axis=1))
        part = jnp.concatenate(parts, axis=0)
        acc += jnp.dot(block, part, preferred_element_type=jnp.float32)
    return acc


def query_kernel(here, there, weight, received, mine_out, other_out):
    acc = both_partials(here, there, weight, received)
    mine_out[...] = acc[:, :HEAD]
    other_out[...] = acc[:, HEAD:].astype(jnp.bfloat16)


def sum_kernel(near, far, cos_t, sin_t, out, factors_out):
    z_odd, y, core = lax.axis_index("z") % 2, lax.axis_index("y"), lax.axis_index("core")
    width = (near.shape[0] - (PAY - ROWS)) // 4
    tail = near[4 * width :, :].astype(jnp.float32) + far[4 * width :, :].astype(jnp.float32)
    square_sum = tail[0:1, :] + tail[1:2, :]
    inverse = lax.rsqrt(square_sum / (ZN * YN * CN * HEAD) + norm_eps)
    factors = jnp.broadcast_to(inverse, (width, ROWS))
    factors_out[...] = jnp.broadcast_to(inverse, (HEAD, ROWS)).T

    def piece(kind, which):
        plane = z_odd ^ kind
        a = near[pl.ds(pl.multiple_of((plane * 2 + (which ^ y)) * width, width), width), :]
        b = far[pl.ds(pl.multiple_of((plane * 2 + 1 - (which ^ y)) * width, width), width), :]
        return ((a.astype(jnp.float32) + b.astype(jnp.float32)) * factors).astype(jnp.bfloat16)

    first, second = piece(0, 0).astype(jnp.float32), piece(0, 1).astype(jnp.float32)
    rows = pl.ds(pl.multiple_of(core * width, width), width)
    c, s = cos_t[rows, :], sin_t[rows, :]
    out[0] = (first * c - second * s).astype(jnp.bfloat16)
    out[1] = (second * c + first * s).astype(jnp.bfloat16)
    out[2] = piece(1, 0)
    out[3] = piece(1, 1)


def rope_kernel(mine, other, factors, cos, sin, out):
    acc = (mine[...] + other[...].astype(jnp.float32)) * factors[...]
    first, second = acc[:, : HEAD // 2], acc[:, HEAD // 2 :]
    c, s = cos[...], sin[...]
    out[...] = jnp.concatenate(
        [first * c - second * s, second * c + first * s], axis=1
    ).astype(jnp.bfloat16)


def attention_kernel(query, own, sibling, out):
    core = lax.axis_index("core")
    keys_values = []
    for kind in range(2):
        parts = []
        for which in range(2):
            a, b = own[2 * kind + which], sibling[2 * kind + which]
            parts += [jnp.where(core == 0, a, b), jnp.where(core == 0, b, a)]
        keys_values.append(jnp.concatenate(parts, axis=0))
    keys, values = keys_values
    scores = jnp.dot(query[...], keys, preferred_element_type=jnp.float32) / math.sqrt(HEAD)
    row = lax.broadcasted_iota(jnp.int32, (ROWS, ROWS), 0)
    column = lax.broadcasted_iota(jnp.int32, (ROWS, ROWS), 1)
    allowed = (column <= row) & ((row < LEN) | (column >= LEN))
    scores = jnp.where(allowed, scores, -1e30)
    peak = jnp.max(scores, axis=-1, keepdims=True)
    raised = jnp.exp(scores - peak)
    weights = (raised / jnp.sum(raised, axis=-1, keepdims=True)).astype(jnp.bfloat16)
    context = lax.dot_general(weights, values, NT, preferred_element_type=jnp.float32)
    out[...] = context.astype(jnp.bfloat16)


def pack_kernel(weight, out):
    far = lax.axis_index("y") ^ 1
    for z in range(ZN):
        out[z] = weight[z, far]


def output_kernel(here, there, weight, received, mine_out, other_out):
    acc = both_partials(here, there, weight, received)
    mine_out[...] = acc[:, :HEAD]
    other_out[...] = acc[:, HEAD:].astype(jnp.bfloat16)


def message_kernel(ids, mine, other, inputs, buffer_out, message_out):
    section = lax.axis_index("section")
    for s in range(SEQS):
        rows = slice(s * LEN, (s + 1) * LEN)
        stored = buffer_out[0, ids[s, section]].astype(jnp.float32)
        mixed = mine[rows, :] + other[rows, :].astype(jnp.float32)
        message_out[s] = (inputs[s].astype(jnp.float32) + mixed - stored).astype(jnp.bfloat16)


def refresh_kernel(ids, message, buffer_out, new_out):
    section = lax.axis_index("section")
    new_out[...] = buffer_out[...]
    for s in range(SEQS):
        slot = ids[s, section]
        stored = buffer_out[0, slot].astype(jnp.float32)
        new_out[0, slot] = (stored + message[s].astype(jnp.float32)).astype(jnp.bfloat16)


def finish_kernel(ids, buffer_in, inputs, arrived, following_out, stored_out):
    section = lax.axis_index("section")
    before = jnp.maximum(section - 1, 0)
    stored_out[...] = buffer_in[...]
    for s in range(SEQS):
        stored_out[0, ids[s, section]] = inputs[s]
    results = []
    for s in range(SEQS):
        current = stored_out[0, ids[s, before]].astype(jnp.float32)
        results.append((current + arrived[s].astype(jnp.float32)).astype(jnp.bfloat16))
    for s in range(SEQS):
        following_out[0, s] = results[s]
        stored_out[0, ids[s, before]] = results[s]


def lane(z, y, core):
    return (z % ZN) * (YN * CN) + y * CN + core


def permute(x, target):
    pairs = [
        (lane(z, y, c), lane(*target(z, y, c)))
        for z in range(ZN)
        for y in range(YN)
        for c in range(CN)
    ]
    return lax.ppermute(x, LANES, pairs)


def swap(x, flip_y, flip_core):
    return permute(x, lambda z, y, c: (z, y ^ flip_y, c ^ flip_core))


def after(x, earlier):
    return lax.optimization_barrier((x, earlier))[0]


def gather_z(x):
    return lax.all_gather(x, "z", axis=0)


def per_device(
    codes, exponents, sample_ids, buffer_in, buffer_out, norm_gain, w_query, w_keyval, w_output
):
    cos, sin = rope_tables()
    sample_ids = sample_ids.T
    kv_width = w_keyval.shape[2]
    half = ZN * CN * HEAD
    w_keyval = jnp.swapaxes(w_keyval, 1, 2)
    partial_flops = 2 * ROWS * half * 256
    wide = shape((ROWS, HEAD), jnp.float32)

    any_spec = pl.BlockSpec(memory_space=pl.ANY)
    bf16, int32 = jnp.bfloat16, jnp.int32
    packed, pay, inputs = pl.pallas_call(
        prepare,
        out_shape=(
            shape((ZN + ZN * kv_width // HEAD, CN * HEAD, HEAD)),
            shape((PAY, HEAD)),
            shape((SEQS, LEN, HEAD)),
        ),
        in_specs=[SMEM] + [any_spec] * 6,
        out_specs=(any_spec, VMEM, VMEM),
        scratch_shapes=[
            pltpu.VMEM(codes.shape, int32),
            pltpu.VMEM(exponents.shape, int32),
            pltpu.VMEM((SEQS, LEN, HEAD), bf16),
            pltpu.VMEM(norm_gain.shape, bf16),
            pltpu.VMEM(w_keyval.shape, bf16),
            pltpu.VMEM((PIECES, ZN // PIECES, CN * HEAD, HEAD), bf16),
            pltpu.VMEM((ZN * kv_width // HEAD, CN * HEAD, HEAD), bf16),
            pltpu.SemaphoreType.DMA((7,)),
            pltpu.SemaphoreType.DMA((2, PIECES)),
        ],
        cost_estimate=pl.CostEstimate(flops=10**7, bytes_accessed=4 * 10**6, transcendentals=0),
    )(
        sample_ids, codes, exponents, buffer_in, norm_gain,
        w_query.reshape(ZN, YN, CN * HEAD, HEAD), w_keyval,
    )
    received = swap(packed, 1, 0).reshape(-1, HEAD)
    here = gather_z(pay)
    there = swap(here, 0, 1)
    packed_out = call(pack_kernel, shape((ZN, CN * HEAD, HEAD)), 1, 10**6, 2 * 10**6)(
        w_output.reshape(ZN, YN, CN * HEAD, HEAD)
    )
    received_out = swap(packed_out, 1, 0).reshape(half, HEAD)

    keyval, sums = call(
        keyval_kernel,
        (shape((2 * kv_width, ROWS)), shape((PAY - ROWS, ROWS))),
        4,
        partial_flops,
        5 * 10**6,
    )(here, there, w_keyval, received)
    even = permute(keyval, lambda z, y, c: (2 * z if z < 8 else 2 * (z - 8) + 1, y, c))
    odd = permute(keyval, lambda z, y, c: (2 * z + 1 if z < 8 else 2 * (z - 8), y, c))
    mine, other = call(
        query_kernel, (wide, shape((ROWS, HEAD))), 4, partial_flops, 6 * 10**6
    )(here, there, w_query, after(received, keyval))
    other = swap(other, 1, 0)
    near = after(jnp.concatenate([even, odd, sums]), mine)
    far = swap(near, 1, 0)
    own, factors = call(
        sum_kernel, (shape((4, kv_width, ROWS)), wide), 4, 10**6, 10**6
    )(after(near, received_out), far, cos.T.copy(), sin.T.copy())
    sibling = swap(own, 0, 1)
    queries = call(rope_kernel, shape((ROWS, HEAD)), 5, 10**6, 10**6)(
        mine, other, factors, cos, sin
    )
    context = call(attention_kernel, shape((ROWS, HEAD)), 3, 4 * ROWS * ROWS * HEAD, 10**6)(
        queries, own, sibling
    )

    here = gather_z(context)
    there = swap(here, 0, 1)
    mine, other = call(
        output_kernel, (wide, shape((ROWS, HEAD))), 4, partial_flops, 6 * 10**6
    )(here, there, w_output, received_out)
    other = swap(other, 1, 0)
    message = call(
        message_kernel, shape((SEQS, LEN, HEAD)), 5, 10**6, 10**6, smem=(0,)
    )(sample_ids, mine, other, inputs, buffer_out)

    sections = lax.axis_size("section")
    arrived = lax.ppermute(message, "section", [(i, i + 1) for i in range(sections - 1)])
    following, new_in = call(
        finish_kernel,
        (shape((1, SEQS, LEN, HEAD)), shape(buffer_in.shape)),
        4,
        10**6,
        10**6,
        smem=(0,),
    )(sample_ids, buffer_in, inputs, arrived)
    new_out = call(refresh_kernel, shape(buffer_out.shape), 3, 10**6, 10**6, smem=(0,))(
        sample_ids, message, buffer_out
    )
    return following, new_in, new_out


def solution(mesh):
    sections = mesh.shape["section"]
    fine = Mesh(mesh.devices.reshape(sections, ZN, YN, CN), ("section",) + LANES)
    return jax.shard_map(
        per_device,
        mesh=fine,
        in_specs=(
            P("section", None, None, LANES),
            P("section", None, None),
            P(),
            P("section", None, None, LANES),
            P("section", None, None, LANES),
            P("section", LANES),
            P("section", None, LANES),
            P("section", None, LANES),
            P("section", None, LANES),
        ),
        out_specs=(
            P("section", None, None, LANES),
            P("section", None, None, LANES),
            P("section", None, None, LANES),
        ),
        check_vma=False,
    )
```

```python
import functools
import math

import jax
import jax.numpy as jnp
import numpy as np
from jax import lax
from jax.experimental import pallas as pl
from jax.experimental.pallas import tpu as pltpu
from jax.sharding import Mesh
from jax.sharding import PartitionSpec as P

SEQS, LEN, SLOTS, HEAD, KV_HEADS = 2, 112, 3, 128, 8
ROWS = SEQS * LEN
PAY = ROWS + 16
ZN, YN, CN = 16, 2, 2
PIECES = 4
EARLY = 3
LANES = ("z", "y", "core")
rope_base = 500000.0
norm_eps = 1e-05

VMEM = pl.BlockSpec(memory_space=pltpu.VMEM)
SMEM = pl.BlockSpec(memory_space=pltpu.SMEM)
PARAMS = pltpu.CompilerParams(vmem_limit_bytes=40 * 1024 * 1024)
NT = (((1,), (1,)), ((), ()))


def rope_tables():
    half = HEAD // 2
    frequency = np.exp(np.arange(half) * (-2.0 * math.log(rope_base) / HEAD))
    positions = np.arange(ROWS) % LEN
    angle = positions[:, None] * frequency[None, :]
    return np.cos(angle).astype(np.float32), np.sin(angle).astype(np.float32)


def call(kernel, outs, n_in, flops, bytes_accessed, smem=(), scratch=()):
    return pl.pallas_call(
        kernel,
        out_shape=outs,
        in_specs=[SMEM if i in smem else VMEM for i in range(n_in)],
        out_specs=jax.tree.map(lambda _: VMEM, outs),
        scratch_shapes=list(scratch),
        compiler_params=PARAMS,
        cost_estimate=pl.CostEstimate(
            flops=flops, bytes_accessed=bytes_accessed, transcendentals=0
        ),
    )


def shape(dims, dtype=jnp.bfloat16):
    return jax.ShapeDtypeStruct(dims, dtype)


def prepare(
    ids, codes, exponents, buffer_in, gain, query, keyval, output,
    packed, pay_out, inputs_out,
    codes_v, exponents_v, stored_v, gain_v, keyval_v, half_v, keyval_half_v, early_v, pay, inputs_v,
    sems, half_sems,
):
    section = lax.axis_index("section")
    far = lax.axis_index("y") ^ 1
    copies = [
        pltpu.make_async_copy(exponents, exponents_v, sems.at[0]),
        pltpu.make_async_copy(gain, gain_v, sems.at[1]),
        pltpu.make_async_copy(codes, codes_v, sems.at[2]),
        pltpu.make_async_copy(buffer_in.at[0, ids[0, section]], stored_v.at[0], sems.at[3]),
        pltpu.make_async_copy(buffer_in.at[0, ids[1, section]], stored_v.at[1], sems.at[4]),
        pltpu.make_async_copy(keyval, keyval_v, sems.at[5]),
    ]
    for item in copies:
        item.start()

    step = ZN // PIECES
    moves = [
        (query.at[pl.ds(i * step, step), far], half_v.at[i], packed.at[pl.ds(i * step, step)])
        for i in range(PIECES)
    ]
    tail = ZN + keyval_half_v.shape[0]
    moves.append((output.at[pl.ds(0, EARLY), far], early_v, packed.at[pl.ds(tail, EARLY)]))
    loads, stores = [], []
    for i, (source, between, target) in enumerate(moves):
        loads.append(pltpu.make_async_copy(source, between, half_sems.at[0, i]))
        stores.append(pltpu.make_async_copy(between, target, half_sems.at[1, i]))
        loads[-1].start()
    for item in copies[:5]:
        item.wait()
    eye = lax.broadcasted_iota(jnp.int32, (LEN, LEN), 0) == lax.broadcasted_iota(
        jnp.int32, (LEN, LEN), 1
    )
    gains = gain_v[...].astype(jnp.float32)
    sums = []
    for s in range(SEQS):
        steps = jnp.exp2(exponents_v[0, s : s + 1, :].astype(jnp.float32))
        diagonal = jnp.where(eye, steps, 0.0).astype(jnp.bfloat16)
        scales = jnp.dot(
            diagonal, jnp.ones((LEN, HEAD), jnp.bfloat16), preferred_element_type=jnp.float32
        )
        stored = stored_v[s].astype(jnp.float32)
        inputs = (stored + codes_v[0, s].astype(jnp.float32) * scales).astype(jnp.bfloat16)
        inputs_v[s] = inputs
        widened = inputs.astype(jnp.float32)
        pay[s * LEN : (s + 1) * LEN, :] = (widened * gains).astype(jnp.bfloat16)
        squares = widened * widened
        high = squares.astype(jnp.bfloat16)
        low = (squares - high.astype(jnp.float32)).astype(jnp.bfloat16)
        ones = jnp.ones((16, HEAD), jnp.bfloat16)
        total = lax.dot_general(ones, high, NT, preferred_element_type=jnp.float32)
        total += lax.dot_general(ones, low, NT, preferred_element_type=jnp.float32)
        sums.append(jnp.concatenate([total, jnp.zeros((16, HEAD - LEN), jnp.float32)], axis=1))
    row = lax.broadcasted_iota(jnp.int32, (16, HEAD), 0)
    value = jnp.where(row % 2 == 0, sums[0], sums[1])
    first = value.astype(jnp.bfloat16).astype(jnp.float32)
    second = value - first
    tail = jnp.where(row < 2, first, jnp.where(row < 4, second, 0.0))
    pay[ROWS:PAY, :] = tail.astype(jnp.bfloat16)
    stores.append(pltpu.make_async_copy(pay, pay_out, sems.at[7]))
    stores[-1].start()
    stores.append(pltpu.make_async_copy(inputs_v, inputs_out, sems.at[8]))
    stores[-1].start()

    copies[5].wait()
    kv_width = keyval.shape[1]
    per_row = CN * HEAD // kv_width
    for z in range(ZN):
        for core in range(CN):
            i = z * CN + core
            start = (i % per_row) * kv_width
            keyval_half_v[i // per_row, start : start + kv_width, :] = keyval_v[
                0, :, head_rows(z, far, core)
            ]
    last = pltpu.make_async_copy(
        keyval_half_v, packed.at[pl.ds(ZN, keyval_half_v.shape[0])], sems.at[6]
    )
    last.start()
    for load, store in zip(loads, stores):
        load.wait()
        store.start()
    last.wait()
    for store in stores:
        store.wait()


def head_rows(z, y, core):
    head = z * (YN * CN) + y * CN + core
    return pl.ds(pl.multiple_of(head * HEAD, HEAD), HEAD)


def half_rows(z, core):
    return pl.ds(pl.multiple_of((z * CN + core) * HEAD, HEAD), HEAD)


def keyval_kernel(here, there, weight, received, out, sums_out):
    y, core = lax.axis_index("y"), lax.axis_index("core")
    kv_width = weight.shape[1]
    sums = jnp.sum(here[:, ROWS:PAY, :].astype(jnp.float32), axis=0)
    sums += jnp.sum(there[:, ROWS:PAY, :].astype(jnp.float32), axis=0)
    sums = jnp.concatenate(
        [sums[s : s + 1, :LEN] + sums[SEQS + s : SEQS + s + 1, :LEN] for s in range(SEQS)], axis=1
    )
    high = sums.astype(jnp.bfloat16).astype(jnp.float32)
    row = lax.broadcasted_iota(jnp.int32, (PAY - ROWS, ROWS), 0)
    tail = jnp.where(row == 0, high, jnp.where(row == 1, sums - high, 0.0))
    sums_out[...] = tail.astype(jnp.bfloat16)
    acc = jnp.zeros((2 * kv_width, ROWS), jnp.float32)
    for z in range(ZN):
        block = jnp.concatenate([here[z, :ROWS, :], there[z, :ROWS, :]], axis=1)
        parts = []
        for side in (core, core ^ 1):
            start = ZN * CN * HEAD + (z * CN + side) * kv_width
            mine = weight[0, :, head_rows(z, y, side)]
            other = received[pl.ds(pl.multiple_of(start, kv_width), kv_width), :]
            parts.append(jnp.concatenate([mine, other], axis=0))
        part = jnp.concatenate(parts, axis=1)
        acc += lax.dot_general(part, block, NT, preferred_element_type=jnp.float32)
    out[...] = acc.astype(jnp.bfloat16)


def both_partials(here, there, weight, received_rows):
    y, core = lax.axis_index("y"), lax.axis_index("core")
    acc = jnp.zeros((ROWS, 2 * HEAD), jnp.float32)
    for z in range(ZN):
        block = jnp.concatenate([here[z, :ROWS, :], there[z, :ROWS, :]], axis=1)
        parts = []
        for side in (core, core ^ 1):
            mine = weight[0, head_rows(z, y, side), :]
            other = received_rows(z, side)
            parts.append(jnp.concatenate([mine, other], axis=1))
        part = jnp.concatenate(parts, axis=0)
        acc += jnp.dot(block, part, preferred_element_type=jnp.float32)
    return acc


def query_kernel(here, there, weight, received, mine_out, other_out):
    acc = both_partials(here, there, weight, lambda z, side: received[half_rows(z, side), :])
    mine_out[...] = acc[:, :HEAD]
    other_out[...] = acc[:, HEAD:].astype(jnp.bfloat16)


def sum_kernel(near, far, cos_t, sin_t, out, factors_out):
    z_odd, y, core = lax.axis_index("z") % 2, lax.axis_index("y"), lax.axis_index("core")
    width = (near.shape[0] - (PAY - ROWS)) // 4
    tail = near[4 * width :, :].astype(jnp.float32) + far[4 * width :, :].astype(jnp.float32)
    square_sum = tail[0:1, :] + tail[1:2, :]
    inverse = lax.rsqrt(square_sum / (ZN * YN * CN * HEAD) + norm_eps)
    factors = jnp.broadcast_to(inverse, (width, ROWS))
    factors_out[...] = jnp.broadcast_to(inverse, (HEAD, ROWS)).T

    def piece(kind, which):
        plane = z_odd ^ kind
        a = near[pl.ds(pl.multiple_of((plane * 2 + (which ^ y)) * width, width), width), :]
        b = far[pl.ds(pl.multiple_of((plane * 2 + 1 - (which ^ y)) * width, width), width), :]
        return ((a.astype(jnp.float32) + b.astype(jnp.float32)) * factors).astype(jnp.bfloat16)

    first, second = piece(0, 0).astype(jnp.float32), piece(0, 1).astype(jnp.float32)
    rows = pl.ds(pl.multiple_of(core * width, width), width)
    c, s = cos_t[rows, :], sin_t[rows, :]
    out[0] = (first * c - second * s).astype(jnp.bfloat16)
    out[1] = (second * c + first * s).astype(jnp.bfloat16)
    out[2] = piece(1, 0)
    out[3] = piece(1, 1)


def rope_kernel(mine, other, factors, cos, sin, out):
    acc = (mine[...] + other[...].astype(jnp.float32)) * factors[...]
    first, second = acc[:, : HEAD // 2], acc[:, HEAD // 2 :]
    c, s = cos[...], sin[...]
    out[...] = jnp.concatenate(
        [first * c - second * s, second * c + first * s], axis=1
    ).astype(jnp.bfloat16)


def attention_kernel(query, own, sibling, out):
    core = lax.axis_index("core")
    keys_values = []
    for kind in range(2):
        parts = []
        for which in range(2):
            a, b = own[2 * kind + which], sibling[2 * kind + which]
            parts += [jnp.where(core == 0, a, b), jnp.where(core == 0, b, a)]
        keys_values.append(jnp.concatenate(parts, axis=0))
    keys, values = keys_values
    scores = jnp.dot(query[...], keys, preferred_element_type=jnp.float32) / math.sqrt(HEAD)
    row = lax.broadcasted_iota(jnp.int32, (ROWS, ROWS), 0)
    column = lax.broadcasted_iota(jnp.int32, (ROWS, ROWS), 1)
    allowed = (column <= row) & ((row < LEN) | (column >= LEN))
    scores = jnp.where(allowed, scores, -1e30)
    peak = jnp.max(scores, axis=-1, keepdims=True)
    raised = jnp.exp(scores - peak)
    weights = (raised / jnp.sum(raised, axis=-1, keepdims=True)).astype(jnp.bfloat16)
    context = lax.dot_general(weights, values, NT, preferred_element_type=jnp.float32)
    out[...] = context.astype(jnp.bfloat16)


def pack_kernel(weight, out):
    far = lax.axis_index("y") ^ 1
    for z in range(EARLY, ZN):
        out[z - EARLY] = weight[z, far]


def output_kernel(here, there, weight, early, received, mine_out, other_out):
    def received_rows(z, side):
        if z < EARLY:
            return early[half_rows(z, side), :]
        return received[half_rows(z - EARLY, side), :]

    acc = both_partials(here, there, weight, received_rows)
    mine_out[...] = acc[:, :HEAD]
    other_out[...] = acc[:, HEAD:].astype(jnp.bfloat16)


def message_kernel(ids, mine, other, inputs, buffer_out, message_out):
    section = lax.axis_index("section")
    for s in range(SEQS):
        rows = slice(s * LEN, (s + 1) * LEN)
        stored = buffer_out[0, ids[s, section]].astype(jnp.float32)
        mixed = mine[rows, :] + other[rows, :].astype(jnp.float32)
        message_out[s] = (inputs[s].astype(jnp.float32) + mixed - stored).astype(jnp.bfloat16)


def refresh_kernel(ids, message, buffer_out, new_out):
    section = lax.axis_index("section")
    new_out[...] = buffer_out[...]
    for s in range(SEQS):
        slot = ids[s, section]
        stored = buffer_out[0, slot].astype(jnp.float32)
        new_out[0, slot] = (stored + message[s].astype(jnp.float32)).astype(jnp.bfloat16)


def finish_kernel(ids, buffer_in, inputs, arrived, following_out, stored_out):
    section = lax.axis_index("section")
    before = jnp.maximum(section - 1, 0)
    stored_out[...] = buffer_in[...]
    for s in range(SEQS):
        stored_out[0, ids[s, section]] = inputs[s]
    results = []
    for s in range(SEQS):
        current = stored_out[0, ids[s, before]].astype(jnp.float32)
        results.append((current + arrived[s].astype(jnp.float32)).astype(jnp.bfloat16))
    for s in range(SEQS):
        following_out[0, s] = results[s]
        stored_out[0, ids[s, before]] = results[s]


def lane(z, y, core):
    return (z % ZN) * (YN * CN) + y * CN + core


def permute(x, target):
    pairs = [
        (lane(z, y, c), lane(*target(z, y, c)))
        for z in range(ZN)
        for y in range(YN)
        for c in range(CN)
    ]
    return lax.ppermute(x, LANES, pairs)


def swap(x, flip_y, flip_core):
    return permute(x, lambda z, y, c: (z, y ^ flip_y, c ^ flip_core))


def after(x, earlier):
    return lax.optimization_barrier((x, earlier))[0]


def gather_z(x):
    return lax.all_gather(x, "z", axis=0)


def per_device(
    codes, exponents, sample_ids, buffer_in, buffer_out, norm_gain, w_query, w_keyval, w_output
):
    cos, sin = rope_tables()
    sample_ids = sample_ids.T
    kv_width = w_keyval.shape[2]
    half = ZN * CN * HEAD
    w_keyval = jnp.swapaxes(w_keyval, 1, 2)
    partial_flops = 2 * ROWS * half * 256
    wide = shape((ROWS, HEAD), jnp.float32)

    by_half = (ZN, YN, CN * HEAD, HEAD)
    any_spec = pl.BlockSpec(memory_space=pl.ANY)
    bf16, int32 = jnp.bfloat16, jnp.int32
    packed, pay, inputs = pl.pallas_call(
        prepare,
        out_shape=(
            shape((ZN + ZN * kv_width // HEAD + EARLY, CN * HEAD, HEAD)),
            shape((PAY, HEAD)),
            shape((SEQS, LEN, HEAD)),
        ),
        in_specs=[SMEM] + [any_spec] * 7,
        out_specs=(any_spec,) * 3,
        scratch_shapes=[
            pltpu.VMEM(codes.shape, int32),
            pltpu.VMEM(exponents.shape, int32),
            pltpu.VMEM((SEQS, LEN, HEAD), bf16),
            pltpu.VMEM(norm_gain.shape, bf16),
            pltpu.VMEM(w_keyval.shape, bf16),
            pltpu.VMEM((PIECES, ZN // PIECES, CN * HEAD, HEAD), bf16),
            pltpu.VMEM((ZN * kv_width // HEAD, CN * HEAD, HEAD), bf16),
            pltpu.VMEM((EARLY, CN * HEAD, HEAD), bf16),
            pltpu.VMEM((PAY, HEAD), bf16),
            pltpu.VMEM((SEQS, LEN, HEAD), bf16),
            pltpu.SemaphoreType.DMA((9,)),
            pltpu.SemaphoreType.DMA((2, PIECES + 1)),
        ],
        cost_estimate=pl.CostEstimate(flops=10**7, bytes_accessed=4 * 10**6, transcendentals=0),
    )(
        sample_ids, codes, exponents, buffer_in, norm_gain,
        w_query.reshape(by_half), w_keyval, w_output.reshape(by_half),
    )
    received = swap(packed, 1, 0).reshape(-1, HEAD)
    here = gather_z(pay)
    there = swap(here, 0, 1)
    packed_out = call(pack_kernel, shape((ZN - EARLY, CN * HEAD, HEAD)), 1, 10**6, 2 * 10**6)(
        w_output.reshape(by_half)
    )
    received_out = swap(packed_out, 1, 0).reshape(-1, HEAD)

    keyval, sums = call(
        keyval_kernel,
        (shape((2 * kv_width, ROWS)), shape((PAY - ROWS, ROWS))),
        4,
        partial_flops,
        5 * 10**6,
    )(here, there, w_keyval, received)
    even = permute(keyval, lambda z, y, c: (2 * z if z < 8 else 2 * (z - 8) + 1, y, c))
    odd = permute(keyval, lambda z, y, c: (2 * z + 1 if z < 8 else 2 * (z - 8), y, c))
    mine, other = call(
        query_kernel, (wide, shape((ROWS, HEAD))), 4, partial_flops, 6 * 10**6
    )(here, there, w_query, after(received, keyval))
    other = swap(other, 1, 0)
    near = after(jnp.concatenate([even, odd, sums]), mine)
    far = swap(near, 1, 0)
    own, factors = call(
        sum_kernel, (shape((4, kv_width, ROWS)), wide), 4, 10**6, 10**6
    )(after(near, received_out), far, cos.T.copy(), sin.T.copy())
    sibling = swap(own, 0, 1)
    queries = call(rope_kernel, shape((ROWS, HEAD)), 5, 10**6, 10**6)(
        mine, other, factors, cos, sin
    )
    context = call(attention_kernel, shape((ROWS, HEAD)), 3, 4 * ROWS * ROWS * HEAD, 10**6)(
        queries, own, sibling
    )

    here = gather_z(context)
    there = swap(here, 0, 1)
    mine, other = call(
        output_kernel, (wide, shape((ROWS, HEAD))), 5, partial_flops, 6 * 10**6
    )(here, there, w_output, received[-EARLY * CN * HEAD :], received_out)
    other = swap(other, 1, 0)
    message = call(
        message_kernel, shape((SEQS, LEN, HEAD)), 5, 10**6, 10**6, smem=(0,)
    )(sample_ids, mine, other, inputs, buffer_out)

    sections = lax.axis_size("section")
    arrived = lax.ppermute(message, "section", [(i, i + 1) for i in range(sections - 1)])
    following, new_in = call(
        finish_kernel,
        (shape((1, SEQS, LEN, HEAD)), shape(buffer_in.shape)),
        4,
        10**6,
        10**6,
        smem=(0,),
    )(sample_ids, buffer_in, inputs, arrived)
    new_out = call(refresh_kernel, shape(buffer_out.shape), 3, 10**6, 10**6, smem=(0,))(
        sample_ids, message, buffer_out
    )
    return following, new_in, new_out


def solution(mesh):
    sections = mesh.shape["section"]
    fine = Mesh(mesh.devices.reshape(sections, ZN, YN, CN), ("section",) + LANES)
    return jax.shard_map(
        per_device,
        mesh=fine,
        in_specs=(
            P("section", None, None, LANES),
            P("section", None, None),
            P(),
            P("section", None, None, LANES),
            P("section", None, None, LANES),
            P("section", LANES),
            P("section", None, LANES),
            P("section", None, LANES),
            P("section", None, LANES),
        ),
        out_specs=(
            P("section", None, None, LANES),
            P("section", None, None, LANES),
            P("section", None, None, LANES),
        ),
        check_vma=False,
    )
```

```python
import functools
import math

import jax
import jax.numpy as jnp
import numpy as np
from jax import lax
from jax.experimental import pallas as pl
from jax.experimental.pallas import tpu as pltpu
from jax.sharding import Mesh
from jax.sharding import PartitionSpec as P

SEQS, LEN, SLOTS, HEAD, KV_HEADS = 2, 112, 3, 128, 8
ROWS = SEQS * LEN
PAY = ROWS + 16
ZN, YN, CN = 16, 2, 2
PIECES = 4
LANES = ("z", "y", "core")
rope_base = 500000.0
norm_eps = 1e-05

VMEM = pl.BlockSpec(memory_space=pltpu.VMEM)
SMEM = pl.BlockSpec(memory_space=pltpu.SMEM)
PARAMS = pltpu.CompilerParams(vmem_limit_bytes=40 * 1024 * 1024)
NT = (((1,), (1,)), ((), ()))


def rope_tables():
    half = HEAD // 2
    frequency = np.exp(np.arange(half) * (-2.0 * math.log(rope_base) / HEAD))
    positions = np.arange(ROWS) % LEN
    angle = positions[:, None] * frequency[None, :]
    return np.cos(angle).astype(np.float32), np.sin(angle).astype(np.float32)


def call(kernel, outs, n_in, flops, bytes_accessed, smem=(), scratch=()):
    return pl.pallas_call(
        kernel,
        out_shape=outs,
        in_specs=[SMEM if i in smem else VMEM for i in range(n_in)],
        out_specs=jax.tree.map(lambda _: VMEM, outs),
        scratch_shapes=list(scratch),
        compiler_params=PARAMS,
        cost_estimate=pl.CostEstimate(
            flops=flops, bytes_accessed=bytes_accessed, transcendentals=0
        ),
    )


def shape(dims, dtype=jnp.bfloat16):
    return jax.ShapeDtypeStruct(dims, dtype)


def prepare(
    ids, codes, exponents, buffer_in, gain, query, keyval,
    packed, pay_out, inputs_out,
    codes_v, exponents_v, stored_v, gain_v, keyval_v, half_v, keyval_half_v, pay, inputs_v,
    sems, half_sems,
):
    section = lax.axis_index("section")
    far = lax.axis_index("y") ^ 1
    copies = [
        pltpu.make_async_copy(exponents, exponents_v, sems.at[0]),
        pltpu.make_async_copy(gain, gain_v, sems.at[1]),
        pltpu.make_async_copy(codes, codes_v, sems.at[2]),
        pltpu.make_async_copy(buffer_in.at[0, ids[0, section]], stored_v.at[0], sems.at[3]),
        pltpu.make_async_copy(buffer_in.at[0, ids[1, section]], stored_v.at[1], sems.at[4]),
        pltpu.make_async_copy(keyval, keyval_v, sems.at[5]),
    ]
    for item in copies:
        item.start()

    step = ZN // PIECES
    moves = [
        (query.at[pl.ds(i * step, step), far], half_v.at[i], packed.at[pl.ds(i * step, step)])
        for i in range(PIECES)
    ]
    loads, stores = [], []
    for i, (source, between, target) in enumerate(moves):
        loads.append(pltpu.make_async_copy(source, between, half_sems.at[0, i]))
        stores.append(pltpu.make_async_copy(between, target, half_sems.at[1, i]))
        loads[-1].start()
    for item in copies[:5]:
        item.wait()
    eye = lax.broadcasted_iota(jnp.int32, (LEN, LEN), 0) == lax.broadcasted_iota(
        jnp.int32, (LEN, LEN), 1
    )
    gains = gain_v[...].astype(jnp.float32)
    sums = []
    for s in range(SEQS):
        steps = jnp.exp2(exponents_v[0, s : s + 1, :].astype(jnp.float32))
        diagonal = jnp.where(eye, steps, 0.0).astype(jnp.bfloat16)
        scales = jnp.dot(
            diagonal, jnp.ones((LEN, HEAD), jnp.bfloat16), preferred_element_type=jnp.float32
        )
        stored = stored_v[s].astype(jnp.float32)
        inputs = (stored + codes_v[0, s].astype(jnp.float32) * scales).astype(jnp.bfloat16)
        inputs_v[s] = inputs
        widened = inputs.astype(jnp.float32)
        pay[s * LEN : (s + 1) * LEN, :] = (widened * gains).astype(jnp.bfloat16)
        squares = widened * widened
        high = squares.astype(jnp.bfloat16)
        low = (squares - high.astype(jnp.float32)).astype(jnp.bfloat16)
        ones = jnp.ones((16, HEAD), jnp.bfloat16)
        total = lax.dot_general(ones, high, NT, preferred_element_type=jnp.float32)
        total += lax.dot_general(ones, low, NT, preferred_element_type=jnp.float32)
        sums.append(jnp.concatenate([total, jnp.zeros((16, HEAD - LEN), jnp.float32)], axis=1))
    row = lax.broadcasted_iota(jnp.int32, (16, HEAD), 0)
    value = jnp.where(row % 2 == 0, sums[0], sums[1])
    first = value.astype(jnp.bfloat16).astype(jnp.float32)
    second = value - first
    tail = jnp.where(row < 2, first, jnp.where(row < 4, second, 0.0))
    pay[ROWS:PAY, :] = tail.astype(jnp.bfloat16)
    stores.append(pltpu.make_async_copy(pay, pay_out, sems.at[7]))
    stores[-1].start()
    stores.append(pltpu.make_async_copy(inputs_v, inputs_out, sems.at[8]))
    stores[-1].start()

    copies[5].wait()
    kv_width = keyval.shape[1]
    per_row = CN * HEAD // kv_width
    for z in range(ZN):
        for core in range(CN):
            i = z * CN + core
            start = (i % per_row) * kv_width
            keyval_half_v[i // per_row, start : start + kv_width, :] = keyval_v[
                0, :, head_rows(z, far, core)
            ]
    last = pltpu.make_async_copy(
        keyval_half_v, packed.at[pl.ds(ZN, keyval_half_v.shape[0])], sems.at[6]
    )
    last.start()
    for load, store in zip(loads, stores):
        load.wait()
        store.start()
    last.wait()
    for store in stores:
        store.wait()


def head_rows(z, y, core):
    head = z * (YN * CN) + y * CN + core
    return pl.ds(pl.multiple_of(head * HEAD, HEAD), HEAD)


def half_rows(z, core):
    return pl.ds(pl.multiple_of((z * CN + core) * HEAD, HEAD), HEAD)


def keyval_kernel(here, there, weight, received, out, sums_out):
    y, core = lax.axis_index("y"), lax.axis_index("core")
    kv_width = weight.shape[1]
    sums = jnp.sum(here[:, ROWS:PAY, :].astype(jnp.float32), axis=0)
    sums += jnp.sum(there[:, ROWS:PAY, :].astype(jnp.float32), axis=0)
    sums = jnp.concatenate(
        [sums[s : s + 1, :LEN] + sums[SEQS + s : SEQS + s + 1, :LEN] for s in range(SEQS)], axis=1
    )
    high = sums.astype(jnp.bfloat16).astype(jnp.float32)
    row = lax.broadcasted_iota(jnp.int32, (PAY - ROWS, ROWS), 0)
    tail = jnp.where(row == 0, high, jnp.where(row == 1, sums - high, 0.0))
    sums_out[...] = tail.astype(jnp.bfloat16)
    acc = jnp.zeros((2 * kv_width, ROWS), jnp.float32)
    for z in range(ZN):
        block = jnp.concatenate([here[z, :ROWS, :], there[z, :ROWS, :]], axis=1)
        parts = []
        for side in (core, core ^ 1):
            start = ZN * CN * HEAD + (z * CN + side) * kv_width
            mine = weight[0, :, head_rows(z, y, side)]
            other = received[pl.ds(pl.multiple_of(start, kv_width), kv_width), :]
            parts.append(jnp.concatenate([mine, other], axis=0))
        part = jnp.concatenate(parts, axis=1)
        acc += lax.dot_general(part, block, NT, preferred_element_type=jnp.float32)
    out[...] = acc.astype(jnp.bfloat16)


def both_partials(here, there, weight, received):
    y, core = lax.axis_index("y"), lax.axis_index("core")
    acc = jnp.zeros((ROWS, 2 * HEAD), jnp.float32)
    for z in range(ZN):
        block = jnp.concatenate([here[z, :ROWS, :], there[z, :ROWS, :]], axis=1)
        parts = []
        for side in (core, core ^ 1):
            mine = weight[0, head_rows(z, y, side), :]
            other = received[half_rows(z, side), :]
            parts.append(jnp.concatenate([mine, other], axis=1))
        part = jnp.concatenate(parts, axis=0)
        acc += jnp.dot(block, part, preferred_element_type=jnp.float32)
    return acc


def query_kernel(here, there, weight, received, mine_out, other_out):
    acc = both_partials(here, there, weight, received)
    mine_out[...] = acc[:, :HEAD]
    other_out[...] = acc[:, HEAD:].astype(jnp.bfloat16)


def sum_kernel(near, far, cos_t, sin_t, out, factors_out):
    even, y, core = lax.axis_index("z") % 2 == 0, lax.axis_index("y"), lax.axis_index("core")
    width = (near.shape[0] - (PAY - ROWS)) // 2
    tail = near[2 * width :, :].astype(jnp.float32) + far[2 * width :, :].astype(jnp.float32)
    square_sum = tail[0:1, :] + tail[1:2, :]
    inverse = lax.rsqrt(square_sum / (ZN * YN * CN * HEAD) + norm_eps)
    factors = jnp.broadcast_to(inverse, (width, ROWS))
    factors_out[...] = jnp.broadcast_to(inverse, (HEAD, ROWS)).T

    def piece(which):
        a = near[pl.ds(pl.multiple_of((which ^ y) * width, width), width), :]
        b = far[pl.ds(pl.multiple_of((1 - (which ^ y)) * width, width), width), :]
        total = (a.astype(jnp.float32) + b.astype(jnp.float32)) * factors
        return total.astype(jnp.bfloat16).astype(jnp.float32)

    first, second = piece(0), piece(1)
    rows = pl.ds(pl.multiple_of(core * width, width), width)
    c, s = cos_t[rows, :], sin_t[rows, :]
    out[0] = jnp.where(even, first * c - second * s, first).astype(jnp.bfloat16)
    out[1] = jnp.where(even, second * c + first * s, second).astype(jnp.bfloat16)


def rope_kernel(mine, other, factors, cos, sin, out):
    acc = (mine[...] + other[...].astype(jnp.float32)) * factors[...]
    first, second = acc[:, : HEAD // 2], acc[:, HEAD // 2 :]
    c, s = cos[...], sin[...]
    out[...] = jnp.concatenate(
        [first * c - second * s, second * c + first * s], axis=1
    ).astype(jnp.bfloat16)


def attention_kernel(query, own, sibling, out):
    even, core = lax.axis_index("z") % 2 == 0, lax.axis_index("core")
    planes = []
    for plane in range(2):
        parts = []
        for which in range(2):
            a, b = own[plane, which], sibling[plane, which]
            parts += [jnp.where(core == 0, a, b), jnp.where(core == 0, b, a)]
        planes.append(jnp.concatenate(parts, axis=0))
    keys = jnp.where(even, planes[0], planes[1])
    values = jnp.where(even, planes[1], planes[0])
    scores = jnp.dot(query[...], keys, preferred_element_type=jnp.float32) / math.sqrt(HEAD)
    row = lax.broadcasted_iota(jnp.int32, (ROWS, ROWS), 0)
    column = lax.broadcasted_iota(jnp.int32, (ROWS, ROWS), 1)
    allowed = (column <= row) & ((row < LEN) | (column >= LEN))
    scores = jnp.where(allowed, scores, -1e30)
    peak = jnp.max(scores, axis=-1, keepdims=True)
    raised = jnp.exp(scores - peak)
    weights = (raised / jnp.sum(raised, axis=-1, keepdims=True)).astype(jnp.bfloat16)
    context = lax.dot_general(weights, values, NT, preferred_element_type=jnp.float32)
    out[...] = context.astype(jnp.bfloat16)


def pack_kernel(weight, out):
    far = lax.axis_index("y") ^ 1
    for z in range(ZN):
        out[z] = weight[z, far]


def output_kernel(here, there, weight, received, mine_out, other_out):
    acc = both_partials(here, there, weight, received)
    mine_out[...] = acc[:, :HEAD]
    other_out[...] = acc[:, HEAD:].astype(jnp.bfloat16)


def message_kernel(ids, mine, other, inputs, buffer_out, message_out):
    section = lax.axis_index("section")
    for s in range(SEQS):
        rows = slice(s * LEN, (s + 1) * LEN)
        stored = buffer_out[0, ids[s, section]].astype(jnp.float32)
        mixed = mine[rows, :] + other[rows, :].astype(jnp.float32)
        message_out[s] = (inputs[s].astype(jnp.float32) + mixed - stored).astype(jnp.bfloat16)


def refresh_kernel(ids, message, buffer_out, new_out):
    section = lax.axis_index("section")
    new_out[...] = buffer_out[...]
    for s in range(SEQS):
        slot = ids[s, section]
        stored = buffer_out[0, slot].astype(jnp.float32)
        new_out[0, slot] = (stored + message[s].astype(jnp.float32)).astype(jnp.bfloat16)


def finish_kernel(ids, buffer_in, inputs, arrived, following_out, stored_out):
    section = lax.axis_index("section")
    before = jnp.maximum(section - 1, 0)
    stored_out[...] = buffer_in[...]
    for s in range(SEQS):
        stored_out[0, ids[s, section]] = inputs[s]
    results = []
    for s in range(SEQS):
        current = stored_out[0, ids[s, before]].astype(jnp.float32)
        results.append((current + arrived[s].astype(jnp.float32)).astype(jnp.bfloat16))
    for s in range(SEQS):
        following_out[0, s] = results[s]
        stored_out[0, ids[s, before]] = results[s]


def lane(z, y, core):
    return (z % ZN) * (YN * CN) + y * CN + core


def permute(x, target):
    pairs = [
        (lane(z, y, c), lane(*target(z, y, c)))
        for z in range(ZN)
        for y in range(YN)
        for c in range(CN)
    ]
    return lax.ppermute(x, LANES, pairs)


def swap(x, flip_y, flip_core):
    return permute(x, lambda z, y, c: (z, y ^ flip_y, c ^ flip_core))


def after(x, earlier):
    return lax.optimization_barrier((x, earlier))[0]


def gather_z(x):
    return lax.all_gather(x, "z", axis=0)


def per_device(
    codes, exponents, sample_ids, buffer_in, buffer_out, norm_gain, w_query, w_keyval, w_output
):
    cos, sin = rope_tables()
    sample_ids = sample_ids.T
    kv_width = w_keyval.shape[2]
    half = ZN * CN * HEAD
    w_keyval = jnp.swapaxes(w_keyval, 1, 2)
    partial_flops = 2 * ROWS * half * 256
    wide = shape((ROWS, HEAD), jnp.float32)

    by_half = (ZN, YN, CN * HEAD, HEAD)
    any_spec = pl.BlockSpec(memory_space=pl.ANY)
    bf16, int32 = jnp.bfloat16, jnp.int32
    packed, pay, inputs = pl.pallas_call(
        prepare,
        out_shape=(
            shape((ZN + ZN * kv_width // HEAD, CN * HEAD, HEAD)),
            shape((PAY, HEAD)),
            shape((SEQS, LEN, HEAD)),
        ),
        in_specs=[SMEM] + [any_spec] * 6,
        out_specs=(any_spec,) * 3,
        scratch_shapes=[
            pltpu.VMEM(codes.shape, int32),
            pltpu.VMEM(exponents.shape, int32),
            pltpu.VMEM((SEQS, LEN, HEAD), bf16),
            pltpu.VMEM(norm_gain.shape, bf16),
            pltpu.VMEM(w_keyval.shape, bf16),
            pltpu.VMEM((PIECES, ZN // PIECES, CN * HEAD, HEAD), bf16),
            pltpu.VMEM((ZN * kv_width // HEAD, CN * HEAD, HEAD), bf16),
            pltpu.VMEM((PAY, HEAD), bf16),
            pltpu.VMEM((SEQS, LEN, HEAD), bf16),
            pltpu.SemaphoreType.DMA((9,)),
            pltpu.SemaphoreType.DMA((2, PIECES)),
        ],
        cost_estimate=pl.CostEstimate(flops=10**7, bytes_accessed=4 * 10**6, transcendentals=0),
    )(
        sample_ids, codes, exponents, buffer_in, norm_gain,
        w_query.reshape(by_half), w_keyval,
    )
    received = swap(packed, 1, 0).reshape(-1, HEAD)
    here = gather_z(pay)
    there = swap(here, 0, 1)
    packed_out = call(pack_kernel, shape((ZN, CN * HEAD, HEAD)), 1, 10**6, 2 * 10**6)(
        w_output.reshape(by_half)
    )

    keyval, sums = call(
        keyval_kernel,
        (shape((2 * kv_width, ROWS)), shape((PAY - ROWS, ROWS))),
        4,
        partial_flops,
        5 * 10**6,
    )(here, there, w_keyval, received)
    keyval = permute(keyval, lambda z, y, c: (2 * z if z < 8 else 2 * (z - 8) + 1, y, c))
    mine, other = call(
        query_kernel, (wide, shape((ROWS, HEAD))), 4, partial_flops, 6 * 10**6
    )(here, there, w_query, after(received, sums))
    other = swap(other, 1, 0)
    near = after(jnp.concatenate([keyval, sums]), other)
    far = swap(near, 1, 0)
    received_out = swap(after(packed_out, near), 1, 0).reshape(half, HEAD)
    own, factors = call(
        sum_kernel, (shape((2, kv_width, ROWS)), wide), 4, 10**6, 10**6
    )(near, far, cos.T.copy(), sin.T.copy())
    own = jnp.stack([own, permute(own, lambda z, y, c: (z ^ 1, y, c))])
    sibling = swap(own, 0, 1)
    queries = call(rope_kernel, shape((ROWS, HEAD)), 5, 10**6, 10**6)(
        mine, other, factors, cos, sin
    )
    context = call(attention_kernel, shape((ROWS, HEAD)), 3, 4 * ROWS * ROWS * HEAD, 10**6)(
        queries, own, sibling
    )

    here = gather_z(context)
    there = swap(here, 0, 1)
    mine, other = call(
        output_kernel, (wide, shape((ROWS, HEAD))), 4, partial_flops, 6 * 10**6
    )(here, there, w_output, received_out)
    other = swap(other, 1, 0)
    message = call(
        message_kernel, shape((SEQS, LEN, HEAD)), 5, 10**6, 10**6, smem=(0,)
    )(sample_ids, mine, other, inputs, buffer_out)

    sections = lax.axis_size("section")
    arrived = lax.ppermute(message, "section", [(i, i + 1) for i in range(sections - 1)])
    following, new_in = call(
        finish_kernel,
        (shape((1, SEQS, LEN, HEAD)), shape(buffer_in.shape)),
        4,
        10**6,
        10**6,
        smem=(0,),
    )(sample_ids, buffer_in, inputs, arrived)
    new_out = call(refresh_kernel, shape(buffer_out.shape), 3, 10**6, 10**6, smem=(0,))(
        sample_ids, message, buffer_out
    )
    return following, new_in, new_out


def solution(mesh):
    sections = mesh.shape["section"]
    fine = Mesh(mesh.devices.reshape(sections, ZN, YN, CN), ("section",) + LANES)
    return jax.shard_map(
        per_device,
        mesh=fine,
        in_specs=(
            P("section", None, None, LANES),
            P("section", None, None),
            P(),
            P("section", None, None, LANES),
            P("section", None, None, LANES),
            P("section", LANES),
            P("section", None, LANES),
            P("section", None, LANES),
            P("section", None, LANES),
        ),
        out_specs=(
            P("section", None, None, LANES),
            P("section", None, None, LANES),
            P("section", None, None, LANES),
        ),
        check_vma=False,
    )
```

```python
import functools
import math

import jax
import jax.numpy as jnp
import numpy as np
from jax import lax
from jax.experimental import pallas as pl
from jax.experimental.pallas import tpu as pltpu
from jax.sharding import Mesh
from jax.sharding import PartitionSpec as P

SEQS, LEN, SLOTS, HEAD, KV_HEADS = 2, 112, 3, 128, 8
ROWS = SEQS * LEN
PAY = ROWS + 16
ZN, YN, CN = 16, 2, 2
PIECES = 4
EARLY = 4
LANES = ("z", "y", "core")
rope_base = 500000.0
norm_eps = 1e-05

VMEM = pl.BlockSpec(memory_space=pltpu.VMEM)
SMEM = pl.BlockSpec(memory_space=pltpu.SMEM)
PARAMS = pltpu.CompilerParams(vmem_limit_bytes=40 * 1024 * 1024)
NT = (((1,), (1,)), ((), ()))


def rope_tables():
    half = HEAD // 2
    frequency = np.exp(np.arange(half) * (-2.0 * math.log(rope_base) / HEAD))
    positions = np.arange(ROWS) % LEN
    angle = positions[:, None] * frequency[None, :]
    return np.cos(angle).astype(np.float32), np.sin(angle).astype(np.float32)


def call(kernel, outs, n_in, flops, bytes_accessed, smem=(), scratch=()):
    return pl.pallas_call(
        kernel,
        out_shape=outs,
        in_specs=[SMEM if i in smem else VMEM for i in range(n_in)],
        out_specs=jax.tree.map(lambda _: VMEM, outs),
        scratch_shapes=list(scratch),
        compiler_params=PARAMS,
        cost_estimate=pl.CostEstimate(
            flops=flops, bytes_accessed=bytes_accessed, transcendentals=0
        ),
    )


def shape(dims, dtype=jnp.bfloat16):
    return jax.ShapeDtypeStruct(dims, dtype)


def prepare(
    ids, codes, exponents, buffer_in, gain, query, keyval, output,
    packed, pay_out, inputs_out,
    codes_v, exponents_v, stored_v, gain_v, keyval_v, half_v, keyval_half_v, early_v, pay, inputs_v,
    sems, half_sems,
):
    section = lax.axis_index("section")
    far = lax.axis_index("y") ^ 1
    copies = [
        pltpu.make_async_copy(exponents, exponents_v, sems.at[0]),
        pltpu.make_async_copy(gain, gain_v, sems.at[1]),
        pltpu.make_async_copy(codes, codes_v, sems.at[2]),
        pltpu.make_async_copy(buffer_in.at[0, ids[0, section]], stored_v.at[0], sems.at[3]),
        pltpu.make_async_copy(buffer_in.at[0, ids[1, section]], stored_v.at[1], sems.at[4]),
        pltpu.make_async_copy(keyval, keyval_v, sems.at[5]),
    ]
    for item in copies:
        item.start()

    step = ZN // PIECES
    moves = [
        (query.at[pl.ds(i * step, step), far], half_v.at[i], packed.at[pl.ds(i * step, step)])
        for i in range(PIECES)
    ]
    tail = ZN + keyval_half_v.shape[0]
    moves.append((output.at[pl.ds(0, EARLY), far], early_v, packed.at[pl.ds(tail, EARLY)]))
    loads, stores = [], []
    for i, (source, between, target) in enumerate(moves):
        loads.append(pltpu.make_async_copy(source, between, half_sems.at[0, i]))
        stores.append(pltpu.make_async_copy(between, target, half_sems.at[1, i]))
        loads[-1].start()
    for item in copies[:5]:
        item.wait()
    eye = lax.broadcasted_iota(jnp.int32, (LEN, LEN), 0) == lax.broadcasted_iota(
        jnp.int32, (LEN, LEN), 1
    )
    gains = gain_v[...].astype(jnp.float32)
    sums = []
    for s in range(SEQS):
        steps = jnp.exp2(exponents_v[0, s : s + 1, :].astype(jnp.float32))
        diagonal = jnp.where(eye, steps, 0.0).astype(jnp.bfloat16)
        scales = jnp.dot(
            diagonal, jnp.ones((LEN, HEAD), jnp.bfloat16), preferred_element_type=jnp.float32
        )
        stored = stored_v[s].astype(jnp.float32)
        inputs = (stored + codes_v[0, s].astype(jnp.float32) * scales).astype(jnp.bfloat16)
        inputs_v[s] = inputs
        widened = inputs.astype(jnp.float32)
        pay[s * LEN : (s + 1) * LEN, :] = (widened * gains).astype(jnp.bfloat16)
        squares = widened * widened
        high = squares.astype(jnp.bfloat16)
        low = (squares - high.astype(jnp.float32)).astype(jnp.bfloat16)
        ones = jnp.ones((16, HEAD), jnp.bfloat16)
        total = lax.dot_general(ones, high, NT, preferred_element_type=jnp.float32)
        total += lax.dot_general(ones, low, NT, preferred_element_type=jnp.float32)
        sums.append(jnp.concatenate([total, jnp.zeros((16, HEAD - LEN), jnp.float32)], axis=1))
    row = lax.broadcasted_iota(jnp.int32, (16, HEAD), 0)
    value = jnp.where(row % 2 == 0, sums[0], sums[1])
    first = value.astype(jnp.bfloat16).astype(jnp.float32)
    second = value - first
    tail = jnp.where(row < 2, first, jnp.where(row < 4, second, 0.0))
    pay[ROWS:PAY, :] = tail.astype(jnp.bfloat16)
    stores.append(pltpu.make_async_copy(pay, pay_out, sems.at[7]))
    stores[-1].start()
    stores.append(pltpu.make_async_copy(inputs_v, inputs_out, sems.at[8]))
    stores[-1].start()

    for load, store in zip(loads, stores):
        load.wait()
        store.start()
    copies[5].wait()
    kv_width = keyval.shape[1]
    per_row = CN * HEAD // kv_width
    for z in range(ZN):
        for core in range(CN):
            i = z * CN + core
            start = (i % per_row) * kv_width
            keyval_half_v[i // per_row, start : start + kv_width, :] = keyval_v[
                0, :, head_rows(z, far, core)
            ]
    last = pltpu.make_async_copy(
        keyval_half_v, packed.at[pl.ds(ZN, keyval_half_v.shape[0])], sems.at[6]
    )
    last.start()
    last.wait()
    for store in stores:
        store.wait()


def head_rows(z, y, core):
    head = z * (YN * CN) + y * CN + core
    return pl.ds(pl.multiple_of(head * HEAD, HEAD), HEAD)


def half_rows(z, core):
    return pl.ds(pl.multiple_of((z * CN + core) * HEAD, HEAD), HEAD)


def keyval_kernel(here, there, weight, received, out, sums_out):
    y, core = lax.axis_index("y"), lax.axis_index("core")
    kv_width = weight.shape[1]
    sums = jnp.sum(here[:, ROWS:PAY, :].astype(jnp.float32), axis=0)
    sums += jnp.sum(there[:, ROWS:PAY, :].astype(jnp.float32), axis=0)
    sums = jnp.concatenate(
        [sums[s : s + 1, :LEN] + sums[SEQS + s : SEQS + s + 1, :LEN] for s in range(SEQS)], axis=1
    )
    high = sums.astype(jnp.bfloat16).astype(jnp.float32)
    row = lax.broadcasted_iota(jnp.int32, (PAY - ROWS, ROWS), 0)
    tail = jnp.where(row == 0, high, jnp.where(row == 1, sums - high, 0.0))
    sums_out[...] = tail.astype(jnp.bfloat16)
    acc = jnp.zeros((2 * kv_width, ROWS), jnp.float32)
    for z in range(ZN):
        block = jnp.concatenate([here[z, :ROWS, :], there[z, :ROWS, :]], axis=1)
        parts = []
        for side in (core, core ^ 1):
            start = ZN * CN * HEAD + (z * CN + side) * kv_width
            mine = weight[0, :, head_rows(z, y, side)]
            other = received[pl.ds(pl.multiple_of(start, kv_width), kv_width), :]
            parts.append(jnp.concatenate([mine, other], axis=0))
        part = jnp.concatenate(parts, axis=1)
        acc += lax.dot_general(part, block, NT, preferred_element_type=jnp.float32)
    out[...] = acc.astype(jnp.bfloat16)


def both_partials(here, there, weight, received_rows):
    y, core = lax.axis_index("y"), lax.axis_index("core")
    acc = jnp.zeros((ROWS, 2 * HEAD), jnp.float32)
    for z in range(ZN):
        block = jnp.concatenate([here[z, :ROWS, :], there[z, :ROWS, :]], axis=1)
        parts = []
        for side in (core, core ^ 1):
            mine = weight[0, head_rows(z, y, side), :]
            other = received_rows(z, side)
            parts.append(jnp.concatenate([mine, other], axis=1))
        part = jnp.concatenate(parts, axis=0)
        acc += jnp.dot(block, part, preferred_element_type=jnp.float32)
    return acc


def query_kernel(here, there, weight, received, mine_out, other_out):
    acc = both_partials(here, there, weight, lambda z, side: received[half_rows(z, side), :])
    mine_out[...] = acc[:, :HEAD]
    other_out[...] = acc[:, HEAD:].astype(jnp.bfloat16)


def sum_kernel(near, far, cos_t, sin_t, out, factors_out):
    z_odd, y, core = lax.axis_index("z") % 2, lax.axis_index("y"), lax.axis_index("core")
    width = (near.shape[0] - (PAY - ROWS)) // 4
    tail = near[4 * width :, :].astype(jnp.float32) + far[4 * width :, :].astype(jnp.float32)
    square_sum = tail[0:1, :] + tail[1:2, :]
    inverse = lax.rsqrt(square_sum / (ZN * YN * CN * HEAD) + norm_eps)
    factors = jnp.broadcast_to(inverse, (width, ROWS))
    factors_out[...] = jnp.broadcast_to(inverse, (HEAD, ROWS)).T

    def piece(kind, which):
        plane = z_odd ^ kind
        a = near[pl.ds(pl.multiple_of((plane * 2 + (which ^ y)) * width, width), width), :]
        b = far[pl.ds(pl.multiple_of((plane * 2 + 1 - (which ^ y)) * width, width), width), :]
        return ((a.astype(jnp.float32) + b.astype(jnp.float32)) * factors).astype(jnp.bfloat16)

    first, second = piece(0, 0).astype(jnp.float32), piece(0, 1).astype(jnp.float32)
    rows = pl.ds(pl.multiple_of(core * width, width), width)
    c, s = cos_t[rows, :], sin_t[rows, :]
    out[0] = (first * c - second * s).astype(jnp.bfloat16)
    out[1] = (second * c + first * s).astype(jnp.bfloat16)
    out[2] = piece(1, 0)
    out[3] = piece(1, 1)


def rope_kernel(mine, other, factors, cos, sin, out):
    acc = (mine[...] + other[...].astype(jnp.float32)) * factors[...]
    first, second = acc[:, : HEAD // 2], acc[:, HEAD // 2 :]
    c, s = cos[...], sin[...]
    out[...] = jnp.concatenate(
        [first * c - second * s, second * c + first * s], axis=1
    ).astype(jnp.bfloat16)


def attention_kernel(query, own, sibling, out):
    core = lax.axis_index("core")
    keys_values = []
    for kind in range(2):
        parts = []
        for which in range(2):
            a, b = own[2 * kind + which], sibling[2 * kind + which]
            parts += [jnp.where(core == 0, a, b), jnp.where(core == 0, b, a)]
        keys_values.append(jnp.concatenate(parts, axis=0))
    keys, values = keys_values
    scores = jnp.dot(query[...], keys, preferred_element_type=jnp.float32) / math.sqrt(HEAD)
    row = lax.broadcasted_iota(jnp.int32, (ROWS, ROWS), 0)
    column = lax.broadcasted_iota(jnp.int32, (ROWS, ROWS), 1)
    allowed = (column <= row) & ((row < LEN) | (column >= LEN))
    scores = jnp.where(allowed, scores, -1e30)
    peak = jnp.max(scores, axis=-1, keepdims=True)
    raised = jnp.exp(scores - peak)
    weights = (raised / jnp.sum(raised, axis=-1, keepdims=True)).astype(jnp.bfloat16)
    context = lax.dot_general(weights, values, NT, preferred_element_type=jnp.float32)
    out[...] = context.astype(jnp.bfloat16)


def pack_kernel(weight, out):
    far = lax.axis_index("y") ^ 1
    for z in range(EARLY, ZN):
        out[z - EARLY] = weight[z, far]


def output_kernel(here, there, weight, early, received, mine_out, other_out):
    def received_rows(z, side):
        if z < EARLY:
            return early[half_rows(z, side), :]
        return received[half_rows(z - EARLY, side), :]

    acc = both_partials(here, there, weight, received_rows)
    mine_out[...] = acc[:, :HEAD]
    other_out[...] = acc[:, HEAD:].astype(jnp.bfloat16)


def message_kernel(ids, mine, other, inputs, buffer_out, message_out):
    section = lax.axis_index("section")
    for s in range(SEQS):
        rows = slice(s * LEN, (s + 1) * LEN)
        stored = buffer_out[0, ids[s, section]].astype(jnp.float32)
        mixed = mine[rows, :] + other[rows, :].astype(jnp.float32)
        message_out[s] = (inputs[s].astype(jnp.float32) + mixed - stored).astype(jnp.bfloat16)


def refresh_kernel(ids, message, buffer_out, new_out):
    section = lax.axis_index("section")
    new_out[...] = buffer_out[...]
    for s in range(SEQS):
        slot = ids[s, section]
        stored = buffer_out[0, slot].astype(jnp.float32)
        new_out[0, slot] = (stored + message[s].astype(jnp.float32)).astype(jnp.bfloat16)


def finish_kernel(ids, buffer_in, inputs, arrived, following_out, stored_out):
    section = lax.axis_index("section")
    before = jnp.maximum(section - 1, 0)
    stored_out[...] = buffer_in[...]
    for s in range(SEQS):
        stored_out[0, ids[s, section]] = inputs[s]
    results = []
    for s in range(SEQS):
        current = stored_out[0, ids[s, before]].astype(jnp.float32)
        results.append((current + arrived[s].astype(jnp.float32)).astype(jnp.bfloat16))
    for s in range(SEQS):
        following_out[0, s] = results[s]
        stored_out[0, ids[s, before]] = results[s]


def lane(z, y, core):
    return (z % ZN) * (YN * CN) + y * CN + core


def permute(x, target):
    pairs = [
        (lane(z, y, c), lane(*target(z, y, c)))
        for z in range(ZN)
        for y in range(YN)
        for c in range(CN)
    ]
    return lax.ppermute(x, LANES, pairs)


def swap(x, flip_y, flip_core):
    return permute(x, lambda z, y, c: (z, y ^ flip_y, c ^ flip_core))


def after(x, earlier):
    return lax.optimization_barrier((x, earlier))[0]


def gather_z(x):
    return lax.all_gather(x, "z", axis=0)


def per_device(
    codes, exponents, sample_ids, buffer_in, buffer_out, norm_gain, w_query, w_keyval, w_output
):
    cos, sin = rope_tables()
    sample_ids = sample_ids.T
    kv_width = w_keyval.shape[2]
    half = ZN * CN * HEAD
    w_keyval = jnp.swapaxes(w_keyval, 1, 2)
    partial_flops = 2 * ROWS * half * 256
    wide = shape((ROWS, HEAD), jnp.float32)

    by_half = (ZN, YN, CN * HEAD, HEAD)
    any_spec = pl.BlockSpec(memory_space=pl.ANY)
    bf16, int32 = jnp.bfloat16, jnp.int32
    packed, pay, inputs = pl.pallas_call(
        prepare,
        out_shape=(
            shape((ZN + ZN * kv_width // HEAD + EARLY, CN * HEAD, HEAD)),
            shape((PAY, HEAD)),
            shape((SEQS, LEN, HEAD)),
        ),
        in_specs=[SMEM] + [any_spec] * 7,
        out_specs=(any_spec,) * 3,
        scratch_shapes=[
            pltpu.VMEM(codes.shape, int32),
            pltpu.VMEM(exponents.shape, int32),
            pltpu.VMEM((SEQS, LEN, HEAD), bf16),
            pltpu.VMEM(norm_gain.shape, bf16),
            pltpu.VMEM(w_keyval.shape, bf16),
            pltpu.VMEM((PIECES, ZN // PIECES, CN * HEAD, HEAD), bf16),
            pltpu.VMEM((ZN * kv_width // HEAD, CN * HEAD, HEAD), bf16),
            pltpu.VMEM((EARLY, CN * HEAD, HEAD), bf16),
            pltpu.VMEM((PAY, HEAD), bf16),
            pltpu.VMEM((SEQS, LEN, HEAD), bf16),
            pltpu.SemaphoreType.DMA((9,)),
            pltpu.SemaphoreType.DMA((2, PIECES + 1)),
        ],
        cost_estimate=pl.CostEstimate(flops=10**7, bytes_accessed=4 * 10**6, transcendentals=0),
    )(
        sample_ids, codes, exponents, buffer_in, norm_gain,
        w_query.reshape(by_half), w_keyval, w_output.reshape(by_half),
    )
    received = swap(packed, 1, 0).reshape(-1, HEAD)
    here = gather_z(pay)
    there = swap(here, 0, 1)
    packed_out = call(pack_kernel, shape((ZN - EARLY, CN * HEAD, HEAD)), 1, 10**6, 2 * 10**6)(
        w_output.reshape(by_half)
    )
    received_out = swap(packed_out, 1, 0).reshape(-1, HEAD)

    keyval, sums = call(
        keyval_kernel,
        (shape((2 * kv_width, ROWS)), shape((PAY - ROWS, ROWS))),
        4,
        partial_flops,
        5 * 10**6,
    )(here, there, w_keyval, received)
    even = permute(keyval, lambda z, y, c: (2 * z if z < 8 else 2 * (z - 8) + 1, y, c))
    odd = permute(after(keyval, even), lambda z, y, c: (2 * z + 1 if z < 8 else 2 * (z - 8), y, c))
    mine, other = call(
        query_kernel, (wide, shape((ROWS, HEAD))), 4, partial_flops, 6 * 10**6
    )(here, there, w_query, after(received, keyval))
    other = swap(other, 1, 0)
    near = after(jnp.concatenate([even, odd, sums]), mine)
    far = swap(near, 1, 0)
    own, factors = call(
        sum_kernel, (shape((4, kv_width, ROWS)), wide), 4, 10**6, 10**6
    )(after(near, received_out), far, cos.T.copy(), sin.T.copy())
    sibling = swap(own, 0, 1)
    queries = call(rope_kernel, shape((ROWS, HEAD)), 5, 10**6, 10**6)(
        mine, other, factors, cos, sin
    )
    context = call(attention_kernel, shape((ROWS, HEAD)), 3, 4 * ROWS * ROWS * HEAD, 10**6)(
        queries, own, sibling
    )

    here = gather_z(context)
    there = swap(here, 0, 1)
    mine, other = call(
        output_kernel, (wide, shape((ROWS, HEAD))), 5, partial_flops, 6 * 10**6
    )(here, there, w_output, received[-EARLY * CN * HEAD :], received_out)
    other = swap(other, 1, 0)
    message = call(
        message_kernel, shape((SEQS, LEN, HEAD)), 5, 10**6, 10**6, smem=(0,)
    )(sample_ids, mine, other, inputs, buffer_out)

    sections = lax.axis_size("section")
    arrived = lax.ppermute(message, "section", [(i, i + 1) for i in range(sections - 1)])
    following, new_in = call(
        finish_kernel,
        (shape((1, SEQS, LEN, HEAD)), shape(buffer_in.shape)),
        4,
        10**6,
        10**6,
        smem=(0,),
    )(sample_ids, buffer_in, inputs, arrived)
    new_out = call(refresh_kernel, shape(buffer_out.shape), 3, 10**6, 10**6, smem=(0,))(
        sample_ids, message, buffer_out
    )
    return following, new_in, new_out


def solution(mesh):
    sections = mesh.shape["section"]
    fine = Mesh(mesh.devices.reshape(sections, ZN, YN, CN), ("section",) + LANES)
    return jax.shard_map(
        per_device,
        mesh=fine,
        in_specs=(
            P("section", None, None, LANES),
            P("section", None, None),
            P(),
            P("section", None, None, LANES),
            P("section", None, None, LANES),
            P("section", LANES),
            P("section", None, LANES),
            P("section", None, LANES),
            P("section", None, LANES),
        ),
        out_specs=(
            P("section", None, None, LANES),
            P("section", None, None, LANES),
            P("section", None, None, LANES),
        ),
        check_vma=False,
    )
```

```python
import functools
import math

import jax
import jax.numpy as jnp
import numpy as np
from jax import lax
from jax.experimental import pallas as pl
from jax.experimental.pallas import tpu as pltpu
from jax.sharding import Mesh
from jax.sharding import PartitionSpec as P

SEQS, LEN, SLOTS, HEAD, KV_HEADS = 2, 112, 3, 128, 8
ROWS = SEQS * LEN
PAY = ROWS + 16
ZN, YN, CN = 16, 2, 2
PIECES = 4
EARLY = 4
LANES = ("z", "y", "core")
rope_base = 500000.0
norm_eps = 1e-05

VMEM = pl.BlockSpec(memory_space=pltpu.VMEM)
SMEM = pl.BlockSpec(memory_space=pltpu.SMEM)
PARAMS = pltpu.CompilerParams(vmem_limit_bytes=40 * 1024 * 1024)
NT = (((1,), (1,)), ((), ()))


def rope_tables():
    half = HEAD // 2
    frequency = np.exp(np.arange(half) * (-2.0 * math.log(rope_base) / HEAD))
    positions = np.arange(ROWS) % LEN
    angle = positions[:, None] * frequency[None, :]
    return np.cos(angle).astype(np.float32), np.sin(angle).astype(np.float32)


def call(kernel, outs, n_in, flops, bytes_accessed, smem=(), scratch=()):
    return pl.pallas_call(
        kernel,
        out_shape=outs,
        in_specs=[SMEM if i in smem else VMEM for i in range(n_in)],
        out_specs=jax.tree.map(lambda _: VMEM, outs),
        scratch_shapes=list(scratch),
        compiler_params=PARAMS,
        cost_estimate=pl.CostEstimate(
            flops=flops, bytes_accessed=bytes_accessed, transcendentals=0
        ),
    )


def shape(dims, dtype=jnp.bfloat16):
    return jax.ShapeDtypeStruct(dims, dtype)


def prepare(
    ids, codes, exponents, buffer_in, gain, query, keyval, output,
    packed, pay_out, inputs_out,
    codes_v, exponents_v, stored_v, gain_v, keyval_v, half_v, keyval_half_v, early_v, pay, inputs_v,
    sems, half_sems,
):
    section = lax.axis_index("section")
    far = lax.axis_index("y") ^ 1
    copies = [
        pltpu.make_async_copy(exponents, exponents_v, sems.at[0]),
        pltpu.make_async_copy(gain, gain_v, sems.at[1]),
        pltpu.make_async_copy(codes, codes_v, sems.at[2]),
        pltpu.make_async_copy(buffer_in.at[0, ids[0, section]], stored_v.at[0], sems.at[3]),
        pltpu.make_async_copy(buffer_in.at[0, ids[1, section]], stored_v.at[1], sems.at[4]),
        pltpu.make_async_copy(keyval, keyval_v, sems.at[5]),
    ]
    for item in copies:
        item.start()

    step = ZN // PIECES
    moves = [
        (query.at[pl.ds(i * step, step), far], half_v.at[i], packed.at[pl.ds(i * step, step)])
        for i in range(PIECES)
    ]
    tail = ZN + keyval_half_v.shape[0]
    moves.append((output.at[pl.ds(0, EARLY), far], early_v, packed.at[pl.ds(tail, EARLY)]))
    loads, stores = [], []
    for i, (source, between, target) in enumerate(moves):
        loads.append(pltpu.make_async_copy(source, between, half_sems.at[0, i]))
        stores.append(pltpu.make_async_copy(between, target, half_sems.at[1, i]))
        loads[-1].start()
    for item in copies[:5]:
        item.wait()
    eye = lax.broadcasted_iota(jnp.int32, (LEN, LEN), 0) == lax.broadcasted_iota(
        jnp.int32, (LEN, LEN), 1
    )
    gains = gain_v[...].astype(jnp.float32)
    sums = []
    for s in range(SEQS):
        steps = jnp.exp2(exponents_v[0, s : s + 1, :].astype(jnp.float32))
        diagonal = jnp.where(eye, steps, 0.0).astype(jnp.bfloat16)
        scales = jnp.dot(
            diagonal, jnp.ones((LEN, HEAD), jnp.bfloat16), preferred_element_type=jnp.float32
        )
        stored = stored_v[s].astype(jnp.float32)
        inputs = (stored + codes_v[0, s].astype(jnp.float32) * scales).astype(jnp.bfloat16)
        inputs_v[s] = inputs
        widened = inputs.astype(jnp.float32)
        pay[s * LEN : (s + 1) * LEN, :] = (widened * gains).astype(jnp.bfloat16)
        squares = widened * widened
        high = squares.astype(jnp.bfloat16)
        low = (squares - high.astype(jnp.float32)).astype(jnp.bfloat16)
        ones = jnp.ones((16, HEAD), jnp.bfloat16)
        total = lax.dot_general(ones, high, NT, preferred_element_type=jnp.float32)
        total += lax.dot_general(ones, low, NT, preferred_element_type=jnp.float32)
        sums.append(jnp.concatenate([total, jnp.zeros((16, HEAD - LEN), jnp.float32)], axis=1))
    row = lax.broadcasted_iota(jnp.int32, (16, HEAD), 0)
    value = jnp.where(row % 2 == 0, sums[0], sums[1])
    first = value.astype(jnp.bfloat16).astype(jnp.float32)
    second = value - first
    tail = jnp.where(row < 2, first, jnp.where(row < 4, second, 0.0))
    pay[ROWS:PAY, :] = tail.astype(jnp.bfloat16)
    stores.append(pltpu.make_async_copy(pay, pay_out, sems.at[7]))
    stores[-1].start()
    stores.append(pltpu.make_async_copy(inputs_v, inputs_out, sems.at[8]))
    stores[-1].start()

    for load, store in zip(loads, stores):
        load.wait()
        store.start()
    copies[5].wait()
    kv_width = keyval.shape[1]
    per_row = CN * HEAD // kv_width
    for z in range(ZN):
        for core in range(CN):
            i = z * CN + core
            start = (i % per_row) * kv_width
            keyval_half_v[i // per_row, start : start + kv_width, :] = keyval_v[
                0, :, head_rows(z, far, core)
            ]
    last = pltpu.make_async_copy(
        keyval_half_v, packed.at[pl.ds(ZN, keyval_half_v.shape[0])], sems.at[6]
    )
    last.start()
    last.wait()
    for store in stores:
        store.wait()


def head_rows(z, y, core):
    head = z * (YN * CN) + y * CN + core
    return pl.ds(pl.multiple_of(head * HEAD, HEAD), HEAD)


def half_rows(z, core):
    return pl.ds(pl.multiple_of((z * CN + core) * HEAD, HEAD), HEAD)


def keyval_kernel(here, there, weight, received, out, sums_out):
    y, core = lax.axis_index("y"), lax.axis_index("core")
    kv_width = weight.shape[1]
    sums = jnp.sum(here[:, ROWS:PAY, :].astype(jnp.float32), axis=0)
    sums += jnp.sum(there[:, ROWS:PAY, :].astype(jnp.float32), axis=0)
    sums = jnp.concatenate(
        [sums[s : s + 1, :LEN] + sums[SEQS + s : SEQS + s + 1, :LEN] for s in range(SEQS)], axis=1
    )
    high = sums.astype(jnp.bfloat16).astype(jnp.float32)
    row = lax.broadcasted_iota(jnp.int32, (PAY - ROWS, ROWS), 0)
    tail = jnp.where(row == 0, high, jnp.where(row == 1, sums - high, 0.0))
    sums_out[...] = tail.astype(jnp.bfloat16)
    acc = jnp.zeros((2 * kv_width, ROWS), jnp.float32)
    for z in range(ZN):
        block = jnp.concatenate([here[z, :ROWS, :], there[z, :ROWS, :]], axis=1)
        parts = []
        for side in (core, core ^ 1):
            start = ZN * CN * HEAD + (z * CN + side) * kv_width
            mine = weight[0, :, head_rows(z, y, side)]
            other = received[pl.ds(pl.multiple_of(start, kv_width), kv_width), :]
            parts.append(jnp.concatenate([mine, other], axis=0))
        part = jnp.concatenate(parts, axis=1)
        acc += lax.dot_general(part, block, NT, preferred_element_type=jnp.float32)
    out[...] = acc.astype(jnp.bfloat16)


def both_partials(here, there, weight, received):
    y, core = lax.axis_index("y"), lax.axis_index("core")
    acc = jnp.zeros((ROWS, 2 * HEAD), jnp.float32)
    for z in range(ZN):
        block = jnp.concatenate([here[z, :ROWS, :], there[z, :ROWS, :]], axis=1)
        parts = []
        for side in (core, core ^ 1):
            mine = weight[0, head_rows(z, y, side), :]
            other = received[half_rows(z, side), :]
            parts.append(jnp.concatenate([mine, other], axis=1))
        part = jnp.concatenate(parts, axis=0)
        acc += jnp.dot(block, part, preferred_element_type=jnp.float32)
    return acc


def query_kernel(here, there, weight, received, mine_out, other_out):
    acc = both_partials(here, there, weight, received)
    mine_out[...] = acc[:, :HEAD]
    other_out[...] = acc[:, HEAD:].astype(jnp.bfloat16)


def sum_kernel(near, far, cos_t, sin_t, out, factors_out):
    z_odd, y, core = lax.axis_index("z") % 2, lax.axis_index("y"), lax.axis_index("core")
    width = (near.shape[0] - (PAY - ROWS)) // 4
    tail = near[4 * width :, :].astype(jnp.float32) + far[4 * width :, :].astype(jnp.float32)
    square_sum = tail[0:1, :] + tail[1:2, :]
    inverse = lax.rsqrt(square_sum / (ZN * YN * CN * HEAD) + norm_eps)
    factors = jnp.broadcast_to(inverse, (width, ROWS))
    factors_out[...] = jnp.broadcast_to(inverse, (HEAD, ROWS)).T

    def piece(kind, which):
        plane = z_odd ^ kind
        a = near[pl.ds(pl.multiple_of((plane * 2 + (which ^ y)) * width, width), width), :]
        b = far[pl.ds(pl.multiple_of((plane * 2 + 1 - (which ^ y)) * width, width), width), :]
        return ((a.astype(jnp.float32) + b.astype(jnp.float32)) * factors).astype(jnp.bfloat16)

    first, second = piece(0, 0).astype(jnp.float32), piece(0, 1).astype(jnp.float32)
    rows = pl.ds(pl.multiple_of(core * width, width), width)
    c, s = cos_t[rows, :], sin_t[rows, :]
    out[0] = (first * c - second * s).astype(jnp.bfloat16)
    out[1] = (second * c + first * s).astype(jnp.bfloat16)
    out[2] = piece(1, 0)
    out[3] = piece(1, 1)


def rope_kernel(mine, other, factors, cos, sin, out):
    acc = (mine[...] + other[...].astype(jnp.float32)) * factors[...]
    first, second = acc[:, : HEAD // 2], acc[:, HEAD // 2 :]
    c, s = cos[...], sin[...]
    out[...] = jnp.concatenate(
        [first * c - second * s, second * c + first * s], axis=1
    ).astype(jnp.bfloat16)


def attention_kernel(query, own, sibling, out):
    core = lax.axis_index("core")
    keys_values = []
    for kind in range(2):
        parts = []
        for which in range(2):
            a, b = own[2 * kind + which], sibling[2 * kind + which]
            parts += [jnp.where(core == 0, a, b), jnp.where(core == 0, b, a)]
        keys_values.append(jnp.concatenate(parts, axis=0))
    keys, values = keys_values
    scores = jnp.dot(query[...], keys, preferred_element_type=jnp.float32) / math.sqrt(HEAD)
    row = lax.broadcasted_iota(jnp.int32, (ROWS, ROWS), 0)
    column = lax.broadcasted_iota(jnp.int32, (ROWS, ROWS), 1)
    allowed = (column <= row) & ((row < LEN) | (column >= LEN))
    scores = jnp.where(allowed, scores, -1e30)
    peak = jnp.max(scores, axis=-1, keepdims=True)
    raised = jnp.exp(scores - peak)
    weights = (raised / jnp.sum(raised, axis=-1, keepdims=True)).astype(jnp.bfloat16)
    context = lax.dot_general(weights, values, NT, preferred_element_type=jnp.float32)
    out[...] = context.astype(jnp.bfloat16)


def pack_kernel(weight, out):
    far = lax.axis_index("y") ^ 1
    for z in range(EARLY, ZN):
        out[z - EARLY] = weight[z, far]


def line_product(line, rows):
    acc = None
    for z in range(0, ZN, 2):
        block = jnp.concatenate([line[z], line[z + 1]], axis=1)
        part = jnp.concatenate([rows(z), rows(z + 1)], axis=0)
        term = jnp.dot(block, part, preferred_element_type=jnp.float32)
        acc = term if acc is None else acc + term
    return acc


def far_rows(z, core, early, received):
    if z < EARLY:
        return early[half_rows(z, core), :]
    return received[half_rows(z - EARLY, core), :]


def own_line_kernel(line, weight, early, received, out):
    y, core = lax.axis_index("y"), lax.axis_index("core")

    def rows(z):
        mine = weight[0, head_rows(z, y, core), :]
        return jnp.concatenate([mine, far_rows(z, core, early, received)], axis=1)

    out[...] = line_product(line, rows)


def far_columns_kernel(line, acc, early, received, out):
    side = lax.axis_index("core") ^ 1
    total = line_product(line, lambda z: far_rows(z, side, early, received))
    out[...] = (acc[:, HEAD:] + total).astype(jnp.bfloat16)


def own_columns_kernel(line, acc, weight, out):
    y, side = lax.axis_index("y"), lax.axis_index("core") ^ 1
    out[...] = acc[:, :HEAD] + line_product(line, lambda z: weight[0, head_rows(z, y, side), :])


def message_kernel(ids, mine, other, inputs, buffer_out, message_out):
    section = lax.axis_index("section")
    for s in range(SEQS):
        rows = slice(s * LEN, (s + 1) * LEN)
        stored = buffer_out[0, ids[s, section]].astype(jnp.float32)
        mixed = mine[rows, :] + other[rows, :].astype(jnp.float32)
        message_out[s] = (inputs[s].astype(jnp.float32) + mixed - stored).astype(jnp.bfloat16)


def refresh_kernel(ids, message, buffer_out, new_out):
    section = lax.axis_index("section")
    new_out[...] = buffer_out[...]
    for s in range(SEQS):
        slot = ids[s, section]
        stored = buffer_out[0, slot].astype(jnp.float32)
        new_out[0, slot] = (stored + message[s].astype(jnp.float32)).astype(jnp.bfloat16)


def finish_kernel(ids, buffer_in, inputs, arrived, following_out, stored_out, following, stored, sems):
    section = lax.axis_index("section")
    before = jnp.maximum(section - 1, 0)
    stored[...] = buffer_in[0]
    for s in range(SEQS):
        stored[ids[s, section]] = inputs[s]
    copies = []
    for s in range(SEQS):
        current = stored[ids[s, before]].astype(jnp.float32)
        following[s] = (current + arrived[s].astype(jnp.float32)).astype(jnp.bfloat16)
        copies.append(
            pltpu.make_async_copy(following.at[s], following_out.at[0, s], sems.at[s])
        )
        copies[-1].start()
    for s in range(SEQS):
        stored[ids[s, before]] = following[s]
    copies.append(pltpu.make_async_copy(stored, stored_out.at[0], sems.at[SEQS]))
    copies[-1].start()
    for item in copies:
        item.wait()


def lane(z, y, core):
    return (z % ZN) * (YN * CN) + y * CN + core


def permute(x, target):
    pairs = [
        (lane(z, y, c), lane(*target(z, y, c)))
        for z in range(ZN)
        for y in range(YN)
        for c in range(CN)
    ]
    return lax.ppermute(x, LANES, pairs)


def swap(x, flip_y, flip_core):
    return permute(x, lambda z, y, c: (z, y ^ flip_y, c ^ flip_core))


def after(x, earlier):
    return lax.optimization_barrier((x, earlier))[0]


def gather_z(x):
    return lax.all_gather(x, "z", axis=0)


def per_device(
    codes, exponents, sample_ids, buffer_in, buffer_out, norm_gain, w_query, w_keyval, w_output
):
    cos, sin = rope_tables()
    sample_ids = sample_ids.T
    kv_width = w_keyval.shape[2]
    half = ZN * CN * HEAD
    w_keyval = jnp.swapaxes(w_keyval, 1, 2)
    partial_flops = 2 * ROWS * half * 256
    wide = shape((ROWS, HEAD), jnp.float32)

    by_half = (ZN, YN, CN * HEAD, HEAD)
    any_spec = pl.BlockSpec(memory_space=pl.ANY)
    bf16, int32 = jnp.bfloat16, jnp.int32
    packed, pay, inputs = pl.pallas_call(
        prepare,
        out_shape=(
            shape((ZN + ZN * kv_width // HEAD + EARLY, CN * HEAD, HEAD)),
            shape((PAY, HEAD)),
            shape((SEQS, LEN, HEAD)),
        ),
        in_specs=[SMEM] + [any_spec] * 7,
        out_specs=(any_spec,) * 3,
        scratch_shapes=[
            pltpu.VMEM(codes.shape, int32),
            pltpu.VMEM(exponents.shape, int32),
            pltpu.VMEM((SEQS, LEN, HEAD), bf16),
            pltpu.VMEM(norm_gain.shape, bf16),
            pltpu.VMEM(w_keyval.shape, bf16),
            pltpu.VMEM((PIECES, ZN // PIECES, CN * HEAD, HEAD), bf16),
            pltpu.VMEM((ZN * kv_width // HEAD, CN * HEAD, HEAD), bf16),
            pltpu.VMEM((EARLY, CN * HEAD, HEAD), bf16),
            pltpu.VMEM((PAY, HEAD), bf16),
            pltpu.VMEM((SEQS, LEN, HEAD), bf16),
            pltpu.SemaphoreType.DMA((9,)),
            pltpu.SemaphoreType.DMA((2, PIECES + 1)),
        ],
        cost_estimate=pl.CostEstimate(flops=10**7, bytes_accessed=4 * 10**6, transcendentals=0),
    )(
        sample_ids, codes, exponents, buffer_in, norm_gain,
        w_query.reshape(by_half), w_keyval, w_output.reshape(by_half),
    )
    received = swap(packed, 1, 0).reshape(-1, HEAD)
    here = gather_z(pay)
    there = swap(here, 0, 1)
    packed_out = call(pack_kernel, shape((ZN - EARLY, CN * HEAD, HEAD)), 1, 10**6, 2 * 10**6)(
        w_output.reshape(by_half)
    )
    received_out = swap(packed_out, 1, 0).reshape(-1, HEAD)

    keyval, sums = call(
        keyval_kernel,
        (shape((2 * kv_width, ROWS)), shape((PAY - ROWS, ROWS))),
        4,
        partial_flops,
        5 * 10**6,
    )(here, there, w_keyval, received)
    even = permute(keyval, lambda z, y, c: (2 * z if z < 8 else 2 * (z - 8) + 1, y, c))
    odd = permute(keyval, lambda z, y, c: (2 * z + 1 if z < 8 else 2 * (z - 8), y, c))
    mine, other = call(
        query_kernel, (wide, shape((ROWS, HEAD))), 4, partial_flops, 6 * 10**6
    )(here, there, w_query, after(received, keyval))
    other = swap(other, 1, 0)
    near = after(jnp.concatenate([even, odd, sums]), mine)
    far = swap(near, 1, 0)
    own, factors = call(
        sum_kernel, (shape((4, kv_width, ROWS)), wide), 4, 10**6, 10**6
    )(after(near, received_out), far, cos.T.copy(), sin.T.copy())
    sibling = swap(own, 0, 1)
    queries = call(rope_kernel, shape((ROWS, HEAD)), 5, 10**6, 10**6)(
        mine, other, factors, cos, sin
    )
    context = call(attention_kernel, shape((ROWS, HEAD)), 3, 4 * ROWS * ROWS * HEAD, 10**6)(
        queries, own, sibling
    )

    here = gather_z(context)
    there = swap(here, 0, 1)
    early = received[-EARLY * CN * HEAD :]
    line_flops = partial_flops // 2
    both = call(
        own_line_kernel, shape((ROWS, 2 * HEAD), jnp.float32), 4, line_flops, 4 * 10**6
    )(here, w_output, early, received_out)
    other = call(far_columns_kernel, shape((ROWS, HEAD)), 4, line_flops, 2 * 10**6)(
        there, both, early, received_out
    )
    other = swap(other, 1, 0)
    mine = call(own_columns_kernel, wide, 3, line_flops, 3 * 10**6)(there, both, w_output)
    message = call(
        message_kernel, shape((SEQS, LEN, HEAD)), 5, 10**6, 10**6, smem=(0,)
    )(sample_ids, mine, other, inputs, buffer_out)

    sections = lax.axis_size("section")
    arrived = lax.ppermute(message, "section", [(i, i + 1) for i in range(sections - 1)])
    following, new_in = pl.pallas_call(
        finish_kernel,
        out_shape=(shape((1, SEQS, LEN, HEAD)), shape(buffer_in.shape)),
        in_specs=[SMEM] + [VMEM] * 3,
        out_specs=(any_spec,) * 2,
        scratch_shapes=[
            pltpu.VMEM((SEQS, LEN, HEAD), bf16),
            pltpu.VMEM((SLOTS, LEN, HEAD), bf16),
            pltpu.SemaphoreType.DMA((SEQS + 1,)),
        ],
        compiler_params=PARAMS,
        cost_estimate=pl.CostEstimate(flops=10**6, bytes_accessed=10**6, transcendentals=0),
    )(sample_ids, buffer_in, inputs, arrived)
    new_out = call(refresh_kernel, shape(buffer_out.shape), 3, 10**6, 10**6, smem=(0,))(
        sample_ids, message, buffer_out
    )
    return following, new_in, new_out


def solution(mesh):
    sections = mesh.shape["section"]
    fine = Mesh(mesh.devices.reshape(sections, ZN, YN, CN), ("section",) + LANES)
    return jax.shard_map(
        per_device,
        mesh=fine,
        in_specs=(
            P("section", None, None, LANES),
            P("section", None, None),
            P(),
            P("section", None, None, LANES),
            P("section", None, None, LANES),
            P("section", LANES),
            P("section", None, LANES),
            P("section", None, LANES),
            P("section", None, LANES),
        ),
        out_specs=(
            P("section", None, None, LANES),
            P("section", None, None, LANES),
            P("section", None, None, LANES),
        ),
        check_vma=False,
    )
```

```python
import functools
import math

import jax
import jax.numpy as jnp
import numpy as np
from jax import lax
from jax.experimental import pallas as pl
from jax.experimental.pallas import tpu as pltpu
from jax.sharding import Mesh
from jax.sharding import PartitionSpec as P

SEQS, LEN, SLOTS, HEAD, KV_HEADS = 2, 112, 3, 128, 8
ROWS = SEQS * LEN
PAY = ROWS + 16
ZN, YN, CN = 16, 2, 2
PIECES = 4
EARLY = 4
LANES = ("z", "y", "core")
rope_base = 500000.0
norm_eps = 1e-05

VMEM = pl.BlockSpec(memory_space=pltpu.VMEM)
SMEM = pl.BlockSpec(memory_space=pltpu.SMEM)
PARAMS = pltpu.CompilerParams(vmem_limit_bytes=40 * 1024 * 1024)
NT = (((1,), (1,)), ((), ()))


def rope_tables():
    half = HEAD // 2
    frequency = np.exp(np.arange(half) * (-2.0 * math.log(rope_base) / HEAD))
    positions = np.arange(ROWS) % LEN
    angle = positions[:, None] * frequency[None, :]
    return np.cos(angle).astype(np.float32), np.sin(angle).astype(np.float32)


def call(kernel, outs, n_in, flops, bytes_accessed, smem=(), scratch=()):
    return pl.pallas_call(
        kernel,
        out_shape=outs,
        in_specs=[SMEM if i in smem else VMEM for i in range(n_in)],
        out_specs=jax.tree.map(lambda _: VMEM, outs),
        scratch_shapes=list(scratch),
        compiler_params=PARAMS,
        cost_estimate=pl.CostEstimate(
            flops=flops, bytes_accessed=bytes_accessed, transcendentals=0
        ),
    )


def shape(dims, dtype=jnp.bfloat16):
    return jax.ShapeDtypeStruct(dims, dtype)


def prepare(
    ids, codes, exponents, buffer_in, gain, query, keyval, output,
    packed, pay_out, inputs_out,
    codes_v, exponents_v, stored_v, gain_v, keyval_v, half_v, keyval_half_v, early_v, pay, inputs_v,
    sems, half_sems,
):
    section = lax.axis_index("section")
    far = lax.axis_index("y") ^ 1
    copies = [
        pltpu.make_async_copy(exponents, exponents_v, sems.at[0]),
        pltpu.make_async_copy(gain, gain_v, sems.at[1]),
        pltpu.make_async_copy(codes, codes_v, sems.at[2]),
        pltpu.make_async_copy(buffer_in.at[0, ids[0, section]], stored_v.at[0], sems.at[3]),
        pltpu.make_async_copy(buffer_in.at[0, ids[1, section]], stored_v.at[1], sems.at[4]),
        pltpu.make_async_copy(keyval, keyval_v, sems.at[5]),
    ]
    for item in copies:
        item.start()

    step = ZN // PIECES
    moves = [
        (query.at[pl.ds(i * step, step), far], half_v.at[i], packed.at[pl.ds(i * step, step)])
        for i in range(PIECES)
    ]
    tail = ZN + keyval_half_v.shape[0]
    moves.append((output.at[pl.ds(0, EARLY), far], early_v, packed.at[pl.ds(tail, EARLY)]))
    loads, stores = [], []
    for i, (source, between, target) in enumerate(moves):
        loads.append(pltpu.make_async_copy(source, between, half_sems.at[0, i]))
        stores.append(pltpu.make_async_copy(between, target, half_sems.at[1, i]))
        loads[-1].start()
    for item in copies[:5]:
        item.wait()
    eye = lax.broadcasted_iota(jnp.int32, (LEN, LEN), 0) == lax.broadcasted_iota(
        jnp.int32, (LEN, LEN), 1
    )
    gains = gain_v[...].astype(jnp.float32)
    sums = []
    for s in range(SEQS):
        steps = jnp.exp2(exponents_v[0, s : s + 1, :].astype(jnp.float32))
        diagonal = jnp.where(eye, steps, 0.0).astype(jnp.bfloat16)
        scales = jnp.dot(
            diagonal, jnp.ones((LEN, HEAD), jnp.bfloat16), preferred_element_type=jnp.float32
        )
        stored = stored_v[s].astype(jnp.float32)
        inputs = (stored + codes_v[0, s].astype(jnp.float32) * scales).astype(jnp.bfloat16)
        inputs_v[s] = inputs
        widened = inputs.astype(jnp.float32)
        pay[s * LEN : (s + 1) * LEN, :] = (widened * gains).astype(jnp.bfloat16)
        squares = widened * widened
        high = squares.astype(jnp.bfloat16)
        low = (squares - high.astype(jnp.float32)).astype(jnp.bfloat16)
        ones = jnp.ones((16, HEAD), jnp.bfloat16)
        total = lax.dot_general(ones, high, NT, preferred_element_type=jnp.float32)
        total += lax.dot_general(ones, low, NT, preferred_element_type=jnp.float32)
        sums.append(jnp.concatenate([total, jnp.zeros((16, HEAD - LEN), jnp.float32)], axis=1))
    row = lax.broadcasted_iota(jnp.int32, (16, HEAD), 0)
    value = jnp.where(row % 2 == 0, sums[0], sums[1])
    first = value.astype(jnp.bfloat16).astype(jnp.float32)
    second = value - first
    tail = jnp.where(row < 2, first, jnp.where(row < 4, second, 0.0))
    pay[ROWS:PAY, :] = tail.astype(jnp.bfloat16)
    stores.append(pltpu.make_async_copy(pay, pay_out, sems.at[7]))
    stores[-1].start()
    stores.append(pltpu.make_async_copy(inputs_v, inputs_out, sems.at[8]))
    stores[-1].start()

    for load, store in zip(loads, stores):
        load.wait()
        store.start()
    copies[5].wait()
    kv_width = keyval.shape[1]
    per_row = CN * HEAD // kv_width
    for z in range(ZN):
        for core in range(CN):
            i = z * CN + core
            start = (i % per_row) * kv_width
            keyval_half_v[i // per_row, start : start + kv_width, :] = keyval_v[
                0, :, head_rows(z, far, core)
            ]
    last = pltpu.make_async_copy(
        keyval_half_v, packed.at[pl.ds(ZN, keyval_half_v.shape[0])], sems.at[6]
    )
    last.start()
    last.wait()
    for store in stores:
        store.wait()


def head_rows(z, y, core):
    head = z * (YN * CN) + y * CN + core
    return pl.ds(pl.multiple_of(head * HEAD, HEAD), HEAD)


def half_rows(z, core):
    return pl.ds(pl.multiple_of((z * CN + core) * HEAD, HEAD), HEAD)


def keyval_kernel(here, there, weight, received, out, sums_out):
    y, core = lax.axis_index("y"), lax.axis_index("core")
    kv_width = weight.shape[1]
    sums = jnp.sum(here[:, ROWS:PAY, :].astype(jnp.float32), axis=0)
    sums += jnp.sum(there[:, ROWS:PAY, :].astype(jnp.float32), axis=0)
    sums = jnp.concatenate(
        [sums[s : s + 1, :LEN] + sums[SEQS + s : SEQS + s + 1, :LEN] for s in range(SEQS)], axis=1
    )
    high = sums.astype(jnp.bfloat16).astype(jnp.float32)
    row = lax.broadcasted_iota(jnp.int32, (PAY - ROWS, ROWS), 0)
    tail = jnp.where(row == 0, high, jnp.where(row == 1, sums - high, 0.0))
    sums_out[...] = tail.astype(jnp.bfloat16)
    acc = jnp.zeros((2 * kv_width, ROWS), jnp.float32)
    for z in range(ZN):
        block = jnp.concatenate([here[z, :ROWS, :], there[z, :ROWS, :]], axis=1)
        parts = []
        for side in (core, core ^ 1):
            start = ZN * CN * HEAD + (z * CN + side) * kv_width
            mine = weight[0, :, head_rows(z, y, side)]
            other = received[pl.ds(pl.multiple_of(start, kv_width), kv_width), :]
            parts.append(jnp.concatenate([mine, other], axis=0))
        part = jnp.concatenate(parts, axis=1)
        acc += lax.dot_general(part, block, NT, preferred_element_type=jnp.float32)
    out[...] = acc.astype(jnp.bfloat16)


def both_partials(here, there, weight, received):
    y, core = lax.axis_index("y"), lax.axis_index("core")
    acc = jnp.zeros((ROWS, 2 * HEAD), jnp.float32)
    for z in range(ZN):
        block = jnp.concatenate([here[z, :ROWS, :], there[z, :ROWS, :]], axis=1)
        parts = []
        for side in (core, core ^ 1):
            mine = weight[0, head_rows(z, y, side), :]
            other = received[half_rows(z, side), :]
            parts.append(jnp.concatenate([mine, other], axis=1))
        part = jnp.concatenate(parts, axis=0)
        acc += jnp.dot(block, part, preferred_element_type=jnp.float32)
    return acc


def query_kernel(here, there, weight, received, mine_out, other_out):
    acc = both_partials(here, there, weight, received)
    mine_out[...] = acc[:, :HEAD]
    other_out[...] = acc[:, HEAD:].astype(jnp.bfloat16)


def sum_kernel(near, far, cos_t, sin_t, out, factors_out):
    z_odd, y, core = lax.axis_index("z") % 2, lax.axis_index("y"), lax.axis_index("core")
    width = (near.shape[0] - (PAY - ROWS)) // 4
    tail = near[4 * width :, :].astype(jnp.float32) + far[4 * width :, :].astype(jnp.float32)
    square_sum = tail[0:1, :] + tail[1:2, :]
    inverse = lax.rsqrt(square_sum / (ZN * YN * CN * HEAD) + norm_eps)
    factors = jnp.broadcast_to(inverse, (width, ROWS))
    factors_out[...] = jnp.broadcast_to(inverse, (HEAD, ROWS)).T

    def piece(kind, which):
        plane = z_odd ^ kind
        a = near[pl.ds(pl.multiple_of((plane * 2 + (which ^ y)) * width, width), width), :]
        b = far[pl.ds(pl.multiple_of((plane * 2 + 1 - (which ^ y)) * width, width), width), :]
        return ((a.astype(jnp.float32) + b.astype(jnp.float32)) * factors).astype(jnp.bfloat16)

    first, second = piece(0, 0).astype(jnp.float32), piece(0, 1).astype(jnp.float32)
    rows = pl.ds(pl.multiple_of(core * width, width), width)
    c, s = cos_t[rows, :], sin_t[rows, :]
    out[0] = (first * c - second * s).astype(jnp.bfloat16)
    out[1] = (second * c + first * s).astype(jnp.bfloat16)
    out[2] = piece(1, 0)
    out[3] = piece(1, 1)


def rope_kernel(mine, other, factors, cos, sin, out):
    acc = (mine[...] + other[...].astype(jnp.float32)) * factors[...]
    first, second = acc[:, : HEAD // 2], acc[:, HEAD // 2 :]
    c, s = cos[...], sin[...]
    out[...] = jnp.concatenate(
        [first * c - second * s, second * c + first * s], axis=1
    ).astype(jnp.bfloat16)


def attention_kernel(query, own, sibling, out):
    core = lax.axis_index("core")
    keys_values = []
    for kind in range(2):
        parts = []
        for which in range(2):
            a, b = own[2 * kind + which], sibling[2 * kind + which]
            parts += [jnp.where(core == 0, a, b), jnp.where(core == 0, b, a)]
        keys_values.append(jnp.concatenate(parts, axis=0))
    keys, values = keys_values
    scores = jnp.dot(query[...], keys, preferred_element_type=jnp.float32) / math.sqrt(HEAD)
    row = lax.broadcasted_iota(jnp.int32, (ROWS, ROWS), 0)
    column = lax.broadcasted_iota(jnp.int32, (ROWS, ROWS), 1)
    allowed = (column <= row) & ((row < LEN) | (column >= LEN))
    scores = jnp.where(allowed, scores, -1e30)
    peak = jnp.max(scores, axis=-1, keepdims=True)
    raised = jnp.exp(scores - peak)
    weights = (raised / jnp.sum(raised, axis=-1, keepdims=True)).astype(jnp.bfloat16)
    context = lax.dot_general(weights, values, NT, preferred_element_type=jnp.float32)
    out[...] = context.astype(jnp.bfloat16)


def pack_kernel(weight, out):
    far = lax.axis_index("y") ^ 1
    for z in range(EARLY, ZN):
        out[z - EARLY] = weight[z, far]


def line_product(line, rows):
    acc = None
    for z in range(0, ZN, 2):
        block = jnp.concatenate([line[z], line[z + 1]], axis=1)
        part = jnp.concatenate([rows(z), rows(z + 1)], axis=0)
        term = jnp.dot(block, part, preferred_element_type=jnp.float32)
        acc = term if acc is None else acc + term
    return acc


def far_rows(z, core, early, received):
    if z < EARLY:
        return early[half_rows(z, core), :]
    return received[half_rows(z - EARLY, core), :]


def own_line_kernel(line, weight, early, received, out):
    y, core = lax.axis_index("y"), lax.axis_index("core")

    def rows(z):
        mine = weight[0, head_rows(z, y, core), :]
        return jnp.concatenate([mine, far_rows(z, core, early, received)], axis=1)

    out[...] = line_product(line, rows)


def far_columns_kernel(line, acc, early, received, out):
    side = lax.axis_index("core") ^ 1
    total = line_product(line, lambda z: far_rows(z, side, early, received))
    out[...] = (acc[:, HEAD:] + total).astype(jnp.bfloat16)


def own_columns_kernel(line, acc, weight, out):
    y, side = lax.axis_index("y"), lax.axis_index("core") ^ 1
    out[...] = acc[:, :HEAD] + line_product(line, lambda z: weight[0, head_rows(z, y, side), :])


def message_kernel(ids, mine, other, inputs, buffer_out, message_out):
    section = lax.axis_index("section")
    for s in range(SEQS):
        rows = slice(s * LEN, (s + 1) * LEN)
        stored = buffer_out[0, ids[s, section]].astype(jnp.float32)
        mixed = mine[rows, :] + other[rows, :].astype(jnp.float32)
        message_out[s] = (inputs[s].astype(jnp.float32) + mixed - stored).astype(jnp.bfloat16)


def refresh_kernel(ids, message, buffer_out, new_out):
    section = lax.axis_index("section")
    new_out[...] = buffer_out[...]
    for s in range(SEQS):
        slot = ids[s, section]
        stored = buffer_out[0, slot].astype(jnp.float32)
        new_out[0, slot] = (stored + message[s].astype(jnp.float32)).astype(jnp.bfloat16)


def finish_kernel(ids, buffer_in, inputs, arrived, following_out, stored_out, following, stored, sems):
    section = lax.axis_index("section")
    before = jnp.maximum(section - 1, 0)
    stored[...] = buffer_in[0]
    for s in range(SEQS):
        stored[ids[s, section]] = inputs[s]
    copies = []
    for s in range(SEQS):
        current = stored[ids[s, before]].astype(jnp.float32)
        following[s] = (current + arrived[s].astype(jnp.float32)).astype(jnp.bfloat16)
        copies.append(
            pltpu.make_async_copy(following.at[s], following_out.at[0, s], sems.at[s])
        )
        copies[-1].start()
    for s in range(SEQS):
        stored[ids[s, before]] = following[s]
    copies.append(pltpu.make_async_copy(stored, stored_out.at[0], sems.at[SEQS]))
    copies[-1].start()
    for item in copies:
        item.wait()


def lane(z, y, core):
    return (z % ZN) * (YN * CN) + y * CN + core


def permute(x, target):
    pairs = [
        (lane(z, y, c), lane(*target(z, y, c)))
        for z in range(ZN)
        for y in range(YN)
        for c in range(CN)
    ]
    return lax.ppermute(x, LANES, pairs)


def swap(x, flip_y, flip_core):
    return permute(x, lambda z, y, c: (z, y ^ flip_y, c ^ flip_core))


def after(x, earlier):
    return lax.optimization_barrier((x, earlier))[0]


def gather_z(x):
    return lax.all_gather(x, "z", axis=0)


def per_device(
    codes, exponents, sample_ids, buffer_in, buffer_out, norm_gain, w_query, w_keyval, w_output
):
    cos, sin = rope_tables()
    sample_ids = sample_ids.T
    kv_width = w_keyval.shape[2]
    half = ZN * CN * HEAD
    w_keyval = jnp.swapaxes(w_keyval, 1, 2)
    partial_flops = 2 * ROWS * half * 256
    wide = shape((ROWS, HEAD), jnp.float32)

    by_half = (ZN, YN, CN * HEAD, HEAD)
    any_spec = pl.BlockSpec(memory_space=pl.ANY)
    bf16, int32 = jnp.bfloat16, jnp.int32
    packed, pay, inputs = pl.pallas_call(
        prepare,
        out_shape=(
            shape((ZN + ZN * kv_width // HEAD + EARLY, CN * HEAD, HEAD)),
            shape((PAY, HEAD)),
            shape((SEQS, LEN, HEAD)),
        ),
        in_specs=[SMEM] + [any_spec] * 7,
        out_specs=(any_spec,) * 3,
        scratch_shapes=[
            pltpu.VMEM(codes.shape, int32),
            pltpu.VMEM(exponents.shape, int32),
            pltpu.VMEM((SEQS, LEN, HEAD), bf16),
            pltpu.VMEM(norm_gain.shape, bf16),
            pltpu.VMEM(w_keyval.shape, bf16),
            pltpu.VMEM((PIECES, ZN // PIECES, CN * HEAD, HEAD), bf16),
            pltpu.VMEM((ZN * kv_width // HEAD, CN * HEAD, HEAD), bf16),
            pltpu.VMEM((EARLY, CN * HEAD, HEAD), bf16),
            pltpu.VMEM((PAY, HEAD), bf16),
            pltpu.VMEM((SEQS, LEN, HEAD), bf16),
            pltpu.SemaphoreType.DMA((9,)),
            pltpu.SemaphoreType.DMA((2, PIECES + 1)),
        ],
        cost_estimate=pl.CostEstimate(flops=10**7, bytes_accessed=4 * 10**6, transcendentals=0),
    )(
        sample_ids, codes, exponents, buffer_in, norm_gain,
        w_query.reshape(by_half), w_keyval, w_output.reshape(by_half),
    )
    received = swap(packed, 1, 0).reshape(-1, HEAD)
    here = gather_z(pay)
    there = swap(here, 0, 1)
    packed_out = call(pack_kernel, shape((ZN - EARLY, CN * HEAD, HEAD)), 1, 10**6, 2 * 10**6)(
        w_output.reshape(by_half)
    )
    received_out = swap(packed_out, 1, 0).reshape(-1, HEAD)

    keyval, sums = call(
        keyval_kernel,
        (shape((2 * kv_width, ROWS)), shape((PAY - ROWS, ROWS))),
        4,
        partial_flops,
        5 * 10**6,
    )(here, there, w_keyval, received)
    even = permute(keyval, lambda z, y, c: (2 * z if z < 8 else 2 * (z - 8) + 1, y, c))
    mine, other = call(
        query_kernel, (wide, shape((ROWS, HEAD))), 4, partial_flops, 6 * 10**6
    )(here, there, w_query, after(received, keyval))
    other = swap(other, 1, 0)
    odd = permute(after(even, mine), lambda z, y, c: (z ^ 1, y, c))
    near = jnp.concatenate([even, odd, sums])
    far = swap(near, 1, 0)
    own, factors = call(
        sum_kernel, (shape((4, kv_width, ROWS)), wide), 4, 10**6, 10**6
    )(after(near, received_out), far, cos.T.copy(), sin.T.copy())
    sibling = swap(own, 0, 1)
    queries = call(rope_kernel, shape((ROWS, HEAD)), 5, 10**6, 10**6)(
        mine, other, factors, cos, sin
    )
    context = call(attention_kernel, shape((ROWS, HEAD)), 3, 4 * ROWS * ROWS * HEAD, 10**6)(
        queries, own, sibling
    )

    here = gather_z(context)
    there = swap(here, 0, 1)
    early = received[-EARLY * CN * HEAD :]
    line_flops = partial_flops // 2
    both = call(
        own_line_kernel, shape((ROWS, 2 * HEAD), jnp.float32), 4, line_flops, 4 * 10**6
    )(here, w_output, early, received_out)
    other = call(far_columns_kernel, shape((ROWS, HEAD)), 4, line_flops, 2 * 10**6)(
        there, both, early, received_out
    )
    other = swap(other, 1, 0)
    mine = call(own_columns_kernel, wide, 3, line_flops, 3 * 10**6)(there, both, w_output)
    message = call(
        message_kernel, shape((SEQS, LEN, HEAD)), 5, 10**6, 10**6, smem=(0,)
    )(sample_ids, mine, other, inputs, buffer_out)

    sections = lax.axis_size("section")
    arrived = lax.ppermute(message, "section", [(i, i + 1) for i in range(sections - 1)])
    following, new_in = pl.pallas_call(
        finish_kernel,
        out_shape=(shape((1, SEQS, LEN, HEAD)), shape(buffer_in.shape)),
        in_specs=[SMEM] + [VMEM] * 3,
        out_specs=(any_spec,) * 2,
        scratch_shapes=[
            pltpu.VMEM((SEQS, LEN, HEAD), bf16),
            pltpu.VMEM((SLOTS, LEN, HEAD), bf16),
            pltpu.SemaphoreType.DMA((SEQS + 1,)),
        ],
        compiler_params=PARAMS,
        cost_estimate=pl.CostEstimate(flops=10**6, bytes_accessed=10**6, transcendentals=0),
    )(sample_ids, buffer_in, inputs, arrived)
    new_out = call(refresh_kernel, shape(buffer_out.shape), 3, 10**6, 10**6, smem=(0,))(
        sample_ids, message, buffer_out
    )
    return following, new_in, new_out


def solution(mesh):
    sections = mesh.shape["section"]
    fine = Mesh(mesh.devices.reshape(sections, ZN, YN, CN), ("section",) + LANES)
    return jax.shard_map(
        per_device,
        mesh=fine,
        in_specs=(
            P("section", None, None, LANES),
            P("section", None, None),
            P(),
            P("section", None, None, LANES),
            P("section", None, None, LANES),
            P("section", LANES),
            P("section", None, LANES),
            P("section", None, LANES),
            P("section", None, LANES),
        ),
        out_specs=(
            P("section", None, None, LANES),
            P("section", None, None, LANES),
            P("section", None, None, LANES),
        ),
        check_vma=False,
    )
```

```python
import functools
import math

import jax
import jax.numpy as jnp
import numpy as np
from jax import lax
from jax.experimental import pallas as pl
from jax.experimental.pallas import tpu as pltpu
from jax.sharding import Mesh
from jax.sharding import PartitionSpec as P

SEQS, LEN, SLOTS, HEAD, KV_HEADS = 2, 112, 3, 128, 8
ROWS = SEQS * LEN
PAY = ROWS + 16
ZN, YN, CN = 16, 2, 2
PIECES = 4
EARLY = 4
LANES = ("z", "y", "core")
rope_base = 500000.0
norm_eps = 1e-05

VMEM = pl.BlockSpec(memory_space=pltpu.VMEM)
SMEM = pl.BlockSpec(memory_space=pltpu.SMEM)
PARAMS = pltpu.CompilerParams(vmem_limit_bytes=40 * 1024 * 1024)
NT = (((1,), (1,)), ((), ()))


def rope_tables():
    half = HEAD // 2
    frequency = np.exp(np.arange(half) * (-2.0 * math.log(rope_base) / HEAD))
    positions = np.arange(ROWS) % LEN
    angle = positions[:, None] * frequency[None, :]
    return np.cos(angle).astype(np.float32), np.sin(angle).astype(np.float32)


def call(kernel, outs, n_in, flops, bytes_accessed, smem=(), scratch=()):
    return pl.pallas_call(
        kernel,
        out_shape=outs,
        in_specs=[SMEM if i in smem else VMEM for i in range(n_in)],
        out_specs=jax.tree.map(lambda _: VMEM, outs),
        scratch_shapes=list(scratch),
        compiler_params=PARAMS,
        cost_estimate=pl.CostEstimate(
            flops=flops, bytes_accessed=bytes_accessed, transcendentals=0
        ),
    )


def shape(dims, dtype=jnp.bfloat16):
    return jax.ShapeDtypeStruct(dims, dtype)


def prepare(
    ids, codes, exponents, buffer_in, gain, query, keyval, output,
    packed, pay_out, inputs_out,
    codes_v, exponents_v, stored_v, gain_v, keyval_v, half_v, keyval_half_v, early_v, pay, inputs_v,
    sems, half_sems,
):
    section = lax.axis_index("section")
    far = lax.axis_index("y") ^ 1
    copies = [
        pltpu.make_async_copy(exponents, exponents_v, sems.at[0]),
        pltpu.make_async_copy(gain, gain_v, sems.at[1]),
        pltpu.make_async_copy(codes, codes_v, sems.at[2]),
        pltpu.make_async_copy(buffer_in.at[0, ids[0, section]], stored_v.at[0], sems.at[3]),
        pltpu.make_async_copy(buffer_in.at[0, ids[1, section]], stored_v.at[1], sems.at[4]),
        pltpu.make_async_copy(keyval, keyval_v, sems.at[5]),
    ]
    for item in copies:
        item.start()

    step = ZN // PIECES
    moves = [
        (query.at[pl.ds(i * step, step), far], half_v.at[i], packed.at[pl.ds(i * step, step)])
        for i in range(PIECES)
    ]
    tail = ZN + keyval_half_v.shape[0]
    moves.append((output.at[pl.ds(0, EARLY), far], early_v, packed.at[pl.ds(tail, EARLY)]))
    loads, stores = [], []
    for i, (source, between, target) in enumerate(moves):
        loads.append(pltpu.make_async_copy(source, between, half_sems.at[0, i]))
        stores.append(pltpu.make_async_copy(between, target, half_sems.at[1, i]))
        loads[-1].start()
    for item in copies[:5]:
        item.wait()
    eye = lax.broadcasted_iota(jnp.int32, (LEN, LEN), 0) == lax.broadcasted_iota(
        jnp.int32, (LEN, LEN), 1
    )
    gains = gain_v[...].astype(jnp.float32)
    sums = []
    for s in range(SEQS):
        steps = jnp.exp2(exponents_v[0, s : s + 1, :].astype(jnp.float32))
        diagonal = jnp.where(eye, steps, 0.0).astype(jnp.bfloat16)
        scales = jnp.dot(
            diagonal, jnp.ones((LEN, HEAD), jnp.bfloat16), preferred_element_type=jnp.float32
        )
        stored = stored_v[s].astype(jnp.float32)
        inputs = (stored + codes_v[0, s].astype(jnp.float32) * scales).astype(jnp.bfloat16)
        inputs_v[s] = inputs
        widened = inputs.astype(jnp.float32)
        pay[s * LEN : (s + 1) * LEN, :] = (widened * gains).astype(jnp.bfloat16)
        squares = widened * widened
        high = squares.astype(jnp.bfloat16)
        low = (squares - high.astype(jnp.float32)).astype(jnp.bfloat16)
        ones = jnp.ones((16, HEAD), jnp.bfloat16)
        total = lax.dot_general(ones, high, NT, preferred_element_type=jnp.float32)
        total += lax.dot_general(ones, low, NT, preferred_element_type=jnp.float32)
        sums.append(jnp.concatenate([total, jnp.zeros((16, HEAD - LEN), jnp.float32)], axis=1))
    row = lax.broadcasted_iota(jnp.int32, (16, HEAD), 0)
    value = jnp.where(row % 2 == 0, sums[0], sums[1])
    first = value.astype(jnp.bfloat16).astype(jnp.float32)
    second = value - first
    tail = jnp.where(row < 2, first, jnp.where(row < 4, second, 0.0))
    pay[ROWS:PAY, :] = tail.astype(jnp.bfloat16)
    stores.append(pltpu.make_async_copy(pay, pay_out, sems.at[7]))
    stores[-1].start()
    stores.append(pltpu.make_async_copy(inputs_v, inputs_out, sems.at[8]))
    stores[-1].start()

    for load, store in zip(loads, stores):
        load.wait()
        store.start()
    copies[5].wait()
    kv_width = keyval.shape[1]
    per_row = CN * HEAD // kv_width
    for z in range(ZN):
        for core in range(CN):
            i = z * CN + core
            start = (i % per_row) * kv_width
            keyval_half_v[i // per_row, start : start + kv_width, :] = keyval_v[
                0, :, head_rows(z, far, core)
            ]
    last = pltpu.make_async_copy(
        keyval_half_v, packed.at[pl.ds(ZN, keyval_half_v.shape[0])], sems.at[6]
    )
    last.start()
    last.wait()
    for store in stores:
        store.wait()


def head_rows(z, y, core):
    head = z * (YN * CN) + y * CN + core
    return pl.ds(pl.multiple_of(head * HEAD, HEAD), HEAD)


def half_rows(z, core):
    return pl.ds(pl.multiple_of((z * CN + core) * HEAD, HEAD), HEAD)


def keyval_kernel(here, there, weight, received, out, sums_out):
    y, core = lax.axis_index("y"), lax.axis_index("core")
    kv_width = weight.shape[1]
    sums = jnp.sum(here[:, ROWS:PAY, :].astype(jnp.float32), axis=0)
    sums += jnp.sum(there[:, ROWS:PAY, :].astype(jnp.float32), axis=0)
    sums = jnp.concatenate(
        [sums[s : s + 1, :LEN] + sums[SEQS + s : SEQS + s + 1, :LEN] for s in range(SEQS)], axis=1
    )
    high = sums.astype(jnp.bfloat16).astype(jnp.float32)
    row = lax.broadcasted_iota(jnp.int32, (PAY - ROWS, ROWS), 0)
    tail = jnp.where(row == 0, high, jnp.where(row == 1, sums - high, 0.0))
    sums_out[...] = tail.astype(jnp.bfloat16)
    acc = jnp.zeros((2 * kv_width, ROWS), jnp.float32)
    for z in range(ZN):
        block = jnp.concatenate([here[z, :ROWS, :], there[z, :ROWS, :]], axis=1)
        parts = []
        for side in (core, core ^ 1):
            start = ZN * CN * HEAD + (z * CN + side) * kv_width
            mine = weight[0, :, head_rows(z, y, side)]
            other = received[pl.ds(pl.multiple_of(start, kv_width), kv_width), :]
            parts.append(jnp.concatenate([mine, other], axis=0))
        part = jnp.concatenate(parts, axis=1)
        acc += lax.dot_general(part, block, NT, preferred_element_type=jnp.float32)
    out[...] = acc.astype(jnp.bfloat16)


def both_partials(here, there, weight, received):
    y, core = lax.axis_index("y"), lax.axis_index("core")
    acc = jnp.zeros((ROWS, 2 * HEAD), jnp.float32)
    for z in range(ZN):
        block = jnp.concatenate([here[z, :ROWS, :], there[z, :ROWS, :]], axis=1)
        parts = []
        for side in (core, core ^ 1):
            mine = weight[0, head_rows(z, y, side), :]
            other = received[half_rows(z, side), :]
            parts.append(jnp.concatenate([mine, other], axis=1))
        part = jnp.concatenate(parts, axis=0)
        acc += jnp.dot(block, part, preferred_element_type=jnp.float32)
    return acc


def query_kernel(here, there, weight, received, mine_out, other_out):
    acc = both_partials(here, there, weight, received)
    mine_out[...] = acc[:, :HEAD]
    other_out[...] = acc[:, HEAD:].astype(jnp.bfloat16)


def sum_kernel(near, far, cos_t, sin_t, out, factors_out):
    y, core = lax.axis_index("y"), lax.axis_index("core")
    keys = lax.axis_index("z") % 2 == core
    width = (near.shape[0] - (PAY - ROWS)) // 4
    tail = near[4 * width :, :].astype(jnp.float32) + far[4 * width :, :].astype(jnp.float32)
    square_sum = tail[0:1, :] + tail[1:2, :]
    inverse = lax.rsqrt(square_sum / (ZN * YN * CN * HEAD) + norm_eps)
    factors = jnp.broadcast_to(inverse, (width, ROWS))
    factors_out[...] = jnp.broadcast_to(inverse, (HEAD, ROWS)).T

    def piece(which, side):
        spot = (side ^ core) * 2
        a = near[pl.ds(pl.multiple_of((spot + (which ^ y)) * width, width), width), :]
        b = far[pl.ds(pl.multiple_of((spot + 1 - (which ^ y)) * width, width), width), :]
        total = (a.astype(jnp.float32) + b.astype(jnp.float32)) * factors
        return total.astype(jnp.bfloat16).astype(jnp.float32)

    for side in range(CN):
        first, second = piece(0, side), piece(1, side)
        rows = slice(side * width, (side + 1) * width)
        c, s = cos_t[rows, :], sin_t[rows, :]
        out[0, rows, :] = jnp.where(keys, first * c - second * s, first).astype(jnp.bfloat16)
        out[1, rows, :] = jnp.where(keys, second * c + first * s, second).astype(jnp.bfloat16)


def rope_kernel(mine, other, factors, cos, sin, out):
    acc = (mine[...] + other[...].astype(jnp.float32)) * factors[...]
    first, second = acc[:, : HEAD // 2], acc[:, HEAD // 2 :]
    c, s = cos[...], sin[...]
    out[...] = jnp.concatenate(
        [first * c - second * s, second * c + first * s], axis=1
    ).astype(jnp.bfloat16)


def attention_kernel(query, own, sibling, out):
    here = jnp.concatenate([own[0], own[1]], axis=0)
    there = jnp.concatenate([sibling[0], sibling[1]], axis=0)
    has_keys = lax.axis_index("z") % 2 == lax.axis_index("core")
    keys, values = jnp.where(has_keys, here, there), jnp.where(has_keys, there, here)
    scores = jnp.dot(query[...], keys, preferred_element_type=jnp.float32) / math.sqrt(HEAD)
    row = lax.broadcasted_iota(jnp.int32, (ROWS, ROWS), 0)
    column = lax.broadcasted_iota(jnp.int32, (ROWS, ROWS), 1)
    allowed = (column <= row) & ((row < LEN) | (column >= LEN))
    scores = jnp.where(allowed, scores, -1e30)
    peak = jnp.max(scores, axis=-1, keepdims=True)
    raised = jnp.exp(scores - peak)
    weights = (raised / jnp.sum(raised, axis=-1, keepdims=True)).astype(jnp.bfloat16)
    context = lax.dot_general(weights, values, NT, preferred_element_type=jnp.float32)
    out[...] = context.astype(jnp.bfloat16)


def pack_kernel(weight, out):
    far = lax.axis_index("y") ^ 1
    for z in range(EARLY, ZN):
        out[z - EARLY] = weight[z, far]


def line_product(line, rows):
    acc = None
    for z in range(0, ZN, 2):
        block = jnp.concatenate([line[z], line[z + 1]], axis=1)
        part = jnp.concatenate([rows(z), rows(z + 1)], axis=0)
        term = jnp.dot(block, part, preferred_element_type=jnp.float32)
        acc = term if acc is None else acc + term
    return acc


def far_rows(z, core, early, received):
    if z < EARLY:
        return early[half_rows(z, core), :]
    return received[half_rows(z - EARLY, core), :]


def own_line_kernel(line, weight, early, received, out):
    y, core = lax.axis_index("y"), lax.axis_index("core")

    def rows(z):
        mine = weight[0, head_rows(z, y, core), :]
        return jnp.concatenate([mine, far_rows(z, core, early, received)], axis=1)

    out[...] = line_product(line, rows)


def far_columns_kernel(line, acc, early, received, out):
    side = lax.axis_index("core") ^ 1
    total = line_product(line, lambda z: far_rows(z, side, early, received))
    out[...] = (acc[:, HEAD:] + total).astype(jnp.bfloat16)


def own_columns_kernel(line, acc, weight, out):
    y, side = lax.axis_index("y"), lax.axis_index("core") ^ 1
    out[...] = acc[:, :HEAD] + line_product(line, lambda z: weight[0, head_rows(z, y, side), :])


def message_kernel(ids, mine, other, inputs, buffer_out, message_out):
    section = lax.axis_index("section")
    for s in range(SEQS):
        rows = slice(s * LEN, (s + 1) * LEN)
        stored = buffer_out[0, ids[s, section]].astype(jnp.float32)
        mixed = mine[rows, :] + other[rows, :].astype(jnp.float32)
        message_out[s] = (inputs[s].astype(jnp.float32) + mixed - stored).astype(jnp.bfloat16)


def refresh_kernel(ids, message, buffer_out, new_out):
    section = lax.axis_index("section")
    new_out[...] = buffer_out[...]
    for s in range(SEQS):
        slot = ids[s, section]
        stored = buffer_out[0, slot].astype(jnp.float32)
        new_out[0, slot] = (stored + message[s].astype(jnp.float32)).astype(jnp.bfloat16)


def finish_kernel(ids, buffer_in, inputs, arrived, following_out, stored_out, following, stored, sems):
    section = lax.axis_index("section")
    before = jnp.maximum(section - 1, 0)
    stored[...] = buffer_in[0]
    for s in range(SEQS):
        stored[ids[s, section]] = inputs[s]
    copies = []
    for s in range(SEQS):
        current = stored[ids[s, before]].astype(jnp.float32)
        following[s] = (current + arrived[s].astype(jnp.float32)).astype(jnp.bfloat16)
        copies.append(
            pltpu.make_async_copy(following.at[s], following_out.at[0, s], sems.at[s])
        )
        copies[-1].start()
    for s in range(SEQS):
        stored[ids[s, before]] = following[s]
    copies.append(pltpu.make_async_copy(stored, stored_out.at[0], sems.at[SEQS]))
    copies[-1].start()
    for item in copies:
        item.wait()


def lane(z, y, core):
    return (z % ZN) * (YN * CN) + y * CN + core


def permute(x, target):
    pairs = [
        (lane(z, y, c), lane(*target(z, y, c)))
        for z in range(ZN)
        for y in range(YN)
        for c in range(CN)
    ]
    return lax.ppermute(x, LANES, pairs)


def swap(x, flip_y, flip_core):
    return permute(x, lambda z, y, c: (z, y ^ flip_y, c ^ flip_core))


def pair_plane(z, y, c):
    kind, g = z // KV_HEADS, z % KV_HEADS
    return 2 * g + (kind ^ c), y, c


def after(x, earlier):
    return lax.optimization_barrier((x, earlier))[0]


def gather_z(x):
    return lax.all_gather(x, "z", axis=0)


def per_device(
    codes, exponents, sample_ids, buffer_in, buffer_out, norm_gain, w_query, w_keyval, w_output
):
    cos, sin = rope_tables()
    sample_ids = sample_ids.T
    kv_width = w_keyval.shape[2]
    half = ZN * CN * HEAD
    w_keyval = jnp.swapaxes(w_keyval, 1, 2)
    partial_flops = 2 * ROWS * half * 256
    wide = shape((ROWS, HEAD), jnp.float32)

    by_half = (ZN, YN, CN * HEAD, HEAD)
    any_spec = pl.BlockSpec(memory_space=pl.ANY)
    bf16, int32 = jnp.bfloat16, jnp.int32
    packed, pay, inputs = pl.pallas_call(
        prepare,
        out_shape=(
            shape((ZN + ZN * kv_width // HEAD + EARLY, CN * HEAD, HEAD)),
            shape((PAY, HEAD)),
            shape((SEQS, LEN, HEAD)),
        ),
        in_specs=[SMEM] + [any_spec] * 7,
        out_specs=(any_spec,) * 3,
        scratch_shapes=[
            pltpu.VMEM(codes.shape, int32),
            pltpu.VMEM(exponents.shape, int32),
            pltpu.VMEM((SEQS, LEN, HEAD), bf16),
            pltpu.VMEM(norm_gain.shape, bf16),
            pltpu.VMEM(w_keyval.shape, bf16),
            pltpu.VMEM((PIECES, ZN // PIECES, CN * HEAD, HEAD), bf16),
            pltpu.VMEM((ZN * kv_width // HEAD, CN * HEAD, HEAD), bf16),
            pltpu.VMEM((EARLY, CN * HEAD, HEAD), bf16),
            pltpu.VMEM((PAY, HEAD), bf16),
            pltpu.VMEM((SEQS, LEN, HEAD), bf16),
            pltpu.SemaphoreType.DMA((9,)),
            pltpu.SemaphoreType.DMA((2, PIECES + 1)),
        ],
        cost_estimate=pl.CostEstimate(flops=10**7, bytes_accessed=4 * 10**6, transcendentals=0),
    )(
        sample_ids, codes, exponents, buffer_in, norm_gain,
        w_query.reshape(by_half), w_keyval, w_output.reshape(by_half),
    )
    received = swap(packed, 1, 0).reshape(-1, HEAD)
    here = gather_z(pay)
    there = swap(here, 0, 1)
    packed_out = call(pack_kernel, shape((ZN - EARLY, CN * HEAD, HEAD)), 1, 10**6, 2 * 10**6)(
        w_output.reshape(by_half)
    )
    received_out = swap(packed_out, 1, 0).reshape(-1, HEAD)

    keyval, sums = call(
        keyval_kernel,
        (shape((2 * kv_width, ROWS)), shape((PAY - ROWS, ROWS))),
        4,
        partial_flops,
        5 * 10**6,
    )(here, there, w_keyval, received)
    keyval = jnp.concatenate([keyval, swap(keyval, 0, 1)])
    keyval = permute(keyval, pair_plane)
    mine, other = call(
        query_kernel, (wide, shape((ROWS, HEAD))), 4, partial_flops, 6 * 10**6
    )(here, there, w_query, after(received, sums))
    other = swap(other, 1, 0)
    near = after(jnp.concatenate([keyval, sums]), mine)
    far = swap(near, 1, 0)
    own, factors = call(
        sum_kernel, (shape((2, HEAD // 2, ROWS)), wide), 4, 10**6, 10**6
    )(after(near, received_out), far, cos.T.copy(), sin.T.copy())
    sibling = swap(own, 0, 1)
    queries = call(rope_kernel, shape((ROWS, HEAD)), 5, 10**6, 10**6)(
        mine, other, factors, cos, sin
    )
    context = call(attention_kernel, shape((ROWS, HEAD)), 3, 4 * ROWS * ROWS * HEAD, 10**6)(
        queries, own, sibling
    )

    here = gather_z(context)
    there = swap(here, 0, 1)
    early = received[-EARLY * CN * HEAD :]
    line_flops = partial_flops // 2
    both = call(
        own_line_kernel, shape((ROWS, 2 * HEAD), jnp.float32), 4, line_flops, 4 * 10**6
    )(here, w_output, early, received_out)
    other = call(far_columns_kernel, shape((ROWS, HEAD)), 4, line_flops, 2 * 10**6)(
        there, both, early, received_out
    )
    other = swap(other, 1, 0)
    mine = call(own_columns_kernel, wide, 3, line_flops, 3 * 10**6)(there, both, w_output)
    message = call(
        message_kernel, shape((SEQS, LEN, HEAD)), 5, 10**6, 10**6, smem=(0,)
    )(sample_ids, mine, other, inputs, buffer_out)

    sections = lax.axis_size("section")
    arrived = lax.ppermute(message, "section", [(i, i + 1) for i in range(sections - 1)])
    following, new_in = pl.pallas_call(
        finish_kernel,
        out_shape=(shape((1, SEQS, LEN, HEAD)), shape(buffer_in.shape)),
        in_specs=[SMEM] + [VMEM] * 3,
        out_specs=(any_spec,) * 2,
        scratch_shapes=[
            pltpu.VMEM((SEQS, LEN, HEAD), bf16),
            pltpu.VMEM((SLOTS, LEN, HEAD), bf16),
            pltpu.SemaphoreType.DMA((SEQS + 1,)),
        ],
        compiler_params=PARAMS,
        cost_estimate=pl.CostEstimate(flops=10**6, bytes_accessed=10**6, transcendentals=0),
    )(sample_ids, buffer_in, inputs, arrived)
    new_out = call(refresh_kernel, shape(buffer_out.shape), 3, 10**6, 10**6, smem=(0,))(
        sample_ids, message, buffer_out
    )
    return following, new_in, new_out


def solution(mesh):
    sections = mesh.shape["section"]
    fine = Mesh(mesh.devices.reshape(sections, ZN, YN, CN), ("section",) + LANES)
    return jax.shard_map(
        per_device,
        mesh=fine,
        in_specs=(
            P("section", None, None, LANES),
            P("section", None, None),
            P(),
            P("section", None, None, LANES),
            P("section", None, None, LANES),
            P("section", LANES),
            P("section", None, LANES),
            P("section", None, LANES),
            P("section", None, LANES),
        ),
        out_specs=(
            P("section", None, None, LANES),
            P("section", None, None, LANES),
            P("section", None, None, LANES),
        ),
        check_vma=False,
    )
```

```python
import functools
import math

import jax
import jax.numpy as jnp
import numpy as np
from jax import lax
from jax.experimental import pallas as pl
from jax.experimental.pallas import tpu as pltpu
from jax.sharding import Mesh
from jax.sharding import PartitionSpec as P

SEQS, LEN, SLOTS, HEAD, KV_HEADS = 2, 112, 3, 128, 8
ROWS = SEQS * LEN
PAY = ROWS + 16
ZN, YN, CN = 16, 2, 2
PIECES = 4
EARLY = 4
LANES = ("z", "y", "core")
rope_base = 500000.0
norm_eps = 1e-05

VMEM = pl.BlockSpec(memory_space=pltpu.VMEM)
SMEM = pl.BlockSpec(memory_space=pltpu.SMEM)
PARAMS = pltpu.CompilerParams(vmem_limit_bytes=40 * 1024 * 1024)
NT = (((1,), (1,)), ((), ()))


def rope_tables():
    half = HEAD // 2
    frequency = np.exp(np.arange(half) * (-2.0 * math.log(rope_base) / HEAD))
    positions = np.arange(ROWS) % LEN
    angle = positions[:, None] * frequency[None, :]
    return np.cos(angle).astype(np.float32), np.sin(angle).astype(np.float32)


def call(kernel, outs, n_in, flops, bytes_accessed, smem=(), scratch=()):
    return pl.pallas_call(
        kernel,
        out_shape=outs,
        in_specs=[SMEM if i in smem else VMEM for i in range(n_in)],
        out_specs=jax.tree.map(lambda _: VMEM, outs),
        scratch_shapes=list(scratch),
        compiler_params=PARAMS,
        cost_estimate=pl.CostEstimate(
            flops=flops, bytes_accessed=bytes_accessed, transcendentals=0
        ),
    )


def shape(dims, dtype=jnp.bfloat16):
    return jax.ShapeDtypeStruct(dims, dtype)


def prepare(
    ids, codes, exponents, buffer_in, gain, query, keyval, output,
    packed, pay_out, inputs_out,
    codes_v, exponents_v, stored_v, gain_v, keyval_v, half_v, keyval_half_v, early_v, pay, inputs_v,
    sems, half_sems,
):
    section = lax.axis_index("section")
    far = lax.axis_index("y") ^ 1
    copies = [
        pltpu.make_async_copy(exponents, exponents_v, sems.at[0]),
        pltpu.make_async_copy(gain, gain_v, sems.at[1]),
        pltpu.make_async_copy(codes, codes_v, sems.at[2]),
        pltpu.make_async_copy(buffer_in.at[0, ids[0, section]], stored_v.at[0], sems.at[3]),
        pltpu.make_async_copy(buffer_in.at[0, ids[1, section]], stored_v.at[1], sems.at[4]),
        pltpu.make_async_copy(keyval, keyval_v, sems.at[5]),
    ]
    for item in copies:
        item.start()

    step = ZN // PIECES
    moves = [
        (query.at[pl.ds(i * step, step), far], half_v.at[i], packed.at[pl.ds(i * step, step)])
        for i in range(PIECES)
    ]
    tail = ZN + keyval_half_v.shape[0]
    moves.append((output.at[pl.ds(0, EARLY), far], early_v, packed.at[pl.ds(tail, EARLY)]))
    loads, stores = [], []
    for i, (source, between, target) in enumerate(moves):
        loads.append(pltpu.make_async_copy(source, between, half_sems.at[0, i]))
        stores.append(pltpu.make_async_copy(between, target, half_sems.at[1, i]))
        loads[-1].start()
    for item in copies[:5]:
        item.wait()
    eye = lax.broadcasted_iota(jnp.int32, (LEN, LEN), 0) == lax.broadcasted_iota(
        jnp.int32, (LEN, LEN), 1
    )
    gains = gain_v[...].astype(jnp.float32)
    sums = []
    for s in range(SEQS):
        steps = jnp.exp2(exponents_v[0, s : s + 1, :].astype(jnp.float32))
        diagonal = jnp.where(eye, steps, 0.0).astype(jnp.bfloat16)
        scales = jnp.dot(
            diagonal, jnp.ones((LEN, HEAD), jnp.bfloat16), preferred_element_type=jnp.float32
        )
        stored = stored_v[s].astype(jnp.float32)
        inputs = (stored + codes_v[0, s].astype(jnp.float32) * scales).astype(jnp.bfloat16)
        inputs_v[s] = inputs
        widened = inputs.astype(jnp.float32)
        pay[s * LEN : (s + 1) * LEN, :] = (widened * gains).astype(jnp.bfloat16)
        squares = widened * widened
        high = squares.astype(jnp.bfloat16)
        low = (squares - high.astype(jnp.float32)).astype(jnp.bfloat16)
        ones = jnp.ones((16, HEAD), jnp.bfloat16)
        total = lax.dot_general(ones, high, NT, preferred_element_type=jnp.float32)
        total += lax.dot_general(ones, low, NT, preferred_element_type=jnp.float32)
        sums.append(jnp.concatenate([total, jnp.zeros((16, HEAD - LEN), jnp.float32)], axis=1))
    row = lax.broadcasted_iota(jnp.int32, (16, HEAD), 0)
    value = jnp.where(row % 2 == 0, sums[0], sums[1])
    first = value.astype(jnp.bfloat16).astype(jnp.float32)
    second = value - first
    tail = jnp.where(row < 2, first, jnp.where(row < 4, second, 0.0))
    pay[ROWS:PAY, :] = tail.astype(jnp.bfloat16)
    stores.append(pltpu.make_async_copy(pay, pay_out, sems.at[7]))
    stores[-1].start()
    stores.append(pltpu.make_async_copy(inputs_v, inputs_out, sems.at[8]))
    stores[-1].start()

    for load, store in zip(loads, stores):
        load.wait()
        store.start()
    copies[5].wait()
    kv_width = keyval.shape[1]
    per_row = CN * HEAD // kv_width
    for z in range(ZN):
        for core in range(CN):
            i = z * CN + core
            start = (i % per_row) * kv_width
            keyval_half_v[i // per_row, start : start + kv_width, :] = keyval_v[
                0, :, head_rows(z, far, core)
            ]
    last = pltpu.make_async_copy(
        keyval_half_v, packed.at[pl.ds(ZN, keyval_half_v.shape[0])], sems.at[6]
    )
    last.start()
    last.wait()
    for store in stores:
        store.wait()


def head_rows(z, y, core):
    head = z * (YN * CN) + y * CN + core
    return pl.ds(pl.multiple_of(head * HEAD, HEAD), HEAD)


def half_rows(z, core):
    return pl.ds(pl.multiple_of((z * CN + core) * HEAD, HEAD), HEAD)


def keyval_kernel(here, there, weight, received, out, sums_out):
    y, core = lax.axis_index("y"), lax.axis_index("core")
    kv_width = weight.shape[1]
    sums = jnp.sum(here[:, ROWS:PAY, :].astype(jnp.float32), axis=0)
    sums += jnp.sum(there[:, ROWS:PAY, :].astype(jnp.float32), axis=0)
    totals = [sums[s : s + 1, :] + sums[SEQS + s : SEQS + s + 1, :] for s in range(SEQS)]
    row = lax.broadcasted_iota(jnp.int32, (PAY - ROWS, HEAD), 0)
    value = jnp.where(row % SEQS == 0, totals[0], totals[1])
    high = value.astype(jnp.bfloat16).astype(jnp.float32)
    tail = jnp.where(row < SEQS, high, jnp.where(row < 2 * SEQS, value - high, 0.0))
    sums_out[...] = tail.astype(jnp.bfloat16)
    acc = jnp.zeros((2 * kv_width, ROWS), jnp.float32)
    for z in range(ZN):
        block = jnp.concatenate([here[z, :ROWS, :], there[z, :ROWS, :]], axis=1)
        parts = []
        for side in (core, core ^ 1):
            start = ZN * CN * HEAD + (z * CN + side) * kv_width
            mine = weight[0, :, head_rows(z, y, side)]
            other = received[pl.ds(pl.multiple_of(start, kv_width), kv_width), :]
            parts.append(jnp.concatenate([mine, other], axis=0))
        part = jnp.concatenate(parts, axis=1)
        acc += lax.dot_general(part, block, NT, preferred_element_type=jnp.float32)
    out[...] = jnp.concatenate([acc[:, :LEN], acc[:, LEN:]], axis=0).T.astype(jnp.bfloat16)


def both_partials(here, there, weight, received):
    y, core = lax.axis_index("y"), lax.axis_index("core")
    acc = jnp.zeros((ROWS, 2 * HEAD), jnp.float32)
    for z in range(ZN):
        block = jnp.concatenate([here[z, :ROWS, :], there[z, :ROWS, :]], axis=1)
        parts = []
        for side in (core, core ^ 1):
            mine = weight[0, head_rows(z, y, side), :]
            other = received[half_rows(z, side), :]
            parts.append(jnp.concatenate([mine, other], axis=1))
        part = jnp.concatenate(parts, axis=0)
        acc += jnp.dot(block, part, preferred_element_type=jnp.float32)
    return acc


def query_kernel(here, there, weight, received, mine_out, other_out):
    acc = both_partials(here, there, weight, received)
    mine_out[...] = acc[:, :HEAD]
    other_out[...] = acc[:, HEAD:].astype(jnp.bfloat16)


def sum_kernel(near, far, cos_t, sin_t, out, factors_out):
    z_odd, y, core = lax.axis_index("z") % 2, lax.axis_index("y"), lax.axis_index("core")
    width = HEAD // SEQS // 2
    tail = near[2 * LEN :, :].astype(jnp.float32) + far[2 * LEN :, :].astype(jnp.float32)
    square_sum = jnp.concatenate(
        [tail[s : s + 1, :LEN] + tail[SEQS + s : SEQS + s + 1, :LEN] for s in range(SEQS)], axis=1
    )
    inverse = lax.rsqrt(square_sum / (ZN * YN * CN * HEAD) + norm_eps)
    factors = jnp.broadcast_to(inverse, (width, ROWS))
    factors_out[...] = jnp.broadcast_to(inverse, (HEAD, ROWS)).T

    def columns(source, kind):
        start = pl.multiple_of((z_odd ^ kind) * LEN, LEN)
        turned = source[pl.ds(start, LEN), :].astype(jnp.float32).T
        both = jnp.concatenate([turned[: HEAD // 2], turned[HEAD // 2 :]], axis=1)
        return both[:width], both[width:]

    held = {(side, kind): columns(ref, kind) for side, ref in enumerate((near, far)) for kind in range(2)}

    def piece(kind, which):
        near_own, near_other = held[0, kind]
        far_own, far_other = held[1, kind]
        own = which == y
        total = jnp.where(own, near_own, near_other) + jnp.where(own, far_other, far_own)
        return (total * factors).astype(jnp.bfloat16)

    first, second = piece(0, 0).astype(jnp.float32), piece(0, 1).astype(jnp.float32)
    rows = pl.ds(pl.multiple_of(core * width, width), width)
    c, s = cos_t[rows, :], sin_t[rows, :]
    out[0] = (first * c - second * s).astype(jnp.bfloat16)
    out[1] = (second * c + first * s).astype(jnp.bfloat16)
    out[2] = piece(1, 0)
    out[3] = piece(1, 1)


def rope_kernel(mine, other, factors, cos, sin, out):
    acc = (mine[...] + other[...].astype(jnp.float32)) * factors[...]
    first, second = acc[:, : HEAD // 2], acc[:, HEAD // 2 :]
    c, s = cos[...], sin[...]
    out[...] = jnp.concatenate(
        [first * c - second * s, second * c + first * s], axis=1
    ).astype(jnp.bfloat16)


def attention_kernel(query, own, sibling, out):
    core = lax.axis_index("core")
    keys_values = []
    for kind in range(2):
        parts = []
        for which in range(2):
            a, b = own[2 * kind + which], sibling[2 * kind + which]
            parts += [jnp.where(core == 0, a, b), jnp.where(core == 0, b, a)]
        keys_values.append(jnp.concatenate(parts, axis=0))
    keys, values = keys_values
    scores = jnp.dot(query[...], keys, preferred_element_type=jnp.float32) / math.sqrt(HEAD)
    row = lax.broadcasted_iota(jnp.int32, (ROWS, ROWS), 0)
    column = lax.broadcasted_iota(jnp.int32, (ROWS, ROWS), 1)
    allowed = (column <= row) & ((row < LEN) | (column >= LEN))
    scores = jnp.where(allowed, scores, -1e30)
    peak = jnp.max(scores, axis=-1, keepdims=True)
    raised = jnp.exp(scores - peak)
    weights = (raised / jnp.sum(raised, axis=-1, keepdims=True)).astype(jnp.bfloat16)
    context = lax.dot_general(weights, values, NT, preferred_element_type=jnp.float32)
    out[...] = context.astype(jnp.bfloat16)


def pack_kernel(weight, out):
    far = lax.axis_index("y") ^ 1
    for z in range(EARLY, ZN):
        out[z - EARLY] = weight[z, far]


def line_product(line, rows):
    acc = None
    for z in range(0, ZN, 2):
        block = jnp.concatenate([line[z], line[z + 1]], axis=1)
        part = jnp.concatenate([rows(z), rows(z + 1)], axis=0)
        term = jnp.dot(block, part, preferred_element_type=jnp.float32)
        acc = term if acc is None else acc + term
    return acc


def far_rows(z, core, early, received):
    if z < EARLY:
        return early[half_rows(z, core), :]
    return received[half_rows(z - EARLY, core), :]


def own_line_kernel(line, weight, early, received, out):
    y, core = lax.axis_index("y"), lax.axis_index("core")

    def rows(z):
        mine = weight[0, head_rows(z, y, core), :]
        return jnp.concatenate([mine, far_rows(z, core, early, received)], axis=1)

    out[...] = line_product(line, rows)


def far_columns_kernel(line, acc, early, received, out):
    side = lax.axis_index("core") ^ 1
    total = line_product(line, lambda z: far_rows(z, side, early, received))
    out[...] = (acc[:, HEAD:] + total).astype(jnp.bfloat16)


def own_columns_kernel(line, acc, weight, out):
    y, side = lax.axis_index("y"), lax.axis_index("core") ^ 1
    out[...] = acc[:, :HEAD] + line_product(line, lambda z: weight[0, head_rows(z, y, side), :])


def message_kernel(ids, mine, other, inputs, buffer_out, message_out):
    section = lax.axis_index("section")
    for s in range(SEQS):
        rows = slice(s * LEN, (s + 1) * LEN)
        stored = buffer_out[0, ids[s, section]].astype(jnp.float32)
        mixed = mine[rows, :] + other[rows, :].astype(jnp.float32)
        message_out[s] = (inputs[s].astype(jnp.float32) + mixed - stored).astype(jnp.bfloat16)


def refresh_kernel(ids, message, buffer_out, new_out):
    section = lax.axis_index("section")
    new_out[...] = buffer_out[...]
    for s in range(SEQS):
        slot = ids[s, section]
        stored = buffer_out[0, slot].astype(jnp.float32)
        new_out[0, slot] = (stored + message[s].astype(jnp.float32)).astype(jnp.bfloat16)


def finish_kernel(ids, buffer_in, inputs, arrived, following_out, stored_out, following, stored, sems):
    section = lax.axis_index("section")
    before = jnp.maximum(section - 1, 0)
    stored[...] = buffer_in[0]
    for s in range(SEQS):
        stored[ids[s, section]] = inputs[s]
    copies = []
    for s in range(SEQS):
        current = stored[ids[s, before]].astype(jnp.float32)
        following[s] = (current + arrived[s].astype(jnp.float32)).astype(jnp.bfloat16)
        copies.append(
            pltpu.make_async_copy(following.at[s], following_out.at[0, s], sems.at[s])
        )
        copies[-1].start()
    for s in range(SEQS):
        stored[ids[s, before]] = following[s]
    copies.append(pltpu.make_async_copy(stored, stored_out.at[0], sems.at[SEQS]))
    copies[-1].start()
    for item in copies:
        item.wait()


def lane(z, y, core):
    return (z % ZN) * (YN * CN) + y * CN + core


def permute(x, target):
    pairs = [
        (lane(z, y, c), lane(*target(z, y, c)))
        for z in range(ZN)
        for y in range(YN)
        for c in range(CN)
    ]
    return lax.ppermute(x, LANES, pairs)


def swap(x, flip_y, flip_core):
    return permute(x, lambda z, y, c: (z, y ^ flip_y, c ^ flip_core))


def after(x, earlier):
    return lax.optimization_barrier((x, earlier))[0]


def gather_z(x):
    return lax.all_gather(x, "z", axis=0)


def per_device(
    codes, exponents, sample_ids, buffer_in, buffer_out, norm_gain, w_query, w_keyval, w_output
):
    cos, sin = rope_tables()
    sample_ids = sample_ids.T
    kv_width = w_keyval.shape[2]
    half = ZN * CN * HEAD
    w_keyval = jnp.swapaxes(w_keyval, 1, 2)
    partial_flops = 2 * ROWS * half * 256
    wide = shape((ROWS, HEAD), jnp.float32)

    by_half = (ZN, YN, CN * HEAD, HEAD)
    any_spec = pl.BlockSpec(memory_space=pl.ANY)
    bf16, int32 = jnp.bfloat16, jnp.int32
    packed, pay, inputs = pl.pallas_call(
        prepare,
        out_shape=(
            shape((ZN + ZN * kv_width // HEAD + EARLY, CN * HEAD, HEAD)),
            shape((PAY, HEAD)),
            shape((SEQS, LEN, HEAD)),
        ),
        in_specs=[SMEM] + [any_spec] * 7,
        out_specs=(any_spec,) * 3,
        scratch_shapes=[
            pltpu.VMEM(codes.shape, int32),
            pltpu.VMEM(exponents.shape, int32),
            pltpu.VMEM((SEQS, LEN, HEAD), bf16),
            pltpu.VMEM(norm_gain.shape, bf16),
            pltpu.VMEM(w_keyval.shape, bf16),
            pltpu.VMEM((PIECES, ZN // PIECES, CN * HEAD, HEAD), bf16),
            pltpu.VMEM((ZN * kv_width // HEAD, CN * HEAD, HEAD), bf16),
            pltpu.VMEM((EARLY, CN * HEAD, HEAD), bf16),
            pltpu.VMEM((PAY, HEAD), bf16),
            pltpu.VMEM((SEQS, LEN, HEAD), bf16),
            pltpu.SemaphoreType.DMA((9,)),
            pltpu.SemaphoreType.DMA((2, PIECES + 1)),
        ],
        cost_estimate=pl.CostEstimate(flops=10**7, bytes_accessed=4 * 10**6, transcendentals=0),
    )(
        sample_ids, codes, exponents, buffer_in, norm_gain,
        w_query.reshape(by_half), w_keyval, w_output.reshape(by_half),
    )
    received = swap(packed, 1, 0).reshape(-1, HEAD)
    here = gather_z(pay)
    there = swap(here, 0, 1)
    packed_out = call(pack_kernel, shape((ZN - EARLY, CN * HEAD, HEAD)), 1, 10**6, 2 * 10**6)(
        w_output.reshape(by_half)
    )
    received_out = swap(packed_out, 1, 0).reshape(-1, HEAD)

    keyval, sums = call(
        keyval_kernel,
        (shape((LEN, HEAD)), shape((PAY - ROWS, HEAD))),
        4,
        partial_flops,
        5 * 10**6,
    )(here, there, w_keyval, received)
    even = permute(keyval, lambda z, y, c: (2 * z if z < 8 else 2 * (z - 8) + 1, y, c))
    odd = permute(keyval, lambda z, y, c: (2 * z + 1 if z < 8 else 2 * (z - 8), y, c))
    mine, other = call(
        query_kernel, (wide, shape((ROWS, HEAD))), 4, partial_flops, 6 * 10**6
    )(here, there, w_query, after(received, keyval))
    other = swap(other, 1, 0)
    near = after(jnp.concatenate([even, odd, sums]), mine)
    far = swap(near, 1, 0)
    own, factors = call(
        sum_kernel, (shape((4, kv_width, ROWS)), wide), 4, 10**6, 10**6
    )(after(near, received_out), far, cos.T.copy(), sin.T.copy())
    sibling = swap(own, 0, 1)
    queries = call(rope_kernel, shape((ROWS, HEAD)), 5, 10**6, 10**6)(
        mine, other, factors, cos, sin
    )
    context = call(attention_kernel, shape((ROWS, HEAD)), 3, 4 * ROWS * ROWS * HEAD, 10**6)(
        queries, own, sibling
    )

    here = gather_z(context)
    there = swap(here, 0, 1)
    early = received[-EARLY * CN * HEAD :]
    line_flops = partial_flops // 2
    both = call(
        own_line_kernel, shape((ROWS, 2 * HEAD), jnp.float32), 4, line_flops, 4 * 10**6
    )(here, w_output, early, received_out)
    other = call(far_columns_kernel, shape((ROWS, HEAD)), 4, line_flops, 2 * 10**6)(
        there, both, early, received_out
    )
    other = swap(other, 1, 0)
    mine = call(own_columns_kernel, wide, 3, line_flops, 3 * 10**6)(there, both, w_output)
    message = call(
        message_kernel, shape((SEQS, LEN, HEAD)), 5, 10**6, 10**6, smem=(0,)
    )(sample_ids, mine, other, inputs, buffer_out)

    sections = lax.axis_size("section")
    arrived = lax.ppermute(message, "section", [(i, i + 1) for i in range(sections - 1)])
    following, new_in = pl.pallas_call(
        finish_kernel,
        out_shape=(shape((1, SEQS, LEN, HEAD)), shape(buffer_in.shape)),
        in_specs=[SMEM] + [VMEM] * 3,
        out_specs=(any_spec,) * 2,
        scratch_shapes=[
            pltpu.VMEM((SEQS, LEN, HEAD), bf16),
            pltpu.VMEM((SLOTS, LEN, HEAD), bf16),
            pltpu.SemaphoreType.DMA((SEQS + 1,)),
        ],
        compiler_params=PARAMS,
        cost_estimate=pl.CostEstimate(flops=10**6, bytes_accessed=10**6, transcendentals=0),
    )(sample_ids, buffer_in, inputs, arrived)
    new_out = call(refresh_kernel, shape(buffer_out.shape), 3, 10**6, 10**6, smem=(0,))(
        sample_ids, message, buffer_out
    )
    return following, new_in, new_out


def solution(mesh):
    sections = mesh.shape["section"]
    fine = Mesh(mesh.devices.reshape(sections, ZN, YN, CN), ("section",) + LANES)
    return jax.shard_map(
        per_device,
        mesh=fine,
        in_specs=(
            P("section", None, None, LANES),
            P("section", None, None),
            P(),
            P("section", None, None, LANES),
            P("section", None, None, LANES),
            P("section", LANES),
            P("section", None, LANES),
            P("section", None, LANES),
            P("section", None, LANES),
        ),
        out_specs=(
            P("section", None, None, LANES),
            P("section", None, None, LANES),
            P("section", None, None, LANES),
        ),
        check_vma=False,
    )
```

```python
import functools
import math

import jax
import jax.numpy as jnp
import numpy as np
from jax import lax
from jax.experimental import pallas as pl
from jax.experimental.pallas import tpu as pltpu
from jax.sharding import Mesh
from jax.sharding import PartitionSpec as P

SEQS, LEN, SLOTS, HEAD, KV_HEADS = 2, 112, 3, 128, 8
ROWS = SEQS * LEN
PAY = ROWS + 16
ZN, YN, CN = 16, 2, 2
PIECES = 4
EARLY = 4
LANES = ("z", "y", "core")
rope_base = 500000.0
norm_eps = 1e-05

VMEM = pl.BlockSpec(memory_space=pltpu.VMEM)
SMEM = pl.BlockSpec(memory_space=pltpu.SMEM)
PARAMS = pltpu.CompilerParams(vmem_limit_bytes=40 * 1024 * 1024)
NT = (((1,), (1,)), ((), ()))


def rope_tables():
    half = HEAD // 2
    frequency = np.exp(np.arange(half) * (-2.0 * math.log(rope_base) / HEAD))
    positions = np.arange(ROWS) % LEN
    angle = positions[:, None] * frequency[None, :]
    return np.cos(angle).astype(np.float32), np.sin(angle).astype(np.float32)


def call(kernel, outs, n_in, flops, bytes_accessed, smem=(), scratch=()):
    return pl.pallas_call(
        kernel,
        out_shape=outs,
        in_specs=[SMEM if i in smem else VMEM for i in range(n_in)],
        out_specs=jax.tree.map(lambda _: VMEM, outs),
        scratch_shapes=list(scratch),
        compiler_params=PARAMS,
        cost_estimate=pl.CostEstimate(
            flops=flops, bytes_accessed=bytes_accessed, transcendentals=0
        ),
    )


def shape(dims, dtype=jnp.bfloat16):
    return jax.ShapeDtypeStruct(dims, dtype)


def prepare(
    ids, codes, exponents, buffer_in, gain, query, keyval, output,
    packed, pay_out, inputs_out,
    codes_v, exponents_v, stored_v, gain_v, keyval_v, half_v, keyval_half_v, early_v, pay, inputs_v,
    sems, half_sems,
):
    section = lax.axis_index("section")
    far = lax.axis_index("y") ^ 1
    copies = [
        pltpu.make_async_copy(exponents, exponents_v, sems.at[0]),
        pltpu.make_async_copy(gain, gain_v, sems.at[1]),
        pltpu.make_async_copy(codes, codes_v, sems.at[2]),
        pltpu.make_async_copy(buffer_in.at[0, ids[0, section]], stored_v.at[0], sems.at[3]),
        pltpu.make_async_copy(buffer_in.at[0, ids[1, section]], stored_v.at[1], sems.at[4]),
        pltpu.make_async_copy(keyval, keyval_v, sems.at[5]),
    ]
    step = ZN // PIECES
    moves = [
        (query.at[pl.ds(i * step, step), far], half_v.at[i], packed.at[pl.ds(i * step, step)])
        for i in range(PIECES)
    ]
    tail = ZN + keyval_half_v.shape[0]
    moves.append((output.at[pl.ds(0, EARLY), far], early_v, packed.at[pl.ds(tail, EARLY)]))
    loads, stores = [], []
    for i, (source, between, target) in enumerate(moves):
        loads.append(pltpu.make_async_copy(source, between, half_sems.at[0, i]))
        stores.append(pltpu.make_async_copy(between, target, half_sems.at[1, i]))
        loads[-1].start()
    for item in copies:
        item.start()
    for load, store in zip(loads, stores):
        load.wait()
        store.start()
    for item in copies[:5]:
        item.wait()
    eye = lax.broadcasted_iota(jnp.int32, (LEN, LEN), 0) == lax.broadcasted_iota(
        jnp.int32, (LEN, LEN), 1
    )
    gains = gain_v[...].astype(jnp.float32)
    sums = []
    for s in range(SEQS):
        steps = jnp.exp2(exponents_v[0, s : s + 1, :].astype(jnp.float32))
        diagonal = jnp.where(eye, steps, 0.0).astype(jnp.bfloat16)
        scales = jnp.dot(
            diagonal, jnp.ones((LEN, HEAD), jnp.bfloat16), preferred_element_type=jnp.float32
        )
        stored = stored_v[s].astype(jnp.float32)
        inputs = (stored + codes_v[0, s].astype(jnp.float32) * scales).astype(jnp.bfloat16)
        inputs_v[s] = inputs
        widened = inputs.astype(jnp.float32)
        pay[s * LEN : (s + 1) * LEN, :] = (widened * gains).astype(jnp.bfloat16)
        squares = widened * widened
        high = squares.astype(jnp.bfloat16)
        low = (squares - high.astype(jnp.float32)).astype(jnp.bfloat16)
        ones = jnp.ones((16, HEAD), jnp.bfloat16)
        total = lax.dot_general(ones, high, NT, preferred_element_type=jnp.float32)
        total += lax.dot_general(ones, low, NT, preferred_element_type=jnp.float32)
        sums.append(jnp.concatenate([total, jnp.zeros((16, HEAD - LEN), jnp.float32)], axis=1))
    row = lax.broadcasted_iota(jnp.int32, (16, HEAD), 0)
    value = jnp.where(row % 2 == 0, sums[0], sums[1])
    first = value.astype(jnp.bfloat16).astype(jnp.float32)
    second = value - first
    tail = jnp.where(row < 2, first, jnp.where(row < 4, second, 0.0))
    pay[ROWS:PAY, :] = tail.astype(jnp.bfloat16)
    stores.append(pltpu.make_async_copy(pay, pay_out, sems.at[7]))
    stores[-1].start()
    stores.append(pltpu.make_async_copy(inputs_v, inputs_out, sems.at[8]))
    stores[-1].start()

    copies[5].wait()
    kv_width = keyval.shape[1]
    per_row = CN * HEAD // kv_width
    for z in range(ZN):
        for core in range(CN):
            i = z * CN + core
            start = (i % per_row) * kv_width
            keyval_half_v[i // per_row, start : start + kv_width, :] = keyval_v[
                0, :, head_rows(z, far, core)
            ]
    last = pltpu.make_async_copy(
        keyval_half_v, packed.at[pl.ds(ZN, keyval_half_v.shape[0])], sems.at[6]
    )
    last.start()
    last.wait()
    for store in stores:
        store.wait()


def head_rows(z, y, core):
    head = z * (YN * CN) + y * CN + core
    return pl.ds(pl.multiple_of(head * HEAD, HEAD), HEAD)


def half_rows(z, core):
    return pl.ds(pl.multiple_of((z * CN + core) * HEAD, HEAD), HEAD)


def keyval_kernel(here, there, weight, received, out, sums_out):
    y, core = lax.axis_index("y"), lax.axis_index("core")
    kv_width = weight.shape[1]
    sums = jnp.sum(here[:, ROWS:PAY, :].astype(jnp.float32), axis=0)
    sums += jnp.sum(there[:, ROWS:PAY, :].astype(jnp.float32), axis=0)
    totals = [sums[s : s + 1, :] + sums[SEQS + s : SEQS + s + 1, :] for s in range(SEQS)]
    row = lax.broadcasted_iota(jnp.int32, (PAY - ROWS, HEAD), 0)
    value = jnp.where(row % SEQS == 0, totals[0], totals[1])
    high = value.astype(jnp.bfloat16).astype(jnp.float32)
    tail = jnp.where(row < SEQS, high, jnp.where(row < 2 * SEQS, value - high, 0.0))
    sums_out[...] = tail.astype(jnp.bfloat16)
    acc = jnp.zeros((2 * kv_width, ROWS), jnp.float32)
    for z in range(ZN):
        block = jnp.concatenate([here[z, :ROWS, :], there[z, :ROWS, :]], axis=1)
        parts = []
        for side in (core, core ^ 1):
            start = ZN * CN * HEAD + (z * CN + side) * kv_width
            mine = weight[0, :, head_rows(z, y, side)]
            other = received[pl.ds(pl.multiple_of(start, kv_width), kv_width), :]
            parts.append(jnp.concatenate([mine, other], axis=0))
        part = jnp.concatenate(parts, axis=1)
        acc += lax.dot_general(part, block, NT, preferred_element_type=jnp.float32)
    out[...] = jnp.concatenate([acc[:, :LEN], acc[:, LEN:]], axis=0).T.astype(jnp.bfloat16)


def both_partials(here, there, weight, received):
    y, core = lax.axis_index("y"), lax.axis_index("core")
    acc = jnp.zeros((ROWS, 2 * HEAD), jnp.float32)
    for z in range(ZN):
        block = jnp.concatenate([here[z, :ROWS, :], there[z, :ROWS, :]], axis=1)
        parts = []
        for side in (core, core ^ 1):
            mine = weight[0, head_rows(z, y, side), :]
            other = received[half_rows(z, side), :]
            parts.append(jnp.concatenate([mine, other], axis=1))
        part = jnp.concatenate(parts, axis=0)
        acc += jnp.dot(block, part, preferred_element_type=jnp.float32)
    return acc


def query_kernel(here, there, weight, received, mine_out, other_out):
    acc = both_partials(here, there, weight, received)
    mine_out[...] = acc[:, :HEAD]
    other_out[...] = acc[:, HEAD:].astype(jnp.bfloat16)


def sum_kernel(near, far, cos_t, sin_t, out, factors_out):
    z_odd, y, core = lax.axis_index("z") % 2, lax.axis_index("y"), lax.axis_index("core")
    width = HEAD // SEQS // 2
    tail = near[2 * LEN :, :].astype(jnp.float32) + far[2 * LEN :, :].astype(jnp.float32)
    square_sum = jnp.concatenate(
        [tail[s : s + 1, :LEN] + tail[SEQS + s : SEQS + s + 1, :LEN] for s in range(SEQS)], axis=1
    )
    inverse = lax.rsqrt(square_sum / (ZN * YN * CN * HEAD) + norm_eps)
    factors = jnp.broadcast_to(inverse, (width, ROWS))
    factors_out[...] = jnp.broadcast_to(inverse, (HEAD, ROWS)).T

    def columns(source, kind):
        start = pl.multiple_of((z_odd ^ kind) * LEN, LEN)
        turned = source[pl.ds(start, LEN), :].astype(jnp.float32).T
        both = jnp.concatenate([turned[: HEAD // 2], turned[HEAD // 2 :]], axis=1)
        return both[:width], both[width:]

    held = {(side, kind): columns(ref, kind) for side, ref in enumerate((near, far)) for kind in range(2)}

    def piece(kind, which):
        near_own, near_other = held[0, kind]
        far_own, far_other = held[1, kind]
        own = which == y
        total = jnp.where(own, near_own, near_other) + jnp.where(own, far_other, far_own)
        return (total * factors).astype(jnp.bfloat16)

    first, second = piece(0, 0).astype(jnp.float32), piece(0, 1).astype(jnp.float32)
    rows = pl.ds(pl.multiple_of(core * width, width), width)
    c, s = cos_t[rows, :], sin_t[rows, :]
    out[0] = (first * c - second * s).astype(jnp.bfloat16)
    out[1] = (second * c + first * s).astype(jnp.bfloat16)
    out[2] = piece(1, 0)
    out[3] = piece(1, 1)


def rope_kernel(mine, other, factors, cos, sin, out):
    acc = (mine[...] + other[...].astype(jnp.float32)) * factors[...]
    first, second = acc[:, : HEAD // 2], acc[:, HEAD // 2 :]
    c, s = cos[...], sin[...]
    out[...] = jnp.concatenate(
        [first * c - second * s, second * c + first * s], axis=1
    ).astype(jnp.bfloat16)


def attention_kernel(query, own, sibling, out):
    core = lax.axis_index("core")
    keys_values = []
    for kind in range(2):
        parts = []
        for which in range(2):
            a, b = own[2 * kind + which], sibling[2 * kind + which]
            parts += [jnp.where(core == 0, a, b), jnp.where(core == 0, b, a)]
        keys_values.append(jnp.concatenate(parts, axis=0))
    keys, values = keys_values
    scores = jnp.dot(query[...], keys, preferred_element_type=jnp.float32) / math.sqrt(HEAD)
    row = lax.broadcasted_iota(jnp.int32, (ROWS, ROWS), 0)
    column = lax.broadcasted_iota(jnp.int32, (ROWS, ROWS), 1)
    allowed = (column <= row) & ((row < LEN) | (column >= LEN))
    scores = jnp.where(allowed, scores, -1e30)
    peak = jnp.max(scores, axis=-1, keepdims=True)
    raised = jnp.exp(scores - peak)
    weights = (raised / jnp.sum(raised, axis=-1, keepdims=True)).astype(jnp.bfloat16)
    context = lax.dot_general(weights, values, NT, preferred_element_type=jnp.float32)
    out[...] = context.astype(jnp.bfloat16)


def pack_kernel(weight, out):
    far = lax.axis_index("y") ^ 1
    for z in range(EARLY, ZN):
        out[z - EARLY] = weight[z, far]


def line_product(line, rows):
    acc = None
    for z in range(0, ZN, 2):
        block = jnp.concatenate([line[z], line[z + 1]], axis=1)
        part = jnp.concatenate([rows(z), rows(z + 1)], axis=0)
        term = jnp.dot(block, part, preferred_element_type=jnp.float32)
        acc = term if acc is None else acc + term
    return acc


def far_rows(z, core, early, received):
    if z < EARLY:
        return early[half_rows(z, core), :]
    return received[half_rows(z - EARLY, core), :]


def own_line_kernel(line, weight, early, received, out):
    y, core = lax.axis_index("y"), lax.axis_index("core")

    def rows(z):
        mine = weight[0, head_rows(z, y, core), :]
        return jnp.concatenate([mine, far_rows(z, core, early, received)], axis=1)

    out[...] = line_product(line, rows)


def far_columns_kernel(line, acc, early, received, out):
    side = lax.axis_index("core") ^ 1
    total = line_product(line, lambda z: far_rows(z, side, early, received))
    out[...] = (acc[:, HEAD:] + total).astype(jnp.bfloat16)


def own_columns_kernel(line, acc, weight, out):
    y, side = lax.axis_index("y"), lax.axis_index("core") ^ 1
    out[...] = acc[:, :HEAD] + line_product(line, lambda z: weight[0, head_rows(z, y, side), :])


def message_kernel(ids, mine, other, inputs, buffer_out, message_out):
    section = lax.axis_index("section")
    for s in range(SEQS):
        rows = slice(s * LEN, (s + 1) * LEN)
        stored = buffer_out[0, ids[s, section]].astype(jnp.float32)
        mixed = mine[rows, :] + other[rows, :].astype(jnp.float32)
        message_out[s] = (inputs[s].astype(jnp.float32) + mixed - stored).astype(jnp.bfloat16)


def refresh_kernel(ids, message, buffer_out, new_out):
    section = lax.axis_index("section")
    new_out[...] = buffer_out[...]
    for s in range(SEQS):
        slot = ids[s, section]
        stored = buffer_out[0, slot].astype(jnp.float32)
        new_out[0, slot] = (stored + message[s].astype(jnp.float32)).astype(jnp.bfloat16)


def finish_kernel(ids, buffer_in, inputs, arrived, following_out, stored_out, following, stored, sems):
    section = lax.axis_index("section")
    before = jnp.maximum(section - 1, 0)
    stored[...] = buffer_in[0]
    for s in range(SEQS):
        stored[ids[s, section]] = inputs[s]
    copies = []
    for s in range(SEQS):
        current = stored[ids[s, before]].astype(jnp.float32)
        following[s] = (current + arrived[s].astype(jnp.float32)).astype(jnp.bfloat16)
        copies.append(
            pltpu.make_async_copy(following.at[s], following_out.at[0, s], sems.at[s])
        )
        copies[-1].start()
    for s in range(SEQS):
        stored[ids[s, before]] = following[s]
    copies.append(pltpu.make_async_copy(stored, stored_out.at[0], sems.at[SEQS]))
    copies[-1].start()
    for item in copies:
        item.wait()


def lane(z, y, core):
    return (z % ZN) * (YN * CN) + y * CN + core


def permute(x, target):
    pairs = [
        (lane(z, y, c), lane(*target(z, y, c)))
        for z in range(ZN)
        for y in range(YN)
        for c in range(CN)
    ]
    return lax.ppermute(x, LANES, pairs)


def swap(x, flip_y, flip_core):
    return permute(x, lambda z, y, c: (z, y ^ flip_y, c ^ flip_core))


def after(x, earlier):
    return lax.optimization_barrier((x, earlier))[0]


def gather_z(x):
    return lax.all_gather(x, "z", axis=0)


def per_device(
    codes, exponents, sample_ids, buffer_in, buffer_out, norm_gain, w_query, w_keyval, w_output
):
    cos, sin = rope_tables()
    sample_ids = sample_ids.T
    kv_width = w_keyval.shape[2]
    half = ZN * CN * HEAD
    w_keyval = jnp.swapaxes(w_keyval, 1, 2)
    partial_flops = 2 * ROWS * half * 256
    wide = shape((ROWS, HEAD), jnp.float32)

    by_half = (ZN, YN, CN * HEAD, HEAD)
    any_spec = pl.BlockSpec(memory_space=pl.ANY)
    bf16, int32 = jnp.bfloat16, jnp.int32
    packed, pay, inputs = pl.pallas_call(
        prepare,
        out_shape=(
            shape((ZN + ZN * kv_width // HEAD + EARLY, CN * HEAD, HEAD)),
            shape((PAY, HEAD)),
            shape((SEQS, LEN, HEAD)),
        ),
        in_specs=[SMEM] + [any_spec] * 7,
        out_specs=(any_spec,) * 3,
        scratch_shapes=[
            pltpu.VMEM(codes.shape, int32),
            pltpu.VMEM(exponents.shape, int32),
            pltpu.VMEM((SEQS, LEN, HEAD), bf16),
            pltpu.VMEM(norm_gain.shape, bf16),
            pltpu.VMEM(w_keyval.shape, bf16),
            pltpu.VMEM((PIECES, ZN // PIECES, CN * HEAD, HEAD), bf16),
            pltpu.VMEM((ZN * kv_width // HEAD, CN * HEAD, HEAD), bf16),
            pltpu.VMEM((EARLY, CN * HEAD, HEAD), bf16),
            pltpu.VMEM((PAY, HEAD), bf16),
            pltpu.VMEM((SEQS, LEN, HEAD), bf16),
            pltpu.SemaphoreType.DMA((9,)),
            pltpu.SemaphoreType.DMA((2, PIECES + 1)),
        ],
        cost_estimate=pl.CostEstimate(flops=10**7, bytes_accessed=4 * 10**6, transcendentals=0),
    )(
        sample_ids, codes, exponents, buffer_in, norm_gain,
        w_query.reshape(by_half), w_keyval, w_output.reshape(by_half),
    )
    received = swap(packed, 1, 0).reshape(-1, HEAD)
    here = gather_z(pay)
    there = swap(here, 0, 1)
    packed_out = call(pack_kernel, shape((ZN - EARLY, CN * HEAD, HEAD)), 1, 10**6, 2 * 10**6)(
        w_output.reshape(by_half)
    )
    received_out = swap(packed_out, 1, 0).reshape(-1, HEAD)

    keyval, sums = call(
        keyval_kernel,
        (shape((LEN, HEAD)), shape((PAY - ROWS, HEAD))),
        4,
        partial_flops,
        5 * 10**6,
    )(here, there, w_keyval, received)
    even = permute(keyval, lambda z, y, c: (2 * z if z < 8 else 2 * (z - 8) + 1, y, c))
    odd = permute(keyval, lambda z, y, c: (2 * z + 1 if z < 8 else 2 * (z - 8), y, c))
    mine, other = call(
        query_kernel, (wide, shape((ROWS, HEAD))), 4, partial_flops, 6 * 10**6
    )(here, there, w_query, after(received, keyval))
    other = swap(other, 1, 0)
    near = after(jnp.concatenate([even, odd, sums]), mine)
    far = swap(near, 1, 0)
    own, factors = call(
        sum_kernel, (shape((4, kv_width, ROWS)), wide), 4, 10**6, 10**6
    )(after(near, received_out), far, cos.T.copy(), sin.T.copy())
    sibling = swap(own, 0, 1)
    queries = call(rope_kernel, shape((ROWS, HEAD)), 5, 10**6, 10**6)(
        mine, other, factors, cos, sin
    )
    context = call(attention_kernel, shape((ROWS, HEAD)), 3, 4 * ROWS * ROWS * HEAD, 10**6)(
        queries, own, sibling
    )

    here = gather_z(context)
    there = swap(here, 0, 1)
    early = received[-EARLY * CN * HEAD :]
    line_flops = partial_flops // 2
    both = call(
        own_line_kernel, shape((ROWS, 2 * HEAD), jnp.float32), 4, line_flops, 4 * 10**6
    )(here, w_output, early, received_out)
    other = call(far_columns_kernel, shape((ROWS, HEAD)), 4, line_flops, 2 * 10**6)(
        there, both, early, received_out
    )
    other = swap(other, 1, 0)
    mine = call(own_columns_kernel, wide, 3, line_flops, 3 * 10**6)(there, both, w_output)
    message = call(
        message_kernel, shape((SEQS, LEN, HEAD)), 5, 10**6, 10**6, smem=(0,)
    )(sample_ids, mine, other, inputs, buffer_out)

    sections = lax.axis_size("section")
    arrived = lax.ppermute(message, "section", [(i, i + 1) for i in range(sections - 1)])
    following, new_in = pl.pallas_call(
        finish_kernel,
        out_shape=(shape((1, SEQS, LEN, HEAD)), shape(buffer_in.shape)),
        in_specs=[SMEM] + [VMEM] * 3,
        out_specs=(any_spec,) * 2,
        scratch_shapes=[
            pltpu.VMEM((SEQS, LEN, HEAD), bf16),
            pltpu.VMEM((SLOTS, LEN, HEAD), bf16),
            pltpu.SemaphoreType.DMA((SEQS + 1,)),
        ],
        compiler_params=PARAMS,
        cost_estimate=pl.CostEstimate(flops=10**6, bytes_accessed=10**6, transcendentals=0),
    )(sample_ids, buffer_in, inputs, arrived)
    new_out = call(refresh_kernel, shape(buffer_out.shape), 3, 10**6, 10**6, smem=(0,))(
        sample_ids, message, buffer_out
    )
    return following, new_in, new_out


def solution(mesh):
    sections = mesh.shape["section"]
    fine = Mesh(mesh.devices.reshape(sections, ZN, YN, CN), ("section",) + LANES)
    return jax.shard_map(
        per_device,
        mesh=fine,
        in_specs=(
            P("section", None, None, LANES),
            P("section", None, None),
            P(),
            P("section", None, None, LANES),
            P("section", None, None, LANES),
            P("section", LANES),
            P("section", None, LANES),
            P("section", None, LANES),
            P("section", None, LANES),
        ),
        out_specs=(
            P("section", None, None, LANES),
            P("section", None, None, LANES),
            P("section", None, None, LANES),
        ),
        check_vma=False,
    )
```
